32 devices in a mesh: dp: 16 (over z, y, x), fsdp: 2 (over core).
Axes of the slice: x: 2, y: 2, z: 4, core: 2. Of those that a mesh axis runs over, the one named last changes fastest.
Arguments:
- tokens: bfloat16 [64, 1024, 768], P(('dp', 'fsdp')), may hold values from -6 to 6
- cotangent: bfloat16 [64, 1024, 768], P(('dp', 'fsdp')), may hold values from -6 to 6
- segments: int32 [64, 1024], P(('dp', 'fsdp')), may hold values from 0 to 3, never falling along the last dimension, each value on 1 to 800 neighbouring positions
- in_gain: bfloat16 [768], P(('dp', 'fsdp')), may hold values from 0.099609375 to 1.8984375
- weight_in: bfloat16 [768, 3352], P(('dp', 'fsdp')), as said below
- conv_weight: bfloat16 [4, 1792], P(None, ('dp', 'fsdp')), may hold values from -3 to 3
- conv_bias: bfloat16 [1792], P(('dp', 'fsdp')), may hold values from -3 to 3
- step_bias: float32 [24], P('fsdp'), may hold values from -9 to -5
- decay_log: float32 [24], P('fsdp'), may hold values from 0 to 2.75
- skip_gain: float32 [24], P('fsdp'), may hold values from 0.5 to 1.5
- gate_gain: bfloat16 [1536], P(('dp', 'fsdp')), may hold values from 0.099609375 to 1.8984375
- weight_out: bfloat16 [1536, 768], P(('dp', 'fsdp')), may hold values from -0.15625 to 0.15625
Outputs:
- layer_out: bfloat16 [64, 1024, 768], P(('dp', 'fsdp'))
- grad_tokens: bfloat16 [64, 1024, 768], P(('dp', 'fsdp'))
- grad_in_gain: float32 [768], P(('dp', 'fsdp'))
- grad_weight_in: float32 [768, 3352], P(('dp', 'fsdp'))
- grad_conv_weight: float32 [4, 1792], P(None, ('dp', 'fsdp'))
- grad_conv_bias: float32 [1792], P(('dp', 'fsdp'))
- grad_step_bias: float32 [24], P('fsdp')
- grad_decay_log: float32 [24], P('fsdp')
- grad_skip_gain: float32 [24], P('fsdp')
- grad_gate_gain: float32 [1536], P(('dp', 'fsdp'))
- grad_weight_out: float32 [1536, 768], P(('dp', 'fsdp'))
The draws below stay inside these ranges and needn't reach their ends.
Inputs may be any that keep to these rules, and one draw needn't show every extreme that they name: `segments`: in each sequence the document numbers never fall; each document holds 1 to 800 tokens, and one holds exactly 800. `weight_in`: A matrix of independent entries of mean zero.
All inputs are finite; a program needn't handle non-finite values.
Results may differ from the reference program's by a relative error of at most 0.014.
Values may be sent and summed in bfloat16 or wider, within the bound.
No kernel may reach another device: no remote copies, remote signals or barrier semaphores. Data moves between devices by JAX's collectives and lax.ppermute only.
A program may use at most 320 MiB of HBM per device.

```python
import math
import jax
import jax.numpy as jnp
import numpy as np
from jax import lax

D = 768
DI = 1536
H = 24
K = 4
SPAN = 256
L = 1024
DOCS = 4
DOC_MOST = 800
SEQS = 64
CONV = 1792
PROJ = 3352


def draw_weight_in(key, part):
    key = jax.random.fold_in(key, 7)
    noise = jax.random.truncated_normal(key, -4.0, 4.0, (D, PROJ), jnp.float32)
    column_scale = jnp.where(jnp.arange(PROJ) >= DI + CONV, 2.0, 1.0) * D ** (-0.5)
    return (noise * column_scale[None, :]).astype(jnp.bfloat16)


def spiked(values, stream_key, source, target, shards_of, factor):
    def block_of(dim):
        return (jnp.arange(values.shape[dim]) // (values.shape[dim] // shards_of)).reshape((-1,) + (1,) * (values.ndim - 1 - dim))

    one_side = jax.random.permutation(stream_key, shards_of)[block_of(target)]
    other_side = (block_of(target) + shards_of // 2) % shards_of
    return jnp.where((block_of(source) == one_side) | (block_of(source) == other_side), factor * values, values)


def block_scale(own_key, extent, shards, least, top_value):
    factor_of, own = 1.0, jax.random.fold_in(own_key, 6)
    for dim, shards_of in shards:
        heights = jnp.exp(jax.random.uniform(jax.random.fold_in(own, dim), (shards_of,), jnp.float32, least / len(shards), top_value / len(shards)))
        factor_of = factor_of * jnp.repeat(heights, extent[dim] // shards_of).reshape([-1 if axis == dim else 1 for axis in range(len(extent))])
    return factor_of


def length_profile(count, total, limit, lean):
    loads = [(1 << 20) // math.isqrt(grade ** lean) + 1 for grade in range(2, count + 1)]
    spare, holding = total - limit - (count - 1), [1] * (count - 1)
    while spare > 0:
        candidates = [i for i in range(count - 1) if holding[i] < limit]
        pool, left = sum([loads[i] for i in candidates]), spare
        for i in candidates:
            addition = min(limit - holding[i], max(1, left * loads[i] // pool), spare)
            holding[i] = holding[i] + addition
            spare = spare - addition
    return np.array([limit] + holding)


def ragged_sizes(own_key, count, total, limit, slope):
    if count == 2:
        one = jax.random.randint(own_key, (), max(1, total - limit), min(limit, total - 1) + 1)
        return jnp.stack([one, total - one])
    tallies = jnp.asarray(length_profile(count, total, limit, slope), jnp.int32)
    couples = (count - 1) // 2
    giver, sink = tallies[1:1 + 2 * couples:2], tallies[2:2 + 2 * couples:2]
    slack = jnp.minimum(giver - 1, limit - sink)
    shifted = jax.random.randint(jax.random.fold_in(own_key, 1), (couples,), 0, 1 << 20) % (slack + 1)
    tallies = tallies.at[1:1 + 2 * couples:2].set(giver - shifted).at[2:2 + 2 * couples:2].set(sink + shifted)
    return tallies[jax.random.permutation(jax.random.fold_in(own_key, 2), count)]


def normal_values(key, extent, scale, most, shards=(), dtype=jnp.bfloat16):
    array = jax.random.normal(key, extent, jnp.float32) * scale
    if len(shards) > 0:
        array = block_scale(key, extent, shards, -0.22, 0.18) * array
    return jnp.clip(array, min=-most, max=most).astype(dtype)


def heavy_noise(own_key, extent, scale, most, cuts, heavy, dtype=jnp.bfloat16):
    entries = scale * jax.random.normal(own_key, extent, jnp.float32)
    if cuts:
        entries = entries * block_scale(own_key, extent, cuts, -0.22, 0.18)
    return jnp.clip(spiked(entries, jax.random.fold_in(own_key, 3), *heavy), -most, most).astype(dtype)


def setup_inputs(seed: int = 0) -> dict:
    seeds = jax.random.split(jax.random.key(seed), 13)
    tokens = heavy_noise(seeds[0], (SEQS, L, D), 1.0, 6.0, ((0, 32),), (0, 2, 32, 2.75))
    cotangent = normal_values(seeds[1], (SEQS, L, D), 1.0, 6.0, ((0, 32),))
    segments = jax.vmap(lambda own: jnp.searchsorted(jnp.cumsum(ragged_sizes(own, DOCS, L, DOC_MOST, 0)), jnp.arange(L), side="right"))(jax.random.split(seeds[2], SEQS)).reshape((SEQS, L)).astype(jnp.int32)
    in_gain = jnp.clip(1.0 + 0.18 * jax.random.normal(seeds[3], (D,), jnp.float32), 0.099609375, 1.8984375).astype(jnp.bfloat16)
    weight_in = draw_weight_in(jax.random.fold_in(seeds[12], 71), 0)
    conv_weight = normal_values(seeds[5], (K, CONV), K ** -0.5, 3.0, ((1, 32),))
    conv_bias = normal_values(seeds[6], (CONV,), 0.5, 3.0, ((0, 32),))
    step_bias = jnp.clip(-9.0 + 4.0 * jax.random.uniform(seeds[7], (H,), jnp.float32) ** block_scale(seeds[7], (H,), ((0, 2),), -0.2, 0.2), -9.0, -5.0)
    decay_log = jnp.clip(2.75 * jax.random.uniform(seeds[8], (H,), jnp.float32) ** block_scale(seeds[8], (H,), ((0, 2),), -0.2, 0.2), 0.0, 2.75)
    skip_gain = jnp.clip(0.5 + 1.0 * jax.random.uniform(seeds[9], (H,), jnp.float32) ** block_scale(seeds[9], (H,), ((0, 2),), -0.2, 0.2), 0.5, 1.5)
    gate_gain = jnp.clip(1.0 + 0.18 * jax.random.normal(seeds[10], (DI,), jnp.float32), 0.099609375, 1.8984375).astype(jnp.bfloat16)
    weight_out = normal_values(seeds[11], (DI, D), DI ** -0.5, 0.15625, ((0, 32),))
    return {"tokens": tokens, "cotangent": cotangent, "segments": segments, "in_gain": in_gain, "weight_in": weight_in, "conv_weight": conv_weight, "conv_bias": conv_bias, "step_bias": step_bias, "decay_log": decay_log, "skip_gain": skip_gain, "gate_gain": gate_gain, "weight_out": weight_out}


epsilon = 1e-05

@jax.custom_vjp
def low(v):
    return lax.optimization_barrier(v.astype(jnp.bfloat16)).astype(jnp.float32)

@jax.custom_vjp
def low_back(v):
    return v

def low_keep(v):
    return (low(v), None)

def low_pass(kept, grad):
    return (grad,)

def back_keep(v):
    return (v, None)

def back_low(kept, grad):
    return (low(grad),)
low.defvjp(low_keep, low_pass)
low_back.defvjp(back_keep, back_low)

def root_norm(rows, gain):
    return rows * lax.rsqrt(lax.optimization_barrier(jnp.mean(rows * rows, axis=-1, keepdims=True)) + epsilon) * gain

def causal_conv(signal, docs, taps_weight, taps_bias):
    seqs, length, chans = signal.shape
    taps = taps_weight.shape[0]
    padded = jnp.pad(signal, ((0, 0), (taps - 1, 0), (0, 0)))
    doc_pad = jnp.pad(docs, ((0, 0), (taps - 1, 0)), constant_values=-1)
    total = jnp.zeros(signal.shape, jnp.float32) + taps_bias
    for offset in range(taps):
        window = padded[:, offset:offset + length]
        same = (doc_pad[:, offset:offset + length] == docs).astype(jnp.float32)[..., None]
        total = total + taps_weight[offset] * window * same
    return jax.nn.silu(total)

def span_update(state, pieces, rate, direct):
    block_x, block_step, block_b, block_c, block_doc, prev_doc = pieces
    width = block_x.shape[1]
    logs = jnp.cumsum(block_step * rate, axis=1)
    causal = jnp.arange(width)[:, None] >= jnp.arange(width)[None, :]
    joined = jnp.logical_and(causal[None], block_doc[:, :, None] == block_doc[:, None, :])[:, None]
    by_head = jnp.transpose(logs, (0, 2, 1))
    spread = by_head[:, :, :, None] - by_head[:, :, None, :]
    decay = jnp.exp(jnp.where(joined, spread, 0.0)) * joined.astype(jnp.float32)
    scores = jnp.einsum('sin,sjn->sij', block_c, block_b, precision=lax.Precision.HIGHEST)
    scaled = block_x * block_step[..., None]
    inside = jnp.einsum('shij,sjhp->sihp', decay * scores[:, None], scaled, precision=lax.Precision.HIGHEST)
    carried = (block_doc == prev_doc[:, None]).astype(jnp.float32)
    reach = jnp.exp(logs) * carried[:, :, None]
    outside = jnp.einsum('sin,shpn->sihp', block_c, state, precision=lax.Precision.HIGHEST) * reach[..., None]
    ending = (block_doc == block_doc[:, -1:]).astype(jnp.float32)
    tail = jnp.exp(logs[:, -1:, :] - logs) * ending[:, :, None]
    fresh = jnp.einsum('sjn,sjhp->shpn', block_b, scaled * tail[..., None], precision=lax.Precision.HIGHEST)
    keeping = jnp.exp(logs[:, -1, :]) * carried[:, -1:]
    state = state * keeping[:, :, None, None] + fresh
    return (state, inside + outside + block_x * direct[None, None, :, None])

def state_space(values, step, rate, inputs_b, outputs_c, docs, direct):
    seqs, length, heads, size = values.shape
    count = length // SPAN

    def split(arr):
        return jnp.swapaxes(arr.reshape((seqs, count, SPAN) + arr.shape[2:]), 0, 1)
    ends = docs.reshape(seqs, count, SPAN)[:, :, -1]
    prevs = jnp.concatenate([jnp.full((seqs, 1), -1, jnp.int32), ends[:, :-1]], axis=1).T
    start = jnp.zeros((seqs, heads, size, inputs_b.shape[-1]), jnp.float32)
    update = jax.checkpoint(lambda state, pieces: span_update(state, pieces, rate, direct))
    _, outs = lax.scan(update, start, (split(values), split(step), split(inputs_b), split(outputs_c), split(docs), prevs))
    return jnp.swapaxes(outs, 0, 1).reshape(seqs, length, heads, size)

def mixer(projected, taps_weight, taps_bias, bias_step, log_decay, direct, gain, docs):
    seqs, length, _ = projected.shape
    inner = gain.shape[0]
    chans = taps_bias.shape[0]
    heads = bias_step.shape[0]
    states = (chans - inner) // 2
    gate = projected[..., :inner]
    conv_in = projected[..., inner:inner + chans]
    step_raw = projected[..., inner + chans:]
    conv_out = causal_conv(conv_in, docs, taps_weight, taps_bias)
    values = conv_out[..., :inner].reshape(seqs, length, heads, inner // heads)
    inputs_b = conv_out[..., inner:inner + states]
    outputs_c = conv_out[..., inner + states:]
    step = jax.nn.softplus(step_raw + bias_step)
    rate = -jnp.exp(log_decay)
    scanned = state_space(values, step, rate, inputs_b, outputs_c, docs, direct).reshape(seqs, length, inner)
    gated = scanned * jax.nn.silu(gate)
    return gated * lax.rsqrt(lax.optimization_barrier(jnp.mean(gated * gated, axis=-1, keepdims=True)) + epsilon) * gain

def reference(tokens, cotangent, segments, in_gain, weight_in, conv_weight, conv_bias, step_bias, decay_log, skip_gain, gate_gain, weight_out):
    floats = [arr.astype(jnp.float32) for arr in (tokens, in_gain, weight_in, conv_weight, conv_bias, step_bias, decay_log, skip_gain, gate_gain, weight_out)]
    group = 4
    total = tokens.shape[0]

    def forward(inputs, gain_in, proj_in, taps_weight, taps_bias, bias_step, log_decay, direct, gain_gate, proj_out):

        def one_group(blocks):
            block_in, block_doc = blocks
            rows = block_in.reshape(-1, D)
            normed = low(root_norm(rows, gain_in))
            projected = low_back(jnp.dot(normed, proj_in, precision=lax.Precision.HIGHEST))
            mixed = mixer(projected.reshape(group, L, -1), taps_weight, taps_bias, bias_step, log_decay, direct, gain_gate, block_doc)
            mixed = low(mixed.reshape(rows.shape[0], -1))
            result = rows + low_back(jnp.dot(mixed, proj_out, precision=lax.Precision.HIGHEST))
            return result.reshape(block_in.shape)
        outs = lax.map(jax.checkpoint(one_group), (inputs.reshape(total // group, group, L, D), segments.reshape(total // group, group, L)))
        return outs.reshape(inputs.shape)
    result, pull_back = jax.vjp(forward, *floats)
    grads = pull_back(cotangent.astype(jnp.float32))
    return (result.astype(jnp.bfloat16), grads[0].astype(jnp.bfloat16), grads[1], grads[2], grads[3], grads[4], grads[5], grads[6], grads[7], grads[8], grads[9])
```

```python
import functools

import jax
import jax.numpy as jnp
import numpy as np
from jax import lax
from jax.experimental import pallas as pl
from jax.experimental.pallas import tpu as pltpu
from jax.sharding import PartitionSpec as P

EPS = 1e-05
LOG2E = 1.4426950408889634
NEG = -1e30
f32, bf16 = jnp.float32, jnp.bfloat16
Q = 128
VM = 60 * 1024 * 1024

D, DI, CONV, N, HD = 768, 1536, 1792, 128, 64


def dot(a, b):
    return lax.dot_general(a, b, (((1,), (0,)), ((), ())), preferred_element_type=f32)


def dot_nt(a, b):
    return lax.dot_general(a, b, (((1,), (1,)), ((), ())), preferred_element_type=f32)


def dot_tn(a, b):
    return lax.dot_general(a, b, (((0,), (0,)), ((), ())), preferred_element_type=f32)


def sigmoid(v):
    return 1.0 / (1.0 + jnp.exp(-v))


def cumsum_rows(v, reverse=False):
    rows = lax.broadcasted_iota(jnp.int32, v.shape, 0)
    count = v.shape[0]
    shift = 1
    while shift < count:
        if reverse:
            moved = pltpu.roll(v, count - shift, 0)
            v = v + jnp.where(rows < count - shift, moved, 0.0)
        else:
            moved = pltpu.roll(v, shift, 0)
            v = v + jnp.where(rows >= shift, moved, 0.0)
        shift *= 2
    return v


def step_terms(z):
    e = jnp.exp(-jnp.abs(z))
    soft = jnp.maximum(z, 0.0) + jnp.log1p(e)
    tiny = z < -15.0
    log_soft = jnp.where(tiny, z, jnp.log(jnp.where(tiny, 1.0, soft)))
    return soft, log_soft


def scan_factors(z, rate, doc, prev_doc):
    soft, log_soft = step_terms(z)
    a = cumsum_rows(soft * (rate * LOG2E))
    b = a - log_soft * LOG2E
    last = a[Q - 1 : Q, :]
    last_doc = doc[Q - 1 : Q, :]
    reach = jnp.where(doc == prev_doc, jnp.exp2(a), 0.0)
    tail = jnp.where(doc == last_doc, jnp.exp2(last - b), 0.0)
    keep = jnp.where(last_doc == prev_doc, jnp.exp2(last), 0.0)
    return soft, a, b, reach, tail, keep


def pair_of(cols, p, low):
    left = jnp.broadcast_to(cols[:, 2 * p : 2 * p + 1], low.shape)
    right = jnp.broadcast_to(cols[:, 2 * p + 1 : 2 * p + 2], low.shape)
    return jnp.where(low, left, right)


def forward_scan_kernel(heads, per_seq, tok, wc, gain, cw, cb, sb, rate, skip, docc, docr, m1, m2, m3,
                        cin_o, pre_o, nrm_o, scan_o, st_o, z_o, pbuf, vbuf, state, pdoc):
    i = pl.program_id(0)

    @pl.when(lax.rem(i, per_seq) == 0)
    def _():
        pbuf[0:8, :] = jnp.zeros((8, CONV), f32)
        state[...] = jnp.zeros_like(state)
        pdoc[...] = jnp.full(pdoc.shape, -1.0, f32)

    x = tok[...].astype(f32)
    r = lax.rsqrt(jnp.mean(x * x, axis=-1, keepdims=True) + EPS)
    nb = (x * r * gain[...]).astype(bf16)
    nrm_o[...] = nb
    proj = dot(nb, wc[...])
    z = proj[:, CONV:] + sb[...]
    z_o[...] = z
    pbuf[8 : 8 + Q, :] = proj[:, :CONV]
    masks = (m3[...].astype(f32), m2[...].astype(f32), m1[...].astype(f32))
    for t in range(CONV // 128):
        cols = slice(128 * t, 128 * t + 128)
        now = pbuf[8 : 8 + Q, cols]
        cin_o[:, cols] = now.astype(bf16)
        pre = cb[:, cols] + cw[3:4, cols] * now
        for k in range(3):
            pre = pre + cw[k : k + 1, cols] * (pbuf[5 + k : 5 + k + Q, cols] * masks[k])
        pre_o[:, cols] = pre.astype(bf16)
        vbuf[:, cols] = (pre * sigmoid(pre)).astype(bf16)
    pbuf[0:8, :] = pbuf[Q : Q + 8, :]

    doc = docc[...]
    prev = pdoc[0:1, :]
    soft, a, b, reach, tail, keep = scan_factors(z, rate[...], doc, prev)
    pdoc[...] = jnp.broadcast_to(doc[Q - 1 : Q, :], pdoc.shape)
    bt = b.T
    row = lax.broadcasted_iota(jnp.int32, (Q, Q), 0)
    lane = lax.broadcasted_iota(jnp.int32, (Q, Q), 1)
    joined = (row >= lane) & (doc == docr[0, 0:1, :])
    low = lane < HD
    low_row = low[0:1, :]
    bmat = vbuf[:, DI : DI + N]
    cmat = vbuf[:, DI + N :]
    bt_mat = bmat.astype(f32).T.astype(bf16)
    s = dot_nt(cmat, bmat)
    st_low = state[...].astype(bf16)
    st_o[0] = st_low
    cs = dot(cmat, st_low)
    zero = jnp.zeros((Q, Q), bf16)
    for p in range(heads // 2):
        cols = slice(128 * p, 128 * p + 128)
        parts = []
        for h in (2 * p, 2 * p + 1):
            spread = jnp.broadcast_to(a[:, h : h + 1], (Q, Q)) - bt[h : h + 1, :]
            parts.append((jnp.exp2(jnp.where(joined, spread, NEG)) * s).astype(bf16))
        xp = vbuf[:, cols]
        xbd = jnp.concatenate([jnp.where(low, xp, zero), jnp.where(low, zero, xp)], axis=0)
        y = dot(jnp.concatenate(parts, axis=1), xbd)
        xf = xp.astype(f32)
        y = y + cs[:, cols] * pair_of(reach, p, low) + xf * skip[:, cols]
        scan_o[:, cols] = y.astype(bf16)
        xw = (xf * pair_of(tail, p, low)).astype(bf16)
        state[:, cols] = state[:, cols] * pair_of(keep, p, low_row) + dot(bt_mat, xw)


def forward_scan(tok, wc, gain, cw, cb, sb, rate, skip, docc, docr, m1, m2, m3, heads, seqs):
    rows = tok.shape[0]
    n = rows // Q
    one = pl.Buffered(buffer_count=1)
    full = lambda arr: pl.BlockSpec(arr.shape, lambda i: (0,) * arr.ndim, pipeline_mode=one)
    blk = lambda w: pl.BlockSpec((Q, w), lambda i: (i, 0))
    return pl.pallas_call(
        functools.partial(forward_scan_kernel, heads, n // seqs),
        grid=(n,),
        in_specs=[blk(D), full(wc), full(gain), full(cw), full(cb), full(sb), full(rate), full(skip),
                  blk(128), pl.BlockSpec((1, 8, 128), lambda i: (i, 0, 0)), blk(128), blk(128), blk(128)],
        out_specs=[blk(CONV), blk(CONV), blk(D), blk(DI), pl.BlockSpec((1, N, DI), lambda i: (i, 0, 0)), blk(128)],
        out_shape=[jax.ShapeDtypeStruct((rows, CONV), bf16), jax.ShapeDtypeStruct((rows, CONV), bf16),
                   jax.ShapeDtypeStruct((rows, D), bf16), jax.ShapeDtypeStruct((rows, DI), bf16),
                   jax.ShapeDtypeStruct((n, N, DI), bf16), jax.ShapeDtypeStruct((rows, 128), f32)],
        scratch_shapes=[pltpu.VMEM((Q + 8, CONV), f32), pltpu.VMEM((Q, CONV), bf16),
                        pltpu.VMEM((N, DI), f32), pltpu.VMEM((8, 128), f32)],
        compiler_params=pltpu.CompilerParams(vmem_limit_bytes=VM),
        name="forward_scan",
    )(tok, wc, gain, cw, cb, sb, rate, skip, docc, docr, m1, m2, m3)


def gate_kernel(nrm, scan, cot, tok, wg_abs, wo, gg, order, out_o, dscan_o, gn_o, gwg_o, gwo_o, acc_g, acc_o, wg):
    i = pl.program_id(0)

    @pl.when(i == 0)
    def _():
        acc_g[...] = jnp.zeros_like(acc_g)
        acc_o[...] = jnp.zeros_like(acc_o)
        wg[...] = dot_tn(order[...], wg_abs[...]).astype(bf16)

    nb = nrm[...]
    up = cot[...]
    gate = dot(nb, wg[...])
    sig = sigmoid(gate)
    act = gate * sig
    sc = scan[...].astype(f32)
    gated = sc * act
    rr = lax.rsqrt(jnp.mean(gated * gated, axis=-1, keepdims=True) + EPS)
    unit = gated * rr
    mixed = (unit * gg[...]).astype(bf16)
    out_o[...] = (tok[...].astype(f32) + dot(mixed, wo[...])).astype(bf16)
    acc_o[...] += dot_tn(mixed, up)
    gm = dot_nt(up, wo[...])
    e = gm * gg[...]
    dgated = rr * (e - unit * jnp.mean(unit * e, axis=-1, keepdims=True))
    dscan_o[...] = (dgated * act).astype(bf16)
    dgate = (dgated * sc * (sig + act * (1.0 - sig))).astype(bf16)
    acc_g[...] += dot_tn(nb, dgate)
    gn_o[...] = dot_nt(dgate, wg[...])

    @pl.when(i == pl.num_programs(0) - 1)
    def _():
        gwg_o[...] = dot(order[...], acc_g[...].astype(bf16)).astype(bf16)
        gwo_o[...] = acc_o[...].astype(bf16)


def gate_pass(nrm, scan, cot, tok, wg, wo, gg, order, bm=256):
    rows = nrm.shape[0]
    one = pl.Buffered(buffer_count=1)
    full = lambda shape: pl.BlockSpec(shape, lambda i: (0,) * len(shape), pipeline_mode=one)
    blk = lambda w: pl.BlockSpec((bm, w), lambda i: (i, 0))
    return pl.pallas_call(
        gate_kernel,
        grid=(rows // bm,),
        in_specs=[blk(D), blk(DI), blk(D), blk(D), full(wg.shape), full(wo.shape), full(gg.shape), full(order.shape)],
        out_specs=[blk(D), blk(DI), blk(D), full((D, DI)), full((DI, D))],
        out_shape=[jax.ShapeDtypeStruct((rows, D), bf16), jax.ShapeDtypeStruct((rows, DI), bf16),
                   jax.ShapeDtypeStruct((rows, D), f32), jax.ShapeDtypeStruct((D, DI), bf16),
                   jax.ShapeDtypeStruct((DI, D), bf16)],
        scratch_shapes=[pltpu.VMEM((D, DI), f32), pltpu.VMEM((DI, D), f32), pltpu.VMEM((D, DI), bf16)],
        compiler_params=pltpu.CompilerParams(vmem_limit_bytes=VM),
        name="gate_pass",
    )(nrm, scan, cot, tok, wg, wo, gg, order)


def head_sums(v, onehot):
    hi = v.astype(bf16)
    lo = (v - hi.astype(f32)).astype(bf16)
    return dot(hi, onehot) + dot(lo, onehot)


def backward_scan_kernel(heads, per_seq, dscan, cin, pre_r, z_r, st, cw, rate, skip, docc, docr, pdocr, m1, m2, m3, onehot,
                         dproj_o, gcw_o, gcb_o, gsk_o, ghd_o,
                         vbuf, dbuf, dstate, p1buf, qbuf, xwbuf, rowbuf, lastbuf, mbuf):
    i = pl.program_id(0)

    @pl.when(i == 0)
    def _():
        gcw_o[...] = jnp.zeros_like(gcw_o)
        gcb_o[...] = jnp.zeros_like(gcb_o)
        gsk_o[...] = jnp.zeros_like(gsk_o)
        ghd_o[...] = jnp.zeros_like(ghd_o)
        rowbuf[...] = jnp.zeros_like(rowbuf)

    @pl.when(lax.rem(i, per_seq) == 0)
    def _():
        mbuf[:, Q : Q + 8, :] = jnp.zeros((3, 8, CONV), f32)
        dstate[...] = jnp.zeros_like(dstate)

    for t in range(CONV // 128):
        cols = slice(128 * t, 128 * t + 128)
        pre = pre_r[:, cols].astype(f32)
        vbuf[:, cols] = (pre * sigmoid(pre)).astype(bf16)

    z = z_r[...]
    doc = docc[...]
    prev = pdocr[0, 0:1, :]
    soft, a, b, reach, tail, keep = scan_factors(z, rate[...], doc, prev)
    at = a.T
    row = lax.broadcasted_iota(jnp.int32, (Q, Q), 0)
    lane = lax.broadcasted_iota(jnp.int32, (Q, Q), 1)
    joined = (lane >= row) & (doc == docr[0, 0:1, :])
    low = lane < HD
    low_row = low[0:1, :]
    bmat = vbuf[:, DI : DI + N]
    cmat = vbuf[:, DI + N :]
    ct_mat = cmat.astype(f32).T.astype(bf16)
    s = dot_nt(bmat, cmat)
    st_low = st[0]
    ds_low = dstate[...].astype(bf16)
    cs = dot(cmat, st_low)
    bd = dot(bmat, ds_low)
    zero = jnp.zeros((Q, Q), bf16)
    dst = jnp.zeros((Q, Q), f32)
    for p in range(heads // 2):
        cols = slice(128 * p, 128 * p + 128)
        xp = vbuf[:, cols]
        dy = dscan[:, cols]
        dybd = jnp.concatenate([jnp.where(low, dy, zero), jnp.where(low, zero, dy)], axis=0)
        dm = dot_nt(xp, dybd)
        parts = []
        for n, h in enumerate((2 * p, 2 * p + 1)):
            spread = at[h : h + 1, :] - jnp.broadcast_to(b[:, h : h + 1], (Q, Q))
            e = jnp.exp2(jnp.where(joined, spread, NEG))
            m = (e * s).astype(bf16)
            parts.append(m)
            dmh = dm[:, 128 * n : 128 * n + 128]
            dst = dst + dmh * e
            rowbuf[h : h + 1, :] = jnp.sum(dmh * m.astype(f32), axis=0, keepdims=True)
        dx = dot(jnp.concatenate(parts, axis=1), dybd)
        xf = xp.astype(f32)
        dyf = dy.astype(f32)
        tp = pair_of(tail, p, low)
        dx_fresh = bd[:, cols] * tp
        p1buf[:, cols] = xf * (dx + dx_fresh)
        dyr = (dyf * pair_of(reach, p, low)).astype(bf16)
        qbuf[:, cols] = dyr.astype(f32) * cs[:, cols]
        keep_p = pair_of(keep, p, low_row)
        ds = dstate[:, cols]
        lastbuf[0:1, cols] = jnp.sum(xf * dx_fresh, axis=0, keepdims=True) + keep_p * jnp.sum(
            ds * st_low[:, cols].astype(f32), axis=0, keepdims=True)
        gsk_o[:, cols] += jnp.sum((dyf * xf).reshape(-1, 8, 128), axis=0)
        dbuf[:, cols] = dx + dx_fresh + skip[:, cols] * dyf
        xwbuf[:, cols] = (xf * tp).astype(bf16)
        xwbuf[:, DI + 128 * p : DI + 128 * p + 128] = dyr
        dstate[:, cols] = ds * keep_p + dot(ct_mat, dyr)
    dst_low = dst.astype(bf16)
    dbuf[:, DI : DI + N] = dot(dst_low, cmat) + dot_nt(xwbuf[:, :DI], ds_low)
    dbuf[:, DI + N :] = dot_tn(dst_low, bmat) + dot_nt(xwbuf[:, DI:], st_low)
    hot = onehot[...]
    p1 = head_sums(p1buf[...], hot)
    last = head_sums(jnp.broadcast_to(lastbuf[0:1, :], (8, DI)), hot)[0:1, :]
    da = head_sums(qbuf[...], hot) - p1 + rowbuf[...].T
    g = cumsum_rows(da, reverse=True) + last
    sig = sigmoid(z)
    ratio = jnp.where(z < -15.0, 1.0, sig / jnp.where(z < -15.0, 1.0, soft))
    dz = g * rate[...] * sig + p1 * ratio
    dproj_o[:, CONV:] = dz.astype(bf16)
    ghd_o[0:8, :] += jnp.sum(dz.reshape(-1, 8, 128), axis=0)
    ghd_o[8:16, :] += jnp.sum((g * soft).reshape(-1, 8, 128), axis=0)

    masks = (m3[...].astype(f32), m2[...].astype(f32), m1[...].astype(f32))
    for t in range(CONV // 128):
        cols = slice(128 * t, 128 * t + 128)
        pre = pre_r[:, cols].astype(f32)
        sg = sigmoid(pre)
        dpre = dbuf[:, cols] * (sg * (1.0 + pre * (1.0 - sg)))
        cv = cin[:, cols].astype(f32)
        dcin = cw[3:4, cols] * dpre
        gcb_o[:, cols] += jnp.sum(dpre.reshape(-1, 8, 128), axis=0)
        gcw_o[24:32, cols] += jnp.sum((cv * dpre).reshape(-1, 8, 128), axis=0)
        for k in range(3):
            s_ = 3 - k
            mbuf[k, 0:Q, cols] = dpre * masks[k]
            moved = mbuf[k, s_ : s_ + Q, cols]
            dcin = dcin + cw[k : k + 1, cols] * moved
            gcw_o[8 * k : 8 * k + 8, cols] += jnp.sum((cv * moved).reshape(-1, 8, 128), axis=0)
        dproj_o[:, cols] = dcin.astype(bf16)
    mbuf[:, Q : Q + 8, :] = mbuf[:, 0:8, :]


def backward_scan(dscan, cin, pre, z, st, cw, rate, skip, docc, docr, pdocr, m1, m2, m3, onehot, heads, seqs):
    rows = dscan.shape[0]
    n = rows // Q
    one = pl.Buffered(buffer_count=1)
    full = lambda shape: pl.BlockSpec(shape, lambda i: (0,) * len(shape), pipeline_mode=one)
    blk = lambda w: pl.BlockSpec((Q, w), lambda i: (n - 1 - i, 0))
    blk3 = lambda s1, s2: pl.BlockSpec((1, s1, s2), lambda i: (n - 1 - i, 0, 0))
    return pl.pallas_call(
        functools.partial(backward_scan_kernel, heads, n // seqs),
        grid=(n,),
        in_specs=[blk(DI), blk(CONV), blk(CONV), blk(128), blk3(N, DI), full(cw.shape), full(rate.shape), full(skip.shape),
                  blk(128), blk3(8, 128), blk3(8, 128), blk(128), blk(128), blk(128), full(onehot.shape)],
        out_specs=[blk(CONV + 128), full((32, CONV)), full((8, CONV)), full((8, DI)), full((16, 128))],
        out_shape=[jax.ShapeDtypeStruct((rows, CONV + 128), bf16), jax.ShapeDtypeStruct((32, CONV), f32),
                   jax.ShapeDtypeStruct((8, CONV), f32), jax.ShapeDtypeStruct((8, DI), f32),
                   jax.ShapeDtypeStruct((16, 128), f32)],
        scratch_shapes=[pltpu.VMEM((Q, CONV), bf16), pltpu.VMEM((Q, CONV), f32), pltpu.VMEM((N, DI), f32),
                        pltpu.VMEM((Q, DI), f32), pltpu.VMEM((Q, DI), f32), pltpu.VMEM((Q, 2 * DI), bf16),
                        pltpu.VMEM((128, 128), f32), pltpu.VMEM((8, DI), f32), pltpu.VMEM((3, Q + 8, CONV), f32)],
        compiler_params=pltpu.CompilerParams(vmem_limit_bytes=VM),
        name="backward_scan",
    )(dscan, cin, pre, z, st, cw, rate, skip, docc, docr, pdocr, m1, m2, m3, onehot)


def norm_back_kernel(dproj, gn, tok, cot, wc, gain, order, out_o):
    grad = gn[...] + dot_nt(dproj[...], wc[...])
    x = tok[...].astype(f32)
    r = lax.rsqrt(jnp.mean(x * x, axis=-1, keepdims=True) + EPS)
    unit = x * r
    e = gain[...] * grad
    back = r * (e - unit * jnp.mean(unit * e, axis=-1, keepdims=True))
    res = (cot[...].astype(f32) + back).astype(bf16)
    out_o[...] = dot_nt(res, order[...]).astype(bf16)


def norm_back(dproj, gn, tok, cot, wc, gain, order, bm=512):
    rows = dproj.shape[0]
    one = pl.Buffered(buffer_count=1)
    full = lambda shape: pl.BlockSpec(shape, lambda i: (0,) * len(shape), pipeline_mode=one)
    blk = lambda w: pl.BlockSpec((bm, w), lambda i: (i, 0))
    return pl.pallas_call(
        norm_back_kernel,
        grid=(rows // bm,),
        in_specs=[blk(CONV + 128), blk(D), blk(D), blk(D), full(wc.shape), full(gain.shape), full(order.shape)],
        out_specs=blk(D),
        out_shape=jax.ShapeDtypeStruct((rows, D), bf16),
        compiler_params=pltpu.CompilerParams(vmem_limit_bytes=VM),
        name="norm_back",
    )(dproj, gn, tok, cot, wc, gain, order)


def stages_of(mesh):
    ndp, nf = mesh.shape["dp"], mesh.shape["fsdp"]
    out = []
    stride = 1
    while stride < nf:
        group = 2 if stride == 1 else min(4, nf // stride)
        out.append(("fsdp", stride, group, stride))
        stride *= group
    stride = 1
    while stride < ndp:
        group = min(4, ndp // stride)
        out.append(("dp", stride, group, stride * nf))
        stride *= group
    return out[::-1]


def swap(arr, axis, size, offset):
    return lax.ppermute(arr, axis, [(i, i ^ offset) for i in range(size)])


def gather_slots(shard, stages, sizes):
    block = shard
    for axis, stride, group, _ in stages:
        block = jnp.stack([block] + [swap(block, axis, sizes[axis], k * stride) for k in range(1, group)])
    return block


def scatter_slots(terms, stages, sizes):
    low, kept = terms, terms
    for axis, stride, group, _ in stages[::-1]:
        got = [swap(low[k], axis, sizes[axis], k * stride) for k in range(1, group)]
        kept = kept[0].astype(f32)
        for part in got:
            kept = kept + part.astype(f32)
        low = kept.astype(bf16)
    return kept


def three_parts(v):
    hi = lax.reduce_precision(v, 8, 7)
    mid = lax.reduce_precision(v - hi, 8, 7)
    return jnp.concatenate([hi.astype(bf16), mid.astype(bf16), (v - hi - mid).astype(bf16)])


def whole_parts(v):
    hi, mid, lo = jnp.split(v.astype(f32), 3, axis=-1)
    return (hi + mid + lo).reshape(-1)


def doc_terms(segments):
    seqs, length = segments.shape
    rows = seqs * length
    n = rows // Q
    seg = segments.astype(f32)
    pad = jnp.pad(seg, ((0, 0), (3, 0)), constant_values=-1.0)
    wide = lambda v: jnp.broadcast_to(v.reshape(rows, 1), (rows, 128))
    same = [wide((pad[:, 3 - s : 3 - s + length] == seg).astype(f32)) for s in (1, 2, 3)]
    docr = jnp.broadcast_to(seg.reshape(n, 1, Q), (n, 8, Q))
    ends = seg.reshape(seqs, length // Q, Q)[:, :, -1]
    prev = jnp.concatenate([jnp.full((seqs, 1), -1.0, f32), ends[:, :-1]], axis=1).reshape(n, 1, 1)
    return wide(seg), docr, jnp.broadcast_to(prev, (n, 8, 128)), same


def local(mesh, tokens, cotangent, segments, in_gain, weight_in, conv_weight, conv_bias, step_bias, decay_log, skip_gain,
          gate_gain, weight_out):
    sizes = {"dp": mesh.shape["dp"], "fsdp": mesh.shape["fsdp"]}
    nf = sizes["fsdp"]
    nd = sizes["dp"] * nf
    axes = ("dp", "fsdp")
    stages = stages_of(mesh)
    me = lax.axis_index("dp") * nf + lax.axis_index("fsdp")
    seqs, length, _ = tokens.shape
    rows = seqs * length
    ri, ro, cc, share = weight_in.shape[0], weight_out.shape[0], conv_bias.shape[0], step_bias.shape[0]
    heads = share * nf
    free = 128 - heads

    rel = np.zeros((1,), np.int32)
    for _, _, group, stride in stages:
        rel = (np.arange(group, dtype=np.int32)[:, None] * stride + rel[None, :]).reshape(-1)
    device = jnp.asarray(rel) ^ me
    feature = (device[:, None] * ri + jnp.arange(ri)[None, :]).reshape(-1)
    order = (jnp.arange(D)[:, None] == feature[None, :]).astype(bf16)
    slot_hot = (device[:, None] == jnp.arange(nd)[None, :]).astype(bf16)

    small = jnp.concatenate([in_gain, conv_weight.reshape(-1), conv_bias, gate_gain, three_parts(step_bias),
                             three_parts(decay_log), three_parts(skip_gain)])
    small = jnp.pad(small, (0, ri * free - small.shape[0])).reshape(ri, free)
    gathered = gather_slots(jnp.concatenate([weight_in[:, DI:], small], axis=1), stages, sizes)
    wc = gathered.reshape(D, CONV + 128)
    later = jnp.concatenate([weight_in[:, :DI], weight_out.reshape(2, ri, D).transpose(1, 0, 2).reshape(ri, DI)], axis=0)
    later = lax.all_gather(later, axes, axis=0)
    tok = tokens.reshape(rows, D)
    up = cotangent.reshape(rows, D)
    tok_s = jnp.dot(tok, order, preferred_element_type=bf16)
    up_s = jnp.dot(up, order, preferred_element_type=bf16)
    docc, docr, pdocr, same = doc_terms(segments)

    packed = gathered.reshape(nd, ri, CONV + 128)[:, :, CONV + heads :].reshape(nd, ri * free)
    gain = packed[:, :ri].reshape(1, D).astype(f32)
    packed = lax.dot_general(slot_hot, packed, (((0,), (0,)), ((), ())), preferred_element_type=f32)
    at = ri
    cw = packed[:, at : at + 4 * cc].reshape(nd, 4, cc).transpose(1, 0, 2).reshape(4, CONV)
    at += 4 * cc
    cb = packed[:, at : at + cc].reshape(1, CONV)
    at += cc
    gg = packed[:, at : at + ro].reshape(1, DI)
    at += ro
    per_head = []
    for _ in range(3):
        per_head.append(whole_parts(packed[:nf, at : at + 3 * share]))
        at += 3 * share
    lanes = lambda v: jnp.pad(v, (0, 128 - heads))[None]
    rate = lanes(-jnp.exp(per_head[1]))
    skip = jnp.repeat(per_head[2], HD)[None]
    cw = jnp.pad(cw, ((0, 4), (0, 0)))
    onehot = (jnp.arange(DI)[:, None] // HD == jnp.arange(128)[None, :]).astype(bf16)

    cin, pre, nrm, scan, st, z = forward_scan(
        tok_s, wc, gain, cw, cb, lanes(per_head[0]), rate, skip, docc, docr, *same, heads, seqs)

    wg = later[:, :ri].reshape(D, DI)
    wo = later[:, ri:].reshape(nd, ri, 2, D).transpose(0, 2, 1, 3).reshape(DI, D)
    out, dscan, gn, gwg, gwo = gate_pass(nrm, scan, up, tok, wg, wo, gg, order)
    early = jnp.concatenate([gwg.reshape(nd, ri, DI), gwo.reshape(nd, 2, ri, D).transpose(0, 2, 1, 3).reshape(nd, ri, DI)], axis=1)
    early = lax.psum_scatter(early, axes, scatter_dimension=0)

    dproj, gcw, gcb, gsk, ghd = backward_scan(
        dscan, cin, pre, z, st, cw, rate, skip, docc, docr, pdocr, *same, onehot, heads, seqs)
    gwc = lax.dot_general(nrm, dproj, (((0,), (0,)), ((), ())), preferred_element_type=f32).astype(bf16)

    taps = jnp.concatenate([gcw.reshape(4, 8, CONV).sum(1), gcb.sum(0)[None]], axis=0)
    taps = taps.reshape(5, nd, cc).transpose(1, 0, 2).reshape(nd, 5 * cc)
    head_terms = jnp.stack([ghd[:8].sum(0)[:heads], ghd[8:16].sum(0)[:heads] * rate[0, :heads],
                            gsk.sum(0).reshape(heads, HD).sum(1)])
    head_terms = jnp.tile(head_terms.reshape(3, nf, share).transpose(1, 0, 2).reshape(nf, 3 * share), (nd // nf, 1))
    terms = jnp.concatenate([taps, head_terms], axis=1)
    hi = lax.reduce_precision(terms, 8, 7)
    both = jnp.concatenate([hi, terms - hi], axis=1).astype(bf16)
    both = jnp.dot(slot_hot, both, preferred_element_type=f32).astype(bf16)
    width = 5 * cc + 3 * share
    both = jnp.pad(both, ((0, 0), (0, ri * free - 2 * width))).reshape(nd, ri, free)
    gwc = jnp.concatenate([gwc.reshape(nd, ri, CONV + 128)[:, :, : CONV + heads], both], axis=2)
    total = scatter_slots(gwc.reshape([g for _, _, g, _ in stages[::-1]] + [ri, CONV + 128]), stages, sizes)

    gtok = norm_back(dproj, gn, tok_s, up_s, wc, gain, order)

    early = early.astype(f32)
    g_in = jnp.concatenate([early[:ri], total[:, : CONV + heads]], axis=1)
    g_out = early[ri:].reshape(ri, 2, D).transpose(1, 0, 2).reshape(ro, D)
    packed = total[:, CONV + heads :].reshape(-1)
    packed = packed[:width] + packed[width : 2 * width]
    g_in_gain = jnp.sum(weight_in.astype(f32) * g_in, axis=1) / in_gain.astype(f32)
    g_gate_gain = jnp.sum(weight_out.astype(f32) * g_out, axis=1) / gate_gain.astype(f32)
    by_head = packed[5 * cc :].reshape(3, share)
    return (out.reshape(tokens.shape), gtok.reshape(tokens.shape), g_in_gain, g_in, packed[: 4 * cc].reshape(4, cc),
            packed[4 * cc : 5 * cc], by_head[0], by_head[1], by_head[2], g_gate_gain, g_out)


def solution(mesh):
    every = ("dp", "fsdp")
    return jax.shard_map(
        functools.partial(local, mesh),
        mesh=mesh,
        in_specs=(P(every, None, None), P(every, None, None), P(every, None), P(every), P(every, None), P(None, every),
                  P(every), P("fsdp"), P("fsdp"), P("fsdp"), P(every), P(every, None)),
        out_specs=(P(every, None, None), P(every, None, None), P(every), P(every, None), P(None, every), P(every),
                   P("fsdp"), P("fsdp"), P("fsdp"), P(every), P(every, None)),
        check_vma=False,
    )
```

```python
import functools

import jax
import jax.numpy as jnp
import numpy as np
from jax import lax
from jax.experimental import pallas as pl
from jax.experimental.pallas import tpu as pltpu
from jax.sharding import PartitionSpec as P

EPS = 1e-05
LOG2E = 1.4426950408889634
NEG = -1e30
f32, bf16 = jnp.float32, jnp.bfloat16
Q = 128
VM = 60 * 1024 * 1024

D, DI, CONV, N, HD = 768, 1536, 1792, 128, 64


def dot(a, b):
    return lax.dot_general(a, b, (((1,), (0,)), ((), ())), preferred_element_type=f32)


def dot_nt(a, b):
    return lax.dot_general(a, b, (((1,), (1,)), ((), ())), preferred_element_type=f32)


def dot_tn(a, b):
    return lax.dot_general(a, b, (((0,), (0,)), ((), ())), preferred_element_type=f32)


def sigmoid(v):
    return 1.0 / (1.0 + jnp.exp(-v))


def cumsum_rows(v, reverse=False):
    rows = lax.broadcasted_iota(jnp.int32, v.shape, 0)
    count = v.shape[0]
    shift = 1
    while shift < count:
        if reverse:
            moved = pltpu.roll(v, count - shift, 0)
            v = v + jnp.where(rows < count - shift, moved, 0.0)
        else:
            moved = pltpu.roll(v, shift, 0)
            v = v + jnp.where(rows >= shift, moved, 0.0)
        shift *= 2
    return v


def step_terms(z):
    e = jnp.exp(-jnp.abs(z))
    soft = jnp.maximum(z, 0.0) + jnp.log1p(e)
    tiny = z < -15.0
    log_soft = jnp.where(tiny, z, jnp.log(jnp.where(tiny, 1.0, soft)))
    return soft, log_soft


def marks(mark):
    mark = mark.astype(f32)
    doc = jnp.floor(mark * 0.25)
    age = mark - 4.0 * doc
    return doc, [(age > s - 0.5).astype(f32) for s in (3, 2, 1)]


def scan_factors(z, rate, doc, prev_doc):
    soft, log_soft = step_terms(z)
    a = cumsum_rows(soft * (rate * LOG2E))
    b = a - log_soft * LOG2E
    last = a[Q - 1 : Q, :]
    last_doc = doc[Q - 1 : Q, :]
    reach = jnp.where(doc == prev_doc, jnp.exp2(a), 0.0)
    tail = jnp.where(doc == last_doc, jnp.exp2(last - b), 0.0)
    keep = jnp.where(last_doc == prev_doc, jnp.exp2(last), 0.0)
    return soft, a, b, reach, tail, keep


def pair_of(cols, p, low):
    left = jnp.broadcast_to(cols[:, 2 * p : 2 * p + 1], low.shape)
    right = jnp.broadcast_to(cols[:, 2 * p + 1 : 2 * p + 2], low.shape)
    return jnp.where(low, left, right)


def forward_scan_kernel(heads, per_seq, tok, wc, gain, cw, cb, sb, rate, skip, mark, docr,
                        cin_o, pre_o, nrm_o, scan_o, st_o, z_o, pbuf, vbuf, state, pdoc):
    i = pl.program_id(0)

    @pl.when(lax.rem(i, per_seq) == 0)
    def _():
        pbuf[0:8, :] = jnp.zeros((8, CONV), f32)
        state[...] = jnp.zeros_like(state)
        pdoc[...] = jnp.full(pdoc.shape, -1.0, f32)

    x = tok[...].astype(f32)
    r = lax.rsqrt(jnp.mean(x * x, axis=-1, keepdims=True) + EPS)
    nb = (x * r * gain[...]).astype(bf16)
    nrm_o[...] = nb
    proj = dot(nb, wc[...])
    z = proj[:, CONV:] + sb[...]
    z_o[...] = z
    pbuf[8 : 8 + Q, :] = proj[:, :CONV]
    doc, masks = marks(mark[...])
    for t in range(CONV // 128):
        cols = slice(128 * t, 128 * t + 128)
        now = pbuf[8 : 8 + Q, cols]
        cin_o[:, cols] = now.astype(bf16)
        pre = cb[:, cols] + cw[3:4, cols] * now
        for k in range(3):
            pre = pre + cw[k : k + 1, cols] * (pbuf[5 + k : 5 + k + Q, cols] * masks[k])
        pre_o[:, cols] = pre.astype(bf16)
        vbuf[:, cols] = (pre * sigmoid(pre)).astype(bf16)
    pbuf[0:8, :] = pbuf[Q : Q + 8, :]

    prev = pdoc[0:1, :]
    soft, a, b, reach, tail, keep = scan_factors(z, rate[...], doc, prev)
    pdoc[...] = jnp.broadcast_to(doc[Q - 1 : Q, :], pdoc.shape)
    bt = b.T
    row = lax.broadcasted_iota(jnp.int32, (Q, Q), 0)
    lane = lax.broadcasted_iota(jnp.int32, (Q, Q), 1)
    joined = (row >= lane) & (doc == docr[0, 0:1, :])
    low = lane < HD
    low_row = low[0:1, :]
    bmat = vbuf[:, DI : DI + N]
    cmat = vbuf[:, DI + N :]
    bt_mat = bmat.astype(f32).T.astype(bf16)
    s = dot_nt(cmat, bmat)
    st_low = state[...].astype(bf16)
    st_o[0] = st_low
    cs = dot(cmat, st_low)
    zero = jnp.zeros((Q, Q), bf16)
    for p in range(heads // 2):
        cols = slice(128 * p, 128 * p + 128)
        parts = []
        for h in (2 * p, 2 * p + 1):
            spread = jnp.broadcast_to(a[:, h : h + 1], (Q, Q)) - bt[h : h + 1, :]
            parts.append((jnp.exp2(jnp.where(joined, spread, NEG)) * s).astype(bf16))
        xp = vbuf[:, cols]
        xbd = jnp.concatenate([jnp.where(low, xp, zero), jnp.where(low, zero, xp)], axis=0)
        y = dot(jnp.concatenate(parts, axis=1), xbd)
        xf = xp.astype(f32)
        y = y + cs[:, cols] * pair_of(reach, p, low) + xf * skip[:, cols]
        scan_o[:, cols] = y.astype(bf16)
        xw = (xf * pair_of(tail, p, low)).astype(bf16)
        state[:, cols] = state[:, cols] * pair_of(keep, p, low_row) + dot(bt_mat, xw)


def forward_scan(tok, wc, gain, cw, cb, sb, rate, skip, mark, docr, heads, seqs):
    rows = tok.shape[0]
    n = rows // Q
    one = pl.Buffered(buffer_count=1)
    full = lambda arr: pl.BlockSpec(arr.shape, lambda i: (0,) * arr.ndim, pipeline_mode=one)
    blk = lambda w: pl.BlockSpec((Q, w), lambda i: (i, 0))
    return pl.pallas_call(
        functools.partial(forward_scan_kernel, heads, n // seqs),
        grid=(n,),
        in_specs=[blk(D), full(wc), full(gain), full(cw), full(cb), full(sb), full(rate), full(skip),
                  blk(128), pl.BlockSpec((1, 8, 128), lambda i: (i, 0, 0))],
        out_specs=[blk(CONV), blk(CONV), blk(D), blk(DI), pl.BlockSpec((1, N, DI), lambda i: (i, 0, 0)), blk(128)],
        out_shape=[jax.ShapeDtypeStruct((rows, CONV), bf16), jax.ShapeDtypeStruct((rows, CONV), bf16),
                   jax.ShapeDtypeStruct((rows, D), bf16), jax.ShapeDtypeStruct((rows, DI), bf16),
                   jax.ShapeDtypeStruct((n, N, DI), bf16), jax.ShapeDtypeStruct((rows, 128), f32)],
        scratch_shapes=[pltpu.VMEM((Q + 8, CONV), f32), pltpu.VMEM((Q, CONV), bf16),
                        pltpu.VMEM((N, DI), f32), pltpu.VMEM((8, 128), f32)],
        compiler_params=pltpu.CompilerParams(vmem_limit_bytes=VM),
        name="forward_scan",
    )(tok, wc, gain, cw, cb, sb, rate, skip, mark, docr)


def block_order(ri):
    row = lax.broadcasted_iota(jnp.int32, (192, 192), 0)
    lane = lax.broadcasted_iota(jnp.int32, (192, 192), 1)
    second = lane >= 96
    at = jnp.where(second, lane - 96, lane)
    owner = lax.div(at, ri)
    target = owner * (2 * ri) + (at - owner * ri) + jnp.where(second, ri, 0)
    return (row == target).astype(bf16)


def gate_kernel(ri, nrm, scan, cot, later, gg, order, mixed_o, dscan_o, dgate_o, early_o, wo_o, wg_o, acc_g, acc_o, wg, wo):
    i = pl.program_id(0)

    @pl.when(i == 0)
    def _():
        acc_g[...] = jnp.zeros_like(acc_g)
        acc_o[...] = jnp.zeros_like(acc_o)
        wg[...] = dot_tn(order[...], later[:, :DI]).astype(bf16)
        blocks = block_order(ri)
        for g in range(D // 96):
            at = slice(96 * g, 96 * g + 96)
            halves = jnp.concatenate([later[at, DI : DI + D], later[at, DI + D :]], axis=0)
            wo[192 * g : 192 * g + 192, :] = dot(blocks, halves).astype(bf16)
        wo_o[...] = wo[...]
        wg_o[...] = wg[...]

    nb = nrm[...]
    up = cot[...]
    gate = dot(nb, wg[...])
    sig = sigmoid(gate)
    act = gate * sig
    sc = scan[...].astype(f32)
    gated = sc * act
    rr = lax.rsqrt(jnp.mean(gated * gated, axis=-1, keepdims=True) + EPS)
    unit = gated * rr
    mixed = (unit * gg[...]).astype(bf16)
    mixed_o[...] = mixed
    acc_o[...] += dot_tn(mixed, up)
    e = dot_nt(up, wo[...]) * gg[...]
    dgated = rr * (e - unit * jnp.mean(unit * e, axis=-1, keepdims=True))
    dscan_o[...] = (dgated * act).astype(bf16)
    dgate = (dgated * sc * (sig + act * (1.0 - sig))).astype(bf16)
    dgate_o[...] = dgate
    acc_g[...] += dot_tn(nb, dgate)

    @pl.when(i == pl.num_programs(0) - 1)
    def _():
        early_o[:, :DI] = dot(order[...], acc_g[...].astype(bf16)).astype(bf16)
        blocks = block_order(ri)
        for g in range(D // 96):
            at = slice(96 * g, 96 * g + 96)
            halves = dot_tn(blocks, acc_o[192 * g : 192 * g + 192, :].astype(bf16)).astype(bf16)
            early_o[at, DI : DI + D] = halves[:96]
            early_o[at, DI + D :] = halves[96:]


def gate_pass(nrm, scan, cot, later, gg, order, ri, bm=256):
    rows = nrm.shape[0]
    one = pl.Buffered(buffer_count=1)
    full = lambda shape: pl.BlockSpec(shape, lambda i: (0,) * len(shape), pipeline_mode=one)
    blk = lambda w: pl.BlockSpec((bm, w), lambda i: (i, 0))
    low = lambda *shape: jax.ShapeDtypeStruct(shape, bf16)
    return pl.pallas_call(
        functools.partial(gate_kernel, ri),
        grid=(rows // bm,),
        in_specs=[blk(D), blk(DI), blk(D), full(later.shape), full(gg.shape), full(order.shape)],
        out_specs=[blk(DI), blk(DI), blk(DI), full((D, 2 * DI)), full((DI, D)), full((D, DI))],
        out_shape=[low(rows, DI), low(rows, DI), low(rows, DI), low(D, 2 * DI), low(DI, D), low(D, DI)],
        scratch_shapes=[pltpu.VMEM((D, DI), f32), pltpu.VMEM((DI, D), f32), pltpu.VMEM((D, DI), bf16),
                        pltpu.VMEM((DI, D), bf16)],
        compiler_params=pltpu.CompilerParams(vmem_limit_bytes=VM),
        name="gate_pass",
    )(nrm, scan, cot, later, gg, order)


def out_kernel(mixed, tok, wo, out_o):
    out_o[...] = (tok[...].astype(f32) + dot(mixed[...], wo[...])).astype(bf16)


def out_pass(mixed, tok, wo, bm=512):
    rows = tok.shape[0]
    blk = lambda w: pl.BlockSpec((bm, w), lambda i: (i, 0))
    return pl.pallas_call(
        out_kernel,
        grid=(rows // bm,),
        in_specs=[blk(DI), blk(D), pl.BlockSpec((DI, D), lambda i: (0, 0), pipeline_mode=pl.Buffered(buffer_count=1))],
        out_specs=blk(D),
        out_shape=jax.ShapeDtypeStruct((rows, D), bf16),
        compiler_params=pltpu.CompilerParams(vmem_limit_bytes=VM),
        name="out_pass",
    )(mixed, tok, wo)


def head_sums(v, onehot):
    hi = v.astype(bf16)
    lo = (v - hi.astype(f32)).astype(bf16)
    return dot(hi, onehot) + dot(lo, onehot)


def backward_scan_kernel(heads, per_seq, dscan, cin, pre_r, z_r, st, cw, rate, skip, mark, docr, pdocr,
                         dproj_o, gcw_o, gcb_o, gsk_o, ghd_o,
                         vbuf, dbuf, dstate, p1buf, qbuf, xwbuf, rowbuf, lastbuf, mbuf, onehot):
    i = pl.program_id(0)

    @pl.when(i == 0)
    def _():
        gcw_o[...] = jnp.zeros_like(gcw_o)
        gcb_o[...] = jnp.zeros_like(gcb_o)
        gsk_o[...] = jnp.zeros_like(gsk_o)
        ghd_o[...] = jnp.zeros_like(ghd_o)
        rowbuf[...] = jnp.zeros_like(rowbuf)
        head = lax.broadcasted_iota(jnp.int32, onehot.shape, 0) >> 6
        onehot[...] = (head == lax.broadcasted_iota(jnp.int32, onehot.shape, 1)).astype(bf16)

    @pl.when(lax.rem(i, per_seq) == 0)
    def _():
        mbuf[:, Q : Q + 8, :] = jnp.zeros((3, 8, CONV), f32)
        dstate[...] = jnp.zeros_like(dstate)

    for t in range(CONV // 128):
        cols = slice(128 * t, 128 * t + 128)
        pre = pre_r[:, cols].astype(f32)
        vbuf[:, cols] = (pre * sigmoid(pre)).astype(bf16)

    z = z_r[...]
    doc, masks = marks(mark[...])
    prev = pdocr[0, 0:1, :]
    soft, a, b, reach, tail, keep = scan_factors(z, rate[...], doc, prev)
    at = a.T
    row = lax.broadcasted_iota(jnp.int32, (Q, Q), 0)
    lane = lax.broadcasted_iota(jnp.int32, (Q, Q), 1)
    joined = (lane >= row) & (doc == docr[0, 0:1, :])
    low = lane < HD
    low_row = low[0:1, :]
    bmat = vbuf[:, DI : DI + N]
    cmat = vbuf[:, DI + N :]
    ct_mat = cmat.astype(f32).T.astype(bf16)
    s = dot_nt(bmat, cmat)
    st_low = st[0]
    ds_low = dstate[...].astype(bf16)
    cs = dot(cmat, st_low)
    bd = dot(bmat, ds_low)
    zero = jnp.zeros((Q, Q), bf16)
    dst = jnp.zeros((Q, Q), f32)
    for p in range(heads // 2):
        cols = slice(128 * p, 128 * p + 128)
        xp = vbuf[:, cols]
        dy = dscan[:, cols]
        dybd = jnp.concatenate([jnp.where(low, dy, zero), jnp.where(low, zero, dy)], axis=0)
        dm = dot_nt(xp, dybd)
        parts = []
        for n, h in enumerate((2 * p, 2 * p + 1)):
            spread = at[h : h + 1, :] - jnp.broadcast_to(b[:, h : h + 1], (Q, Q))
            e = jnp.exp2(jnp.where(joined, spread, NEG))
            m = (e * s).astype(bf16)
            parts.append(m)
            dmh = dm[:, 128 * n : 128 * n + 128]
            dst = dst + dmh * e
            rowbuf[h : h + 1, :] = jnp.sum(dmh * m.astype(f32), axis=0, keepdims=True)
        dx = dot(jnp.concatenate(parts, axis=1), dybd)
        xf = xp.astype(f32)
        dyf = dy.astype(f32)
        tp = pair_of(tail, p, low)
        dx_fresh = bd[:, cols] * tp
        p1buf[:, cols] = xf * (dx + dx_fresh)
        dyr = (dyf * pair_of(reach, p, low)).astype(bf16)
        qbuf[:, cols] = dyr.astype(f32) * cs[:, cols]
        keep_p = pair_of(keep, p, low_row)
        ds = dstate[:, cols]
        lastbuf[0:1, cols] = jnp.sum(xf * dx_fresh, axis=0, keepdims=True) + keep_p * jnp.sum(
            ds * st_low[:, cols].astype(f32), axis=0, keepdims=True)
        gsk_o[:, cols] += jnp.sum((dyf * xf).reshape(-1, 8, 128), axis=0)
        dbuf[:, cols] = dx + dx_fresh + skip[:, cols] * dyf
        xwbuf[:, cols] = (xf * tp).astype(bf16)
        xwbuf[:, DI + 128 * p : DI + 128 * p + 128] = dyr
        dstate[:, cols] = ds * keep_p + dot(ct_mat, dyr)
    dst_low = dst.astype(bf16)
    dbuf[:, DI : DI + N] = dot(dst_low, cmat) + dot_nt(xwbuf[:, :DI], ds_low)
    dbuf[:, DI + N :] = dot_tn(dst_low, bmat) + dot_nt(xwbuf[:, DI:], st_low)
    hot = onehot[...]
    p1 = head_sums(p1buf[...], hot)
    last = head_sums(jnp.broadcast_to(lastbuf[0:1, :], (8, DI)), hot)[0:1, :]
    da = head_sums(qbuf[...], hot) - p1 + rowbuf[...].T
    g = cumsum_rows(da, reverse=True) + last
    sig = sigmoid(z)
    ratio = jnp.where(z < -15.0, 1.0, sig / jnp.where(z < -15.0, 1.0, soft))
    dz = g * rate[...] * sig + p1 * ratio
    dproj_o[:, CONV:] = dz.astype(bf16)
    ghd_o[0:8, :] += jnp.sum(dz.reshape(-1, 8, 128), axis=0)
    ghd_o[8:16, :] += jnp.sum((g * soft).reshape(-1, 8, 128), axis=0)

    for t in range(CONV // 128):
        cols = slice(128 * t, 128 * t + 128)
        pre = pre_r[:, cols].astype(f32)
        sg = sigmoid(pre)
        dpre = dbuf[:, cols] * (sg * (1.0 + pre * (1.0 - sg)))
        cv = cin[:, cols].astype(f32)
        dcin = cw[3:4, cols] * dpre
        gcb_o[:, cols] += jnp.sum(dpre.reshape(-1, 8, 128), axis=0)
        gcw_o[24:32, cols] += jnp.sum((cv * dpre).reshape(-1, 8, 128), axis=0)
        for k in range(3):
            s_ = 3 - k
            mbuf[k, 0:Q, cols] = dpre * masks[k]
            moved = mbuf[k, s_ : s_ + Q, cols]
            dcin = dcin + cw[k : k + 1, cols] * moved
            gcw_o[8 * k : 8 * k + 8, cols] += jnp.sum((cv * moved).reshape(-1, 8, 128), axis=0)
        dproj_o[:, cols] = dcin.astype(bf16)
    mbuf[:, Q : Q + 8, :] = mbuf[:, 0:8, :]


def backward_scan(dscan, cin, pre, z, st, cw, rate, skip, mark, docr, pdocr, heads, seqs):
    rows = dscan.shape[0]
    n = rows // Q
    one = pl.Buffered(buffer_count=1)
    full = lambda shape: pl.BlockSpec(shape, lambda i: (0,) * len(shape), pipeline_mode=one)
    blk = lambda w: pl.BlockSpec((Q, w), lambda i: (n - 1 - i, 0))
    blk3 = lambda s1, s2: pl.BlockSpec((1, s1, s2), lambda i: (n - 1 - i, 0, 0))
    return pl.pallas_call(
        functools.partial(backward_scan_kernel, heads, n // seqs),
        grid=(n,),
        in_specs=[blk(DI), blk(CONV), blk(CONV), blk(128), blk3(N, DI), full(cw.shape), full(rate.shape), full(skip.shape),
                  blk(128), blk3(8, 128), blk3(8, 128)],
        out_specs=[blk(CONV + 128), full((32, CONV)), full((8, CONV)), full((8, DI)), full((16, 128))],
        out_shape=[jax.ShapeDtypeStruct((rows, CONV + 128), bf16), jax.ShapeDtypeStruct((32, CONV), f32),
                   jax.ShapeDtypeStruct((8, CONV), f32), jax.ShapeDtypeStruct((8, DI), f32),
                   jax.ShapeDtypeStruct((16, 128), f32)],
        scratch_shapes=[pltpu.VMEM((Q, CONV), bf16), pltpu.VMEM((Q, CONV), f32), pltpu.VMEM((N, DI), f32),
                        pltpu.VMEM((Q, DI), f32), pltpu.VMEM((Q, DI), f32), pltpu.VMEM((Q, 2 * DI), bf16),
                        pltpu.VMEM((128, 128), f32), pltpu.VMEM((8, DI), f32), pltpu.VMEM((3, Q + 8, CONV), f32),
                        pltpu.VMEM((DI, 128), bf16)],
        compiler_params=pltpu.CompilerParams(vmem_limit_bytes=VM),
        name="backward_scan",
    )(dscan, cin, pre, z, st, cw, rate, skip, mark, docr, pdocr)


def norm_back_kernel(dproj, dgate, tok, cot, wc, wg, gain, order, out_o):
    grad = dot_nt(dgate[...], wg[...]) + dot_nt(dproj[...], wc[...])
    x = tok[...].astype(f32)
    r = lax.rsqrt(jnp.mean(x * x, axis=-1, keepdims=True) + EPS)
    unit = x * r
    e = gain[...] * grad
    back = r * (e - unit * jnp.mean(unit * e, axis=-1, keepdims=True))
    res = (cot[...].astype(f32) + back).astype(bf16)
    out_o[...] = dot_nt(res, order[...]).astype(bf16)


def norm_back(dproj, dgate, tok, cot, wc, wg, gain, order, bm=512):
    rows = dproj.shape[0]
    one = pl.Buffered(buffer_count=1)
    full = lambda shape: pl.BlockSpec(shape, lambda i: (0,) * len(shape), pipeline_mode=one)
    blk = lambda w: pl.BlockSpec((bm, w), lambda i: (i, 0))
    return pl.pallas_call(
        norm_back_kernel,
        grid=(rows // bm,),
        in_specs=[blk(CONV + 128), blk(DI), blk(D), blk(D), full(wc.shape), full(wg.shape), full(gain.shape), full(order.shape)],
        out_specs=blk(D),
        out_shape=jax.ShapeDtypeStruct((rows, D), bf16),
        compiler_params=pltpu.CompilerParams(vmem_limit_bytes=VM),
        name="norm_back",
    )(dproj, dgate, tok, cot, wc, wg, gain, order)


def stages_of(mesh):
    ndp, nf = mesh.shape["dp"], mesh.shape["fsdp"]
    out = []
    stride = 1
    while stride < nf:
        group = 2 if stride == 1 else min(4, nf // stride)
        out.append(("fsdp", stride, group, stride))
        stride *= group
    stride = 1
    while stride < ndp:
        group = min(4, ndp // stride)
        out.append(("dp", stride, group, stride * nf))
        stride *= group
    return out[::-1]


def swap(arr, axis, size, offset):
    return lax.ppermute(arr, axis, [(i, i ^ offset) for i in range(size)])


def gather_stage(block, stage, sizes):
    axis, stride, group, _ = stage
    return jnp.stack([block] + [swap(block, axis, sizes[axis], k * stride) for k in range(1, group)])


def scatter_stage(kept, stage, sizes):
    axis, stride, group, _ = stage
    low = kept.astype(bf16)
    got = [swap(low[k], axis, sizes[axis], k * stride) for k in range(1, group)]
    total = kept[0].astype(f32)
    for part in got:
        total = total + part.astype(f32)
    return total


def before(value, *others):
    return lax.optimization_barrier((value,) + others)


def three_parts(v):
    hi = lax.reduce_precision(v, 8, 7)
    mid = lax.reduce_precision(v - hi, 8, 7)
    return jnp.concatenate([hi, mid, v - hi - mid], axis=0).astype(bf16)


def row(v):
    return jnp.pad(v, ((0, 0), (0, 128 - v.shape[1])))


def doc_terms(segments):
    seqs, length = segments.shape
    rows = seqs * length
    n = rows // Q
    seg = segments.astype(f32)
    pad = jnp.pad(seg, ((0, 0), (3, 0)), constant_values=-1.0)
    mark = 4.0 * seg
    for s in (1, 2, 3):
        mark = mark + (pad[:, 3 - s : 3 - s + length] == seg).astype(f32)
    mark = jnp.broadcast_to(mark.astype(bf16).reshape(rows, 1), (rows, 128))
    docr = jnp.broadcast_to(seg.reshape(n, 1, Q), (n, 8, Q))
    ends = seg.reshape(seqs, length // Q, Q)[:, :, -1]
    prev = jnp.concatenate([jnp.full((seqs, 1), -1.0, f32), ends[:, :-1]], axis=1).reshape(n, 1, 1)
    return mark, docr, jnp.broadcast_to(prev, (n, 8, 128))


def local(mesh, tokens, cotangent, segments, in_gain, weight_in, conv_weight, conv_bias, step_bias, decay_log, skip_gain,
          gate_gain, weight_out):
    sizes = {"dp": mesh.shape["dp"], "fsdp": mesh.shape["fsdp"]}
    nf = sizes["fsdp"]
    nd = sizes["dp"] * nf
    axes = ("dp", "fsdp")
    stages = stages_of(mesh)
    me = lax.axis_index("dp") * nf + lax.axis_index("fsdp")
    seqs, length, _ = tokens.shape
    rows = seqs * length
    ri, ro, cc, share = weight_in.shape[0], weight_out.shape[0], conv_bias.shape[0], step_bias.shape[0]
    heads = share * nf
    free = 128 - heads

    rel = np.zeros((1,), np.int32)
    for _, _, group, stride in stages:
        rel = (np.arange(group, dtype=np.int32)[:, None] * stride + rel[None, :]).reshape(-1)
    device = jnp.asarray(rel) ^ me
    feature = (device[:, None] * ri + jnp.arange(ri)[None, :]).reshape(-1)
    order = (jnp.arange(D)[:, None] == feature[None, :]).astype(bf16)
    slot_hot = (device[:, None] == jnp.arange(nd)[None, :]).astype(bf16)

    later = jnp.concatenate([weight_in[:, :DI], weight_out[:ri], weight_out[ri:]], axis=1)
    later = lax.all_gather(later, axes, axis=0, tiled=True)
    wc = jnp.pad(weight_in[:, DI:], ((0, 0), (0, 128 - heads)))
    small = jnp.concatenate([row(in_gain[None]), row(conv_weight), row(conv_bias[None]), row(gate_gain[None]),
                             row(three_parts(jnp.stack([step_bias, decay_log, skip_gain])))], axis=0)
    tok = tokens.reshape(rows, D)
    up = cotangent.reshape(rows, D)
    mark, docr, pdocr = doc_terms(segments)
    wc = gather_stage(wc, stages[0], sizes)
    wc, order, mark, docr, pdocr, small = before(wc, order, mark, docr, pdocr, small)
    for stage in stages:
        small = gather_stage(small, stage, sizes)
    for stage in stages[1:-1]:
        wc = gather_stage(wc, stage, sizes)
    tok_s = jnp.dot(tok, order, preferred_element_type=bf16)
    up_s = jnp.dot(up, order, preferred_element_type=bf16)

    small = small.reshape(nd, 16 * 128)
    gain = small[:, :ri].reshape(1, D).astype(f32)
    small = lax.dot_general(slot_hot, small, (((0,), (0,)), ((), ())), preferred_element_type=f32).reshape(nd, 16, 128)
    cw = jnp.pad(small[:, 1:5, :cc].transpose(1, 0, 2).reshape(4, CONV), ((0, 4), (0, 0)))
    cb = small[:, 5, :cc].reshape(1, CONV)
    gg = small[:, 6, :ro].reshape(1, DI)
    per_head = small[:nf, 7:16, :share]
    per_head = (per_head[:, 0:3] + per_head[:, 3:6] + per_head[:, 6:9]).transpose(1, 0, 2).reshape(3, heads)
    lanes = lambda v: jnp.pad(v, (0, 128 - heads))[None]
    sb = lanes(per_head[0])
    rate = lanes(-jnp.exp(per_head[1]))
    skip = jnp.repeat(per_head[2], HD)[None]
    wc, tok_s, up_s, gain, cw, cb, gg, sb, rate, skip = before(wc, tok_s, up_s, gain, cw, cb, gg, sb, rate, skip)
    wc = gather_stage(wc, stages[-1], sizes).reshape(D, CONV + 128)

    cin, pre, nrm, scan, st, z = forward_scan(
        tok_s, wc, gain, cw, cb, sb, rate, skip, mark, docr, heads, seqs)
    mixed, dscan, dgate, early, wo, wg = gate_pass(nrm, scan, up, later, gg, order, ri)
    early = lax.psum_scatter(early, axes, scatter_dimension=0, tiled=True)

    dproj, gcw, gcb, gsk, ghd = backward_scan(
        dscan, cin, pre, z, st, cw, rate, skip, mark, docr, pdocr, heads, seqs)
    gwc = lax.dot_general(nrm, dproj, (((0,), (0,)), ((), ())), preferred_element_type=f32).astype(bf16)

    taps = jnp.concatenate([gcw.reshape(4, 8, CONV).sum(1), gcb.sum(0)[None]], axis=0)
    taps = taps.reshape(5, nd, cc).transpose(1, 0, 2).reshape(nd, 5 * cc)
    head_terms = jnp.stack([ghd[:8].sum(0)[:heads], ghd[8:16].sum(0)[:heads] * rate[0, :heads],
                            gsk.sum(0).reshape(heads, HD).sum(1)])
    head_terms = jnp.tile(head_terms.reshape(3, nf, share).transpose(1, 0, 2).reshape(nf, 3 * share), (nd // nf, 1))
    terms = jnp.concatenate([taps, head_terms], axis=1)
    hi = lax.reduce_precision(terms, 8, 7)
    both = jnp.concatenate([hi, terms - hi], axis=1).astype(bf16)
    both = jnp.dot(slot_hot, both, preferred_element_type=f32).astype(bf16)
    width = 5 * cc + 3 * share
    both = jnp.pad(both, ((0, 0), (0, ri * free - 2 * width))).reshape(nd, ri, free)
    gwc = jnp.concatenate([gwc.reshape(nd, ri, CONV + 128)[:, :, : CONV + heads], both], axis=2)
    total = gwc.reshape([g for _, _, g, _ in stages[::-1]] + [ri, CONV + 128])
    for at, stage in enumerate(stages[::-1]):
        if at == len(stages) - 2:
            total, gain = before(total, gain)
            gtok = norm_back(dproj, dgate, tok_s, up_s, wc, wg, gain, order)
        if at == len(stages) - 1:
            total, gtok, wo = before(total, gtok, wo)
        total = scatter_stage(total, stage, sizes)
    out = out_pass(mixed, tok, wo)

    early = early.astype(f32)
    g_in = jnp.concatenate([early[:, :DI], total[:, : CONV + heads]], axis=1)
    g_out = jnp.concatenate([early[:, DI : DI + D], early[:, DI + D :]], axis=0)
    packed = total[:, CONV + heads :].reshape(-1)
    packed = packed[:width] + packed[width : 2 * width]
    g_in_gain = jnp.sum(weight_in.astype(f32) * g_in, axis=1) / in_gain.astype(f32)
    g_gate_gain = jnp.sum(weight_out.astype(f32) * g_out, axis=1) / gate_gain.astype(f32)
    by_head = packed[5 * cc :].reshape(3, share)
    return (out.reshape(tokens.shape), gtok.reshape(tokens.shape), g_in_gain, g_in, packed[: 4 * cc].reshape(4, cc),
            packed[4 * cc : 5 * cc], by_head[0], by_head[1], by_head[2], g_gate_gain, g_out)


def solution(mesh):
    every = ("dp", "fsdp")
    return jax.shard_map(
        functools.partial(local, mesh),
        mesh=mesh,
        in_specs=(P(every, None, None), P(every, None, None), P(every, None), P(every), P(every, None), P(None, every),
                  P(every), P("fsdp"), P("fsdp"), P("fsdp"), P(every), P(every, None)),
        out_specs=(P(every, None, None), P(every, None, None), P(every), P(every, None), P(None, every), P(every),
                   P("fsdp"), P("fsdp"), P("fsdp"), P(every), P(every, None)),
        check_vma=False,
    )
```

```python
import functools

import jax
import jax.numpy as jnp
import numpy as np
from jax import lax
from jax.experimental import pallas as pl
from jax.experimental.pallas import tpu as pltpu
from jax.sharding import PartitionSpec as P

EPS = 1e-05
LOG2E = 1.4426950408889634
NEG = -1e30
f32, bf16 = jnp.float32, jnp.bfloat16
Q = 128
VM = 60 * 1024 * 1024

D, DI, CONV, N, HD = 768, 1536, 1792, 128, 64


def dot(a, b):
    return lax.dot_general(a, b, (((1,), (0,)), ((), ())), preferred_element_type=f32)


def dot_nt(a, b):
    return lax.dot_general(a, b, (((1,), (1,)), ((), ())), preferred_element_type=f32)


def dot_tn(a, b):
    return lax.dot_general(a, b, (((0,), (0,)), ((), ())), preferred_element_type=f32)


def sigmoid(v):
    return 1.0 / (1.0 + jnp.exp(-v))


def cumsum_rows(v, reverse=False):
    rows = lax.broadcasted_iota(jnp.int32, v.shape, 0)
    count = v.shape[0]
    shift = 1
    while shift < count:
        if reverse:
            moved = pltpu.roll(v, count - shift, 0)
            v = v + jnp.where(rows < count - shift, moved, 0.0)
        else:
            moved = pltpu.roll(v, shift, 0)
            v = v + jnp.where(rows >= shift, moved, 0.0)
        shift *= 2
    return v


def step_terms(z):
    e = jnp.exp(-jnp.abs(z))
    soft = jnp.maximum(z, 0.0) + jnp.log1p(e)
    tiny = z < -15.0
    log_soft = jnp.where(tiny, z, jnp.log(jnp.where(tiny, 1.0, soft)))
    return soft, log_soft


def columns(row):
    return jnp.broadcast_to(row, (Q, 128)).T


def documents(row, before_row, docs):
    doc = columns(row)
    docs[0:8, :] = columns(before_row)[Q - 8 : Q, :]
    docs[8 : 8 + Q, :] = doc
    return doc, [(docs[8 - s : 8 - s + Q, :] == doc).astype(f32) for s in (3, 2, 1)]


def scan_factors(z, rate, doc, prev_doc):
    soft, log_soft = step_terms(z)
    a = cumsum_rows(soft * (rate * LOG2E))
    b = a - log_soft * LOG2E
    last = a[Q - 1 : Q, :]
    last_doc = doc[Q - 1 : Q, :]
    reach = jnp.where(doc == prev_doc, jnp.exp2(a), 0.0)
    tail = jnp.where(doc == last_doc, jnp.exp2(last - b), 0.0)
    keep = jnp.where(last_doc == prev_doc, jnp.exp2(last), 0.0)
    return soft, a, b, reach, tail, keep


def pair_of(cols, p, low):
    left = jnp.broadcast_to(cols[:, 2 * p : 2 * p + 1], low.shape)
    right = jnp.broadcast_to(cols[:, 2 * p + 1 : 2 * p + 2], low.shape)
    return jnp.where(low, left, right)


def two_parts(cols):
    hi = cols.astype(bf16)
    return jnp.concatenate([hi, (cols - hi.astype(f32)).astype(bf16)], axis=1)


def head_onehot(shape):
    head = lax.broadcasted_iota(jnp.int32, shape, 1) >> 6
    return (lax.broadcasted_iota(jnp.int32, shape, 0) & 127 == head).astype(bf16)


def pack_kernel(ri, w_in, w_out, in_gain, cw, cb, gg, heads_in, wc_o, later_o, rows):
    wc_o[...] = jnp.zeros_like(wc_o)
    wc_o[0:ri, : w_in.shape[1] - DI] = w_in[:, DI:]
    rows[...] = jnp.zeros_like(rows)
    rows[0:1, : in_gain.shape[1]] = in_gain[...].astype(f32)
    rows[1:5, : cw.shape[1]] = cw[...].astype(f32)
    rows[5:6, : cb.shape[1]] = cb[...].astype(f32)
    rows[6:7, : gg.shape[1]] = gg[...].astype(f32)
    value = heads_in[...]
    for n in range(3):
        part = value.astype(bf16).astype(f32)
        rows[7 + 3 * n : 10 + 3 * n, : value.shape[1]] = part
        value = value - part
    wc_o[0:16, CONV + 128 :] = rows[...].astype(bf16)
    later_o[:, :DI] = w_in[:, :DI]
    later_o[:, DI : DI + D] = w_out[0:ri, :]
    later_o[:, DI + D :] = w_out[ri:, :]


def pack(w_in, w_out, in_gain, cw, cb, gg, heads_in, ri, tall):
    return pl.pallas_call(
        functools.partial(pack_kernel, ri),
        out_shape=[jax.ShapeDtypeStruct((tall, CONV + 256), bf16), jax.ShapeDtypeStruct((ri, 2 * DI), bf16)],
        scratch_shapes=[pltpu.VMEM((16, 128), f32)],
        name="pack",
    )(w_in, w_out, in_gain, cw, cb, gg, heads_in)


def unpack_small(ri, ro, share, small, device, onehot, gain, gain_abs, cw, cb, gg, heads_o, skip):
    nd = small.shape[1]
    slot = lax.broadcasted_iota(jnp.int32, (nd, 128), 0).astype(f32)[:, 0:1]
    owner = device[...][:, 0:1]

    def spread(rows, width, total, who):
        lane = lax.broadcasted_iota(jnp.int32, (128, total), 1).astype(f32)
        piece = jnp.floor((lane + 0.5) * (1.0 / width))
        inner = lane - piece * width
        pick = (lax.broadcasted_iota(jnp.int32, (128, total), 0).astype(f32) == inner).astype(bf16)
        mine = piece[0:1, :] == who
        return [jnp.sum(jnp.where(mine, dot(small[r].astype(bf16), pick), 0.0), axis=0, keepdims=True) for r in rows]

    gain[...] = spread([0], ri, D, slot)[0]
    gain_abs[...] = spread([0], ri, D, owner)[0]
    taps = spread(range(1, 6), CONV // nd, CONV, owner)
    for k in range(4):
        cw[k : k + 1, :] = 0.5 * taps[k]
    cw[4:8, :] = jnp.zeros((4, CONV), f32)
    cb[...] = 0.5 * taps[4]
    gg[...] = spread([6], ro, DI, owner)[0]
    parts = spread(range(7, 16), share, 128, owner)
    per_head = [parts[n] + parts[n + 3] + parts[n + 6] for n in range(3)]
    heads_o[0:1, :] = per_head[0]
    heads_o[1:2, :] = -jnp.exp(per_head[1])
    skip[...] = dot(two_parts(jnp.broadcast_to(per_head[2], (8, 128))), onehot[...])[0:1, :]


def forward_scan_kernel(heads, per_seq, ri, ro, share, first, tok, wc_a, wc_b, small, device, seg, seg_before,
                        cin_o, act_o, dact_o, nrm_o, scan_o, st_o, z_o, gain, gain_abs, cw, cb, gg, heads_o, skip,
                        pbuf, zbuf, nbuf, pnext, znext, nnext, state, docs, onehot, wc, sems):
    i = pl.program_id(0)
    tiles = CONV // 128

    def normed(block):
        x = block[...].astype(f32)
        r = lax.rsqrt(jnp.mean(x * x, axis=-1, keepdims=True) + EPS)
        nnext[...] = (x * r * gain[...]).astype(bf16)

    def project(t):
        part = dot(nnext[...], wc[:, 128 * t : 128 * t + 256])
        pnext[t] = part[:, :128]
        pnext[t + 1] = part[:, 128:]

    def project_step():
        znext[...] = dot(nnext[...], wc[:, CONV:]) + heads_o[0:1, :]

    def advance():
        pbuf[:, 8 : 8 + Q, :] = pnext[...]
        zbuf[...] = znext[...]
        nbuf[...] = nnext[...]

    @pl.when(i == 0)
    def _():
        rows = wc_a.shape[0]
        copies = [pltpu.make_async_copy(wc_a.at[:, : CONV + 128], wc.at[0:rows], sems.at[0]),
                  pltpu.make_async_copy(wc_b.at[:, : CONV + 128], wc.at[rows : 2 * rows], sems.at[1])]
        for copy in copies:
            copy.start()
        onehot[...] = head_onehot(onehot.shape)
        unpack_small(ri, ro, share, small, device, onehot, gain, gain_abs, cw, cb, gg, heads_o, skip)
        normed(first)
        for copy in copies:
            copy.wait()
        for t in range(0, tiles, 2):
            project(t)
        project_step()
        advance()

    @pl.when(lax.rem(i, per_seq) == 0)
    def _():
        pbuf[:, 0:8, :] = jnp.zeros((tiles, 8, 128), f32)
        state[...] = jnp.zeros_like(state)

    nrm_o[...] = nbuf[...]
    z = zbuf[...]
    z_o[...] = z
    doc_row = seg[0].astype(f32)
    before_row = jnp.where(lax.rem(i, per_seq) == 0, -1.0, seg_before[0].astype(f32))
    doc, masks = documents(doc_row, before_row, docs)
    prev = docs[7:8, :]
    soft, a, b, reach, tail, keep = scan_factors(z, heads_o[1:2, :], doc, prev)
    factors = two_parts(jnp.concatenate([reach, tail, jnp.broadcast_to(keep, (8, 128))], axis=0))
    bt = b.T
    row = lax.broadcasted_iota(jnp.int32, (Q, Q), 0)
    lane = lax.broadcasted_iota(jnp.int32, (Q, Q), 1)
    joined = (row >= lane) & (doc == doc_row)
    low = lane < HD
    zero = jnp.zeros((Q, Q), bf16)

    def conv(t):
        cols = slice(128 * t, 128 * t + 128)
        here = pbuf[t, 8 : 8 + Q, :]
        cin_o[:, cols] = here.astype(bf16)
        half = cb[:, cols] + cw[3:4, cols] * here
        for k in range(3):
            half = half + cw[k : k + 1, cols] * (pbuf[t, 5 + k : 5 + k + Q, :] * masks[k])
        pbuf[t, 0:8, :] = pbuf[t, Q : Q + 8, :]
        th = jnp.tanh(half)
        dact_o[:, cols] = ((1.0 + th) * (1.0 + half * (1.0 - th))).astype(bf16)
        act = (half + half * th).astype(bf16)
        act_o[:, cols] = act
        return act

    normed(tok)
    bmat = conv(tiles - 2)
    cmat = conv(tiles - 1)
    bt_mat = bmat.astype(f32).T.astype(bf16)
    s = dot_nt(cmat, bmat)
    for p in range(heads // 2):
        cols = slice(128 * p, 128 * p + 128)
        half = slice(128 * (p % 2), 128 * (p % 2) + 128)
        if p % 2 == 0:
            group = slice(128 * p, 128 * p + 256)
            wide = dot(factors, onehot[:, group])
            st_low = state[:, group].astype(bf16)
            st_o[0, :, group] = st_low
            cs = dot(cmat, st_low)
        xp = conv(p)
        if p < tiles // 2:
            project(2 * p)
        if p == tiles // 2:
            project_step()
        parts = []
        for h in (2 * p, 2 * p + 1):
            spread = jnp.broadcast_to(a[:, h : h + 1], (Q, Q)) - bt[h : h + 1, :]
            parts.append((jnp.exp2(jnp.where(joined, spread, NEG)) * s).astype(bf16))
        xbd = jnp.concatenate([jnp.where(low, xp, zero), jnp.where(low, zero, xp)], axis=0)
        y = dot(jnp.concatenate(parts, axis=1), xbd)
        xf = xp.astype(f32)
        y = y + cs[:, half] * wide[0:Q, half] + xf * skip[:, cols]
        scan_o[:, cols] = y.astype(bf16)
        xw = (xf * wide[Q : 2 * Q, half]).astype(bf16)
        state[:, cols] = state[:, cols] * wide[2 * Q : 2 * Q + 1, half] + dot(bt_mat, xw)
    advance()


def forward_scan(tok, wc_a, wc_b, small, device, seg, seqs, ri, ro, share, heads):
    rows = tok.shape[0]
    n = rows // Q
    one = pl.Buffered(buffer_count=1)
    full = lambda arr: pl.BlockSpec(arr.shape, lambda i: (0,) * arr.ndim, pipeline_mode=one)
    blk = lambda w: pl.BlockSpec((Q, w), lambda i: (i, 0))
    hbm = pl.BlockSpec(memory_space=pl.ANY)
    low = lambda *shape: jax.ShapeDtypeStruct(shape, bf16)
    sides = [(1, D), (1, D), (8, CONV), (1, CONV), (1, DI), (8, 128), (1, DI)]
    side = lambda shape: pl.BlockSpec(shape, lambda i: (0, 0))
    return pl.pallas_call(
        functools.partial(forward_scan_kernel, heads, n // seqs, ri, ro, share),
        grid=(n,),
        in_specs=[pl.BlockSpec((Q, D), lambda i: (0, 0), pipeline_mode=one),
                  pl.BlockSpec((Q, D), lambda i: (jnp.minimum(i + 1, n - 1), 0)), hbm, hbm, full(small), full(device),
                  pl.BlockSpec((1, 1, Q), lambda i: (i, 0, 0)), pl.BlockSpec((1, 1, Q), lambda i: (jnp.maximum(i - 1, 0), 0, 0))],
        out_specs=[blk(CONV), blk(CONV), blk(CONV), blk(D), blk(DI), pl.BlockSpec((1, N, DI), lambda i: (i, 0, 0)), blk(128)]
        + [side(shape) for shape in sides],
        out_shape=[low(rows, CONV), low(rows, CONV), low(rows, CONV), low(rows, D), low(rows, DI), low(n, N, DI),
                   jax.ShapeDtypeStruct((rows, 128), f32)] + [jax.ShapeDtypeStruct(shape, f32) for shape in sides],
        scratch_shapes=[pltpu.VMEM((CONV // 128, Q + 8, 128), f32), pltpu.VMEM((Q, 128), f32), pltpu.VMEM((Q, D), bf16),
                        pltpu.VMEM((CONV // 128, Q, 128), f32), pltpu.VMEM((Q, 128), f32), pltpu.VMEM((Q, D), bf16),
                        pltpu.VMEM((N, DI), f32), pltpu.VMEM((Q + 8, 128), f32), pltpu.VMEM((256, DI), bf16),
                        pltpu.VMEM((D, CONV + 128), bf16), pltpu.SemaphoreType.DMA((2,))],
        compiler_params=pltpu.CompilerParams(vmem_limit_bytes=VM),
        name="forward_scan",
    )(tok, tok, wc_a, wc_b, small, device, seg, seg)


def block_order(ri):
    row = lax.broadcasted_iota(jnp.int32, (192, 192), 0)
    lane = lax.broadcasted_iota(jnp.int32, (192, 192), 1)
    second = lane >= 96
    at = jnp.where(second, lane - 96, lane)
    owner = lax.div(at, ri)
    target = owner * (2 * ri) + (at - owner * ri) + jnp.where(second, ri, 0)
    return (row == target).astype(bf16)


def gate_kernel(ri, tok, scan, cot, later, gain, gg, mixed_o, dscan_o, dgate_o, early_o, wo, acc_g, acc_o,
                nb_s, nbt_s, mixt_s, h_s, e_s, gated_s, eg_s):
    i = pl.program_id(0)
    bm, high = 256, 32
    blocks = tok.shape[0] // bm

    @pl.when(i == 0)
    def _():
        acc_g[...] = jnp.zeros_like(acc_g)
        acc_o[...] = jnp.zeros_like(acc_o)
        put = block_order(ri)
        for g in range(D // 96):
            at = slice(96 * g, 96 * g + 96)
            halves = jnp.concatenate([later[at, DI : DI + D], later[at, DI + D :]], axis=0)
            wo[192 * g : 192 * g + 192, :] = dot(put, halves).astype(bf16)

    x = tok[...].astype(f32)
    r = lax.rsqrt(jnp.mean(x * x, axis=-1, keepdims=True) + EPS)
    nb = (x * r * gain[...]).astype(bf16)
    nb_s[...] = nb * 0.5
    nbt_s[...] = nb.T

    def products(n):
        rows = slice(bm * n, bm * n + bm)
        for c in range(DI // 256):
            cols = slice(256 * c, 256 * c + 256)
            h_s[rows, cols] = dot(nb_s[rows, :], later[:, cols])
            yield
            e_s[rows, cols] = dot_nt(cot[rows, :], wo[cols, :])
            yield

    def sums(n):
        rows = slice(bm * n, bm * n + bm)
        for c in range(DI // 256):
            cols = slice(256 * c, 256 * c + 256)
            mixt_s[cols, :] = mixed_o[rows, cols].T
        for c in range(D // 256):
            cols = slice(256 * c, 256 * c + 256)
            acc_o[:, cols] += dot(mixt_s[...], cot[rows, cols])
            yield
        for c in range(DI // 256):
            cols = slice(256 * c, 256 * c + 256)
            acc_g[:, cols] += dot(nbt_s[:, rows], dgate_o[rows, cols])
            yield

    def elementwise(n, part):
        rows = slice(bm * n + part * high, bm * n + part * high + high)
        squares = jnp.zeros((high, 128), f32)
        cross = jnp.zeros((high, 128), f32)
        for t in range(DI // 128):
            cols = slice(128 * t, 128 * t + 128)
            h = h_s[rows, cols]
            gated = scan[rows, cols].astype(f32) * (h + h * jnp.tanh(h))
            eg = e_s[rows, cols] * gg[:, cols]
            squares = squares + gated * gated
            cross = cross + gated * eg
            gated_s[part, :, cols] = gated
            eg_s[part, :, cols] = eg
        rr = lax.rsqrt(jnp.sum(squares, axis=-1, keepdims=True) * (1.0 / DI) + EPS)
        pull = rr * rr * rr * (jnp.sum(cross, axis=-1, keepdims=True) * (1.0 / DI))
        rr = jnp.broadcast_to(rr, (high, 128))
        pull = jnp.broadcast_to(pull, (high, 128))
        yield
        for t in range(DI // 128):
            cols = slice(128 * t, 128 * t + 128)
            h = h_s[rows, cols]
            th = jnp.tanh(h)
            gated = gated_s[part, :, cols]
            mixed_o[rows, cols] = (gated * rr * gg[:, cols]).astype(bf16)
            dg = eg_s[part, :, cols] * rr - gated * pull
            act = h + h * th
            dscan_o[rows, cols] = (dg * act).astype(bf16)
            dg = dg * scan[rows, cols].astype(f32)
            dgate_o[rows, cols] = (dg * ((1.0 + th) + act * (1.0 - th))).astype(bf16)
        yield

    def both(n, matrix):
        vector = [step for part in range(bm // high) for step in [elementwise(n, part)] * 2]
        for step in vector:
            next(step)
            next(matrix, None)
        for _ in matrix:
            pass

    for _ in products(0):
        pass
    for n in range(blocks):
        both(n, products(n + 1) if n + 1 < blocks else sums(n - 1))
    for _ in sums(blocks - 1):
        pass

    @pl.when(i == pl.num_programs(0) - 1)
    def _():
        early_o[:, :DI] = (0.5 * acc_g[...]).astype(bf16)
        put = block_order(ri)
        for g in range(D // 96):
            at = slice(96 * g, 96 * g + 96)
            halves = dot_tn(put, acc_o[192 * g : 192 * g + 192, :].astype(bf16)).astype(bf16)
            early_o[at, DI : DI + D] = halves[:96]
            early_o[at, DI + D :] = halves[96:]


def gate_pass(tok, scan, cot, later, gain, gg, ri, bm=512):
    rows = tok.shape[0]
    one = pl.Buffered(buffer_count=1)
    full = lambda shape: pl.BlockSpec(shape, lambda i: (0,) * len(shape), pipeline_mode=one)
    blk = lambda w: pl.BlockSpec((bm, w), lambda i: (i, 0))
    low = lambda *shape: jax.ShapeDtypeStruct(shape, bf16)
    return pl.pallas_call(
        functools.partial(gate_kernel, ri),
        grid=(rows // bm,),
        in_specs=[blk(D), blk(DI), blk(D), full(later.shape), full(gain.shape), full(gg.shape)],
        out_specs=[blk(DI), blk(DI), blk(DI), full((D, 2 * DI)), full((DI, D))],
        out_shape=[low(rows, DI), low(rows, DI), low(rows, DI), low(D, 2 * DI), low(DI, D)],
        scratch_shapes=[pltpu.VMEM((D, DI), f32), pltpu.VMEM((DI, D), f32), pltpu.VMEM((bm, D), bf16), pltpu.VMEM((D, bm), bf16),
                        pltpu.VMEM((DI, 256), bf16),
                        pltpu.VMEM((bm, DI), f32), pltpu.VMEM((bm, DI), f32), pltpu.VMEM((8, 32, DI), f32),
                        pltpu.VMEM((8, 32, DI), f32)],
        compiler_params=pltpu.CompilerParams(vmem_limit_bytes=VM),
        name="gate_pass",
    )(tok, scan, cot, later, gain, gg)


def out_kernel(mixed, tok, wo, out_o):
    out_o[...] = (tok[...].astype(f32) + dot(mixed[...], wo[...])).astype(bf16)


def out_pass(mixed, tok, wo, bm=512):
    rows = tok.shape[0]
    blk = lambda w: pl.BlockSpec((bm, w), lambda i: (i, 0))
    return pl.pallas_call(
        out_kernel,
        grid=(rows // bm,),
        in_specs=[blk(DI), blk(D), pl.BlockSpec((DI, D), lambda i: (0, 0), pipeline_mode=pl.Buffered(buffer_count=1))],
        out_specs=blk(D),
        out_shape=jax.ShapeDtypeStruct((rows, D), bf16),
        compiler_params=pltpu.CompilerParams(vmem_limit_bytes=VM),
        cost_estimate=pl.CostEstimate(flops=0, bytes_accessed=0, transcendentals=0),
        name="out_pass",
    )(mixed, tok, wo)


def backward_scan_kernel(heads, per_seq, dscan, cin, act, dact, z_r, st, cw, head_terms, skip, seg, seg_before,
                         dproj_o, gcw_o, gcb_o, gsk_o, ghd_o,
                         dstate, p1buf, qbuf, xwbuf, rowbuf, lastbuf, mbuf, onehot, sums, docs):
    i = pl.program_id(0)

    @pl.when(i == 0)
    def _():
        gcw_o[...] = jnp.zeros_like(gcw_o)
        gcb_o[...] = jnp.zeros_like(gcb_o)
        gsk_o[...] = jnp.zeros_like(gsk_o)
        ghd_o[...] = jnp.zeros_like(ghd_o)
        rowbuf[...] = jnp.zeros_like(rowbuf)
        lastbuf[...] = jnp.zeros_like(lastbuf)
        onehot[...] = head_onehot(onehot.shape)
        head = lax.broadcasted_iota(jnp.int32, sums.shape, 0) >> 6
        sums[...] = (head == lax.broadcasted_iota(jnp.int32, sums.shape, 1)).astype(bf16)

    @pl.when(lax.rem(i, per_seq) == 0)
    def _():
        mbuf[:, :, Q : Q + 8, :] = jnp.zeros((3, CONV // 128, 8, 128), f32)
        dstate[...] = jnp.zeros_like(dstate)

    z = z_r[...]
    rate = head_terms[1:2, :]
    doc_row = seg[0].astype(f32)
    before_row = jnp.where(lax.rem(i, per_seq) == per_seq - 1, -1.0, seg_before[0].astype(f32))
    doc, masks = documents(doc_row, before_row, docs)
    prev = docs[7:8, :]
    soft, a, b, reach, tail, keep = scan_factors(z, rate, doc, prev)
    factors = two_parts(jnp.concatenate([reach, tail, jnp.broadcast_to(keep, (8, 128))], axis=0))
    at = a.T
    row = lax.broadcasted_iota(jnp.int32, (Q, Q), 0)
    lane = lax.broadcasted_iota(jnp.int32, (Q, Q), 1)
    joined = (lane >= row) & (doc == doc_row)
    low = lane < HD
    bmat = act[:, DI : DI + N]
    cmat = act[:, DI + N :]
    ct_mat = cmat.astype(f32).T.astype(bf16)
    s = dot_nt(bmat, cmat)
    ds_low = dstate[...].astype(bf16)
    zero = jnp.zeros((Q, Q), bf16)
    dst = jnp.zeros((Q, Q), f32)

    def conv_back(t, grad):
        cols = slice(128 * t, 128 * t + 128)
        dpre = grad * dact[:, cols].astype(f32)
        for k in range(3):
            mbuf[k, t, 0:Q, :] = dpre * masks[k]
        cv = cin[:, cols].astype(f32)
        dcin = cw[3:4, cols] * dpre
        gcb_o[:, cols] += jnp.sum(dpre.reshape(-1, 8, 128), axis=0)
        gcw_o[24:32, cols] += jnp.sum((cv * dpre).reshape(-1, 8, 128), axis=0)
        for k in range(3):
            moved = mbuf[k, t, 3 - k : 3 - k + Q, :]
            dcin = dcin + cw[k : k + 1, cols] * moved
            gcw_o[8 * k : 8 * k + 8, cols] += jnp.sum((cv * moved).reshape(-1, 8, 128), axis=0)
        dproj_o[:, cols] = dcin.astype(bf16)
        mbuf[:, t, Q : Q + 8, :] = mbuf[:, t, 0:8, :]

    for p in range(heads // 2):
        cols = slice(128 * p, 128 * p + 128)
        half = slice(128 * (p % 2), 128 * (p % 2) + 128)
        if p % 2 == 0:
            group = slice(128 * p, 128 * p + 256)
            wide = dot(factors, onehot[:, group])
            cs = dot(cmat, st[0, :, group])
            bd = dot(bmat, ds_low[:, group])
        xp = act[:, cols]
        dy = dscan[:, cols]
        dybd = jnp.concatenate([jnp.where(low, dy, zero), jnp.where(low, zero, dy)], axis=0)
        dm = dot_nt(xp, dybd)
        parts = []
        for n, h in enumerate((2 * p, 2 * p + 1)):
            spread = at[h : h + 1, :] - jnp.broadcast_to(b[:, h : h + 1], (Q, Q))
            e = jnp.exp2(jnp.where(joined, spread, NEG))
            m = (e * s).astype(bf16)
            parts.append(m)
            dmh = dm[:, 128 * n : 128 * n + 128]
            dst = dst + dmh * e
            rowbuf[h : h + 1, :] = jnp.sum(dmh * m.astype(f32), axis=0, keepdims=True)
        xf = xp.astype(f32)
        dyf = dy.astype(f32)
        tail_p = wide[Q : 2 * Q, half]
        fresh = bd[:, half] * tail_p
        dx = dot(jnp.concatenate(parts, axis=1), dybd) + fresh
        p1 = xf * dx
        hi = p1.astype(bf16)
        p1buf[:, cols] = hi
        p1buf[:, DI + 128 * p : DI + 128 * p + 128] = (p1 - hi.astype(f32)).astype(bf16)
        dyr = dyf * wide[0:Q, half]
        qbuf[:, cols] = (dyr * cs[:, half]).astype(bf16)
        dyr = dyr.astype(bf16)
        ds = dstate[:, cols]
        lastbuf[0:1, cols] = jnp.sum(xf * fresh, axis=0, keepdims=True) + wide[2 * Q : 2 * Q + 1, half] * jnp.sum(
            ds * st[0, :, cols].astype(f32), axis=0, keepdims=True)
        gsk_o[:, cols] += jnp.sum((dyf * xf).reshape(-1, 8, 128), axis=0)
        xwbuf[:, cols] = (xf * tail_p).astype(bf16)
        xwbuf[:, DI + 128 * p : DI + 128 * p + 128] = dyr
        dstate[:, cols] = ds * wide[2 * Q : 2 * Q + 1, half] + dot(ct_mat, dyr)
        conv_back(p, dx + skip[:, cols] * dyf)
    dst_low = dst.astype(bf16)
    conv_back(DI // 128, dot(dst_low, cmat) + dot_nt(xwbuf[:, :DI], ds_low))
    conv_back(DI // 128 + 1, dot_tn(dst_low, bmat) + dot_nt(xwbuf[:, DI:], st[0]))
    hot = sums[...]
    p1 = dot(p1buf[:, :DI], hot) + dot(p1buf[:, DI:], hot)
    last = two_parts(lastbuf[...])
    last = (dot(last[:, :DI], hot) + dot(last[:, DI:], hot))[0:1, :]
    da = dot(qbuf[...], hot) - p1 + rowbuf[...].T
    g = cumsum_rows(da, reverse=True) + last
    sig = sigmoid(z)
    ratio = jnp.where(z < -15.0, 1.0, sig / jnp.where(z < -15.0, 1.0, soft))
    dz = g * rate * sig + p1 * ratio
    dproj_o[:, CONV:] = dz.astype(bf16)
    ghd_o[0:8, :] += jnp.sum(dz.reshape(-1, 8, 128), axis=0)
    ghd_o[8:16, :] += rate * jnp.sum((g * soft).reshape(-1, 8, 128), axis=0)


def backward_scan(dscan, cin, act, dact, z, st, cw, head_terms, skip, seg, heads, seqs):
    rows = dscan.shape[0]
    n = rows // Q
    one = pl.Buffered(buffer_count=1)
    full = lambda shape: pl.BlockSpec(shape, lambda i: (0,) * len(shape), pipeline_mode=one)
    blk = lambda w: pl.BlockSpec((Q, w), lambda i: (n - 1 - i, 0))
    blk3 = lambda s1, s2: pl.BlockSpec((1, s1, s2), lambda i: (n - 1 - i, 0, 0))
    return pl.pallas_call(
        functools.partial(backward_scan_kernel, heads, n // seqs),
        grid=(n,),
        in_specs=[blk(DI), blk(CONV), blk(CONV), blk(CONV), blk(128), blk3(N, DI), full(cw.shape), full(head_terms.shape),
                  full(skip.shape), blk3(1, Q), pl.BlockSpec((1, 1, Q), lambda i: (jnp.maximum(n - 2 - i, 0), 0, 0))],
        out_specs=[blk(CONV + 128), full((32, CONV)), full((8, CONV)), full((8, DI)), full((16, 128))],
        out_shape=[jax.ShapeDtypeStruct((rows, CONV + 128), bf16), jax.ShapeDtypeStruct((32, CONV), f32),
                   jax.ShapeDtypeStruct((8, CONV), f32), jax.ShapeDtypeStruct((8, DI), f32),
                   jax.ShapeDtypeStruct((16, 128), f32)],
        scratch_shapes=[pltpu.VMEM((N, DI), f32), pltpu.VMEM((Q, 2 * DI), bf16), pltpu.VMEM((Q, DI), bf16),
                        pltpu.VMEM((Q, 2 * DI), bf16), pltpu.VMEM((128, 128), f32), pltpu.VMEM((8, DI), f32),
                        pltpu.VMEM((3, CONV // 128, Q + 8, 128), f32), pltpu.VMEM((256, DI), bf16),
                        pltpu.VMEM((DI, 128), bf16), pltpu.VMEM((Q + 8, 128), f32)],
        compiler_params=pltpu.CompilerParams(vmem_limit_bytes=VM),
        cost_estimate=pl.CostEstimate(flops=0, bytes_accessed=0, transcendentals=0),
        name="backward_scan",
    )(dscan, cin, act, dact, z, st, cw, head_terms, skip, seg, seg)


def norm_back_kernel(dproj, dgate, tok, cot, wc_a, wc_b, wg_abs, gain, order, out_o, wc, wg, sems):
    @pl.when(pl.program_id(0) == 0)
    def _():
        rows = wc_a.shape[0]
        copies = [pltpu.make_async_copy(wc_a.at[:, : CONV + 128], wc.at[0:rows], sems.at[0]),
                  pltpu.make_async_copy(wc_b.at[:, : CONV + 128], wc.at[rows : 2 * rows], sems.at[1])]
        for copy in copies:
            copy.start()
        wg[...] = (0.5 * dot_tn(order[...], wg_abs[...])).astype(bf16)
        for copy in copies:
            copy.wait()

    grad = dot_nt(dgate[...], wg[...]) + dot_nt(dproj[...], wc[...])
    x = tok[...].astype(f32)
    r = lax.rsqrt(jnp.mean(x * x, axis=-1, keepdims=True) + EPS)
    unit = x * r
    e = gain[...] * grad
    back = r * (e - unit * jnp.mean(unit * e, axis=-1, keepdims=True))
    res = (cot[...].astype(f32) + back).astype(bf16)
    out_o[...] = dot_nt(res, order[...]).astype(bf16)


def norm_back(dproj, dgate, tok, cot, wc_a, wc_b, later, gain, order, start, count, into=None, bm=512):
    rows = dproj.shape[0]
    one = pl.Buffered(buffer_count=1)
    full = lambda shape: pl.BlockSpec(shape, lambda i: (0,) * len(shape), pipeline_mode=one)
    blk = lambda w: pl.BlockSpec((bm, w), lambda i: (start + i, 0))
    hbm = pl.BlockSpec(memory_space=pl.ANY)
    given = [] if into is None else [into]
    kernel = norm_back_kernel if into is None else lambda *refs: norm_back_kernel(*refs[:9], *refs[10:])
    return pl.pallas_call(
        kernel,
        grid=(count,),
        in_specs=[blk(CONV + 128), blk(DI), blk(D), blk(D), hbm, hbm, full((D, DI)), full(gain.shape), full(order.shape)]
        + [hbm] * len(given),
        out_specs=blk(D),
        out_shape=jax.ShapeDtypeStruct((rows, D), bf16),
        input_output_aliases={9: 0} if given else {},
        scratch_shapes=[pltpu.VMEM((D, CONV + 128), bf16), pltpu.VMEM((D, DI), bf16), pltpu.SemaphoreType.DMA((2,))],
        compiler_params=pltpu.CompilerParams(vmem_limit_bytes=VM),
        cost_estimate=pl.CostEstimate(flops=0, bytes_accessed=0, transcendentals=0),
        name="norm_back",
    )(dproj, dgate, tok, cot, wc_a, wc_b, later, gain, order, *given)


def conv_weight_kernel(nrm, dproj, small, out_o):
    grad = lax.dot_general(dproj[...], nrm[...], (((0,), (0,)), ((), ())), preferred_element_type=f32)
    out_o[...] = grad.astype(bf16).T

    @pl.when(pl.program_id(0) == pl.num_programs(0) - 1)
    def _():
        out_o[:, out_o.shape[1] - 128 :] = (grad[out_o.shape[1] - 128 :].T + small[...].astype(f32)).astype(bf16)


def conv_weight_grad(nrm, dproj, small, bn=640):
    rows = nrm.shape[0]
    one = pl.Buffered(buffer_count=1)
    return pl.pallas_call(
        conv_weight_kernel,
        grid=((CONV + 128) // bn,),
        in_specs=[pl.BlockSpec((rows, D), lambda i: (0, 0), pipeline_mode=one), pl.BlockSpec((rows, bn), lambda i: (0, i)),
                  pl.BlockSpec((D, 128), lambda i: (0, 0), pipeline_mode=one)],
        out_specs=pl.BlockSpec((D, bn), lambda i: (0, i)),
        out_shape=jax.ShapeDtypeStruct((D, CONV + 128), bf16),
        compiler_params=pltpu.CompilerParams(vmem_limit_bytes=VM),
        cost_estimate=pl.CostEstimate(flops=0, bytes_accessed=0, transcendentals=0),
        name="conv_weight_grad",
    )(nrm, dproj, small)


def stages_of(mesh):
    ndp, nf = mesh.shape["dp"], mesh.shape["fsdp"]
    out = []
    stride = 1
    while stride < nf:
        group = 2 if stride == 1 else min(4, nf // stride)
        out.append(("fsdp", stride, group, stride))
        stride *= group
    stride = 1
    while stride < ndp:
        group = min(4, ndp // stride)
        out.append(("dp", stride, group, stride * nf))
        stride *= group
    return out[::-1]


def pairs_of(stages):
    out = []
    for axis, stride, group, number in stages[::-1]:
        step = 1
        while step < group:
            out.append((axis, stride * step, 2, number * step))
            step *= 2
    return out


def slot_devices(stages):
    rel = np.zeros((1,), np.int32)
    for _, _, group, number in stages:
        rel = (np.arange(group, dtype=np.int32)[:, None] * number + rel[None, :]).reshape(-1)
    return jnp.asarray(rel)


def swap(arr, axis, size, offset):
    return lax.ppermute(arr, axis, [(i, i ^ offset) for i in range(size)])


def gather_stage(block, stage, sizes):
    axis, stride, group, _ = stage
    return jnp.stack([block] + [swap(block, axis, sizes[axis], k * stride) for k in range(1, group)])


def scatter_stage(kept, stage, sizes):
    axis, stride, group, _ = stage
    low = kept.astype(bf16)
    got = [swap(low[k], axis, sizes[axis], k * stride) for k in range(1, group)]
    total = kept[0].astype(f32)
    for part in got:
        total = total + part.astype(f32)
    return total


def before(value, *others):
    return lax.optimization_barrier((value,) + others)


def local(mesh, tokens, cotangent, segments, in_gain, weight_in, conv_weight, conv_bias, step_bias, decay_log, skip_gain,
          gate_gain, weight_out):
    sizes = {"dp": mesh.shape["dp"], "fsdp": mesh.shape["fsdp"]}
    nf = sizes["fsdp"]
    nd = sizes["dp"] * nf
    axes = ("dp", "fsdp")
    stages = stages_of(mesh)
    me = lax.axis_index("dp") * nf + lax.axis_index("fsdp")
    seqs, length, _ = tokens.shape
    rows = seqs * length
    ri, ro, cc, share = weight_in.shape[0], weight_out.shape[0], conv_bias.shape[0], step_bias.shape[0]
    heads = share * nf
    free = 128 - heads

    device = slot_devices(stages) ^ me
    feature = (device[:, None] * ri + jnp.arange(ri)[None, :]).reshape(-1)
    order = (jnp.arange(D)[:, None] == feature[None, :]).astype(bf16)
    slot_hot = (device[:, None] == jnp.arange(nd)[None, :]).astype(bf16)

    tall = max(ri, 16)
    wc, later = pack(weight_in, weight_out, in_gain[None], conv_weight, conv_bias[None], gate_gain[None],
                     jnp.stack([step_bias, decay_log, skip_gain]), ri, tall)
    later = lax.all_gather(later, axes, axis=0, tiled=True)
    tok = tokens.reshape(rows, D)
    up = cotangent.reshape(rows, D)
    seg = segments.reshape(rows // Q, 1, Q)
    wc = gather_stage(wc, stages[0], sizes)
    tok_s = jnp.dot(tok, order, preferred_element_type=bf16)
    wc, tok_s = before(wc, tok_s)
    for stage in stages[1:-1]:
        wc = gather_stage(wc, stage, sizes)
    up_s = jnp.dot(up, order, preferred_element_type=bf16)
    wc, up_s = before(wc, up_s)
    wc_b = swap(wc, stages[-1][0], sizes[stages[-1][0]], stages[-1][1])
    halves = [part.reshape(nd // 2, tall, CONV + 256) for part in (wc, wc_b)]
    small = jnp.concatenate([part[:, :16, CONV + 128 :] for part in halves], axis=0).transpose(1, 0, 2).astype(f32)
    wc_a, wc_b = [part[:, :ri].reshape(D // 2, CONV + 256) for part in halves]
    device_rows = jnp.broadcast_to(device.astype(f32)[:, None], (nd, 128))

    cin, act, dact, nrm, scan, st, z, gain, gain_abs, cw, cb, gg, head_terms, skip = forward_scan(
        tok_s, wc_a, wc_b, small, device_rows, seg, seqs, ri, ro, share, heads)
    mixed, dscan, dgate, early, wo = gate_pass(tok, scan, up, later, gain_abs, gg, ri)
    early = lax.psum_scatter(early, axes, scatter_dimension=0, tiled=True)

    dproj, gcw, gcb, gsk, ghd = backward_scan(
        dscan, cin, act, dact, z, st, cw, head_terms, skip, seg, heads, seqs)
    taps = 0.5 * jnp.concatenate([gcw.reshape(4, 8, CONV).sum(1), gcb.sum(0)[None]], axis=0)
    taps = taps.reshape(5, nd, cc).transpose(1, 0, 2).reshape(nd, 5 * cc)
    sums = jnp.stack([ghd[:8].sum(0)[:heads], ghd[8:16].sum(0)[:heads],
                            gsk.sum(0).reshape(heads, HD).sum(1)])
    sums = jnp.tile(sums.reshape(3, nf, share).transpose(1, 0, 2).reshape(nf, 3 * share), (nd // nf, 1))
    terms = jnp.concatenate([taps, sums], axis=1)
    hi = lax.reduce_precision(terms, 8, 7)
    both = jnp.concatenate([hi, terms - hi], axis=1).astype(bf16)
    both = jnp.dot(slot_hot, both, preferred_element_type=f32).astype(bf16)
    width = 5 * cc + 3 * share
    both = jnp.pad(both, ((0, 0), (0, ri * free - 2 * width))).reshape(D, free)
    gwc = conv_weight_grad(nrm, dproj, jnp.pad(both, ((0, 0), (heads, 0))))
    total = gwc.reshape([g for _, _, g, _ in stages[::-1]] + [ri, CONV + 128])
    for at, stage in enumerate(stages[::-1]):
        if at == len(stages) - 2:
            total, gain = before(total, gain)
            gtok = norm_back(dproj, dgate, tok_s, up_s, wc_a, wc_b, later, gain, order, 0, 4)
        if at == len(stages) - 1:
            total, gtok, wo, early = before(total, gtok, wo, early)
        total = scatter_stage(total, stage, sizes)
    out = out_pass(mixed, tok, wo)

    early = early.astype(f32)
    g_in = jnp.concatenate([early[:, :DI], total[:, : CONV + heads]], axis=1)
    g_out = jnp.concatenate([early[:, DI : DI + D], early[:, DI + D :]], axis=0)
    packed = total[:, CONV + heads :].reshape(-1)
    packed = packed[:width] + packed[width : 2 * width]
    g_in_gain = jnp.sum(weight_in.astype(f32) * g_in, axis=1) / in_gain.astype(f32)
    g_gate_gain = jnp.sum(weight_out.astype(f32) * g_out, axis=1) / gate_gain.astype(f32)
    by_head = packed[5 * cc :].reshape(3, share)
    return (out.reshape(tokens.shape), gtok.reshape(tokens.shape), g_in_gain, g_in, packed[: 4 * cc].reshape(4, cc),
            packed[4 * cc : 5 * cc], by_head[0], by_head[1], by_head[2], g_gate_gain, g_out)


def solution(mesh):
    every = ("dp", "fsdp")
    return jax.shard_map(
        functools.partial(local, mesh),
        mesh=mesh,
        in_specs=(P(every, None, None), P(every, None, None), P(every, None), P(every), P(every, None), P(None, every),
                  P(every), P("fsdp"), P("fsdp"), P("fsdp"), P(every), P(every, None)),
        out_specs=(P(every, None, None), P(every, None, None), P(every), P(every, None), P(None, every), P(every),
                   P("fsdp"), P("fsdp"), P("fsdp"), P(every), P(every, None)),
        check_vma=False,
    )
```

```python
import functools

import jax
import jax.numpy as jnp
import numpy as np
from jax import lax
from jax.experimental import pallas as pl
from jax.experimental.pallas import tpu as pltpu
from jax.sharding import PartitionSpec as P

EPS = 1e-05
LOG2E = 1.4426950408889634
NEG = -1e30
f32, bf16 = jnp.float32, jnp.bfloat16
Q = 128
VM = 60 * 1024 * 1024

D, DI, CONV, N, HD = 768, 1536, 1792, 128, 64


def dot(a, b):
    return lax.dot_general(a, b, (((1,), (0,)), ((), ())), preferred_element_type=f32)


def dot_nt(a, b):
    return lax.dot_general(a, b, (((1,), (1,)), ((), ())), preferred_element_type=f32)


def dot_tn(a, b):
    return lax.dot_general(a, b, (((0,), (0,)), ((), ())), preferred_element_type=f32)


def sigmoid(v):
    return 1.0 / (1.0 + jnp.exp(-v))


def cumsum_rows(v, reverse=False):
    rows = lax.broadcasted_iota(jnp.int32, v.shape, 0)
    count = v.shape[0]
    shift = 1
    while shift < count:
        if reverse:
            moved = pltpu.roll(v, count - shift, 0)
            v = v + jnp.where(rows < count - shift, moved, 0.0)
        else:
            moved = pltpu.roll(v, shift, 0)
            v = v + jnp.where(rows >= shift, moved, 0.0)
        shift *= 2
    return v


def step_terms(z):
    e = jnp.exp(-jnp.abs(z))
    soft = jnp.maximum(z, 0.0) + jnp.log1p(e)
    tiny = z < -15.0
    log_soft = jnp.where(tiny, z, jnp.log(jnp.where(tiny, 1.0, soft)))
    return soft, log_soft


def columns(row):
    return jnp.broadcast_to(row, (Q, 128)).T


def documents(row, before_row, docs):
    doc = columns(row)
    docs[0:8, :] = columns(before_row)[Q - 8 : Q, :]
    docs[8 : 8 + Q, :] = doc
    return doc, [(docs[8 - s : 8 - s + Q, :] == doc).astype(f32) for s in (3, 2, 1)]


def scan_factors(z, rate, doc, prev_doc):
    soft, log_soft = step_terms(z)
    a = cumsum_rows(soft * (rate * LOG2E))
    b = a - log_soft * LOG2E
    last = a[Q - 1 : Q, :]
    last_doc = doc[Q - 1 : Q, :]
    reach = jnp.where(doc == prev_doc, jnp.exp2(a), 0.0)
    tail = jnp.where(doc == last_doc, jnp.exp2(last - b), 0.0)
    keep = jnp.where(last_doc == prev_doc, jnp.exp2(last), 0.0)
    return soft, a, b, reach, tail, keep


def pair_of(cols, p, low):
    left = jnp.broadcast_to(cols[:, 2 * p : 2 * p + 1], low.shape)
    right = jnp.broadcast_to(cols[:, 2 * p + 1 : 2 * p + 2], low.shape)
    return jnp.where(low, left, right)


def two_parts(cols):
    hi = cols.astype(bf16)
    return jnp.concatenate([hi, (cols - hi.astype(f32)).astype(bf16)], axis=1)


def head_onehot(shape):
    head = lax.broadcasted_iota(jnp.int32, shape, 1) >> 6
    return (lax.broadcasted_iota(jnp.int32, shape, 0) & 127 == head).astype(bf16)


def pack_kernel(ri, w_in, w_out, in_gain, cw, cb, gg, sb, dl, sg, wc_o, later_o, rows):
    wc_o[...] = jnp.zeros_like(wc_o)
    wc_o[0:ri, : w_in.shape[1] - DI] = w_in[:, DI:]
    rows[...] = jnp.zeros_like(rows)
    rows[0:1, : in_gain.shape[1]] = in_gain[...].astype(f32)
    rows[1:5, : cw.shape[1]] = cw[...].astype(f32)
    rows[5:6, : cb.shape[1]] = cb[...].astype(f32)
    rows[6:7, : gg.shape[1]] = gg[...].astype(f32)
    for k, term in enumerate((sb, dl, sg)):
        value = term[...]
        for n in range(3):
            part = value.astype(bf16).astype(f32)
            rows[7 + 3 * n + k : 8 + 3 * n + k, : value.shape[1]] = part
            value = value - part
    wc_o[0:16, CONV + 128 :] = rows[...].astype(bf16)
    later_o[:, :DI] = w_in[:, :DI]
    later_o[:, DI : DI + D] = w_out[0:ri, :]
    later_o[:, DI + D :] = w_out[ri:, :]


def pack(w_in, w_out, in_gain, cw, cb, gg, sb, dl, sg, ri, tall):
    return pl.pallas_call(
        functools.partial(pack_kernel, ri),
        out_shape=[jax.ShapeDtypeStruct((tall, CONV + 256), bf16), jax.ShapeDtypeStruct((ri, 2 * DI), bf16)],
        scratch_shapes=[pltpu.VMEM((16, 128), f32)],
        name="pack",
    )(w_in, w_out, in_gain, cw, cb, gg, sb, dl, sg)


def unpack_small(ri, ro, share, small, device, onehot, gain, gain_abs, cw, cb, gg, heads_o, skip):
    nd = small.shape[1]
    slot = lax.broadcasted_iota(jnp.int32, (nd, 128), 0).astype(f32)[:, 0:1]
    owner = device[...][:, 0:1]

    def spread(rows, width, total, who):
        lane = lax.broadcasted_iota(jnp.int32, (128, total), 1).astype(f32)
        piece = jnp.floor((lane + 0.5) * (1.0 / width))
        inner = lane - piece * width
        pick = (lax.broadcasted_iota(jnp.int32, (128, total), 0).astype(f32) == inner).astype(bf16)
        mine = piece[0:1, :] == who
        return [jnp.sum(jnp.where(mine, dot(small[r].astype(bf16), pick), 0.0), axis=0, keepdims=True) for r in rows]

    gain[...] = spread([0], ri, D, slot)[0]
    gain_abs[...] = spread([0], ri, D, owner)[0]
    taps = spread(range(1, 6), CONV // nd, CONV, owner)
    for k in range(4):
        cw[k : k + 1, :] = 0.5 * taps[k]
    cw[4:8, :] = jnp.zeros((4, CONV), f32)
    cb[...] = 0.5 * taps[4]
    gg[...] = spread([6], ro, DI, owner)[0]
    parts = spread(range(7, 16), share, 128, owner)
    per_head = [parts[n] + parts[n + 3] + parts[n + 6] for n in range(3)]
    heads_o[0:1, :] = per_head[0]
    heads_o[1:2, :] = -jnp.exp(per_head[1])
    skip[...] = dot(two_parts(jnp.broadcast_to(per_head[2], (8, 128))), onehot[...])[0:1, :]


def forward_scan_kernel(heads, per_seq, ri, ro, share, first, tok, wc_a, wc_b, small, device, seg, seg_before,
                        cin_o, act_o, dact_o, nrm_o, scan_o, st_o, z_o, gain, gain_abs, cw, cb, gg, heads_o, skip,
                        pbuf, zbuf, nbuf, pnext, znext, nnext, state, docs, onehot, wc, sems):
    i = pl.program_id(0)
    tiles = CONV // 128

    def normed(block):
        x = block[...].astype(f32)
        r = lax.rsqrt(jnp.mean(x * x, axis=-1, keepdims=True) + EPS)
        nnext[...] = (x * r * gain[...]).astype(bf16)

    def project(t):
        part = dot(nnext[...], wc[:, 128 * t : 128 * t + 256])
        pnext[t] = part[:, :128]
        pnext[t + 1] = part[:, 128:]

    def project_step():
        znext[...] = dot(nnext[...], wc[:, CONV:]) + heads_o[0:1, :]

    def advance():
        pbuf[:, 8 : 8 + Q, :] = pnext[...]
        zbuf[...] = znext[...]
        nbuf[...] = nnext[...]

    @pl.when(i == 0)
    def _():
        rows = wc_a.shape[0]
        copies = [pltpu.make_async_copy(wc_a.at[:, : CONV + 128], wc.at[0:rows], sems.at[0]),
                  pltpu.make_async_copy(wc_b.at[:, : CONV + 128], wc.at[rows : 2 * rows], sems.at[1])]
        for copy in copies:
            copy.start()
        onehot[...] = head_onehot(onehot.shape)
        unpack_small(ri, ro, share, small, device, onehot, gain, gain_abs, cw, cb, gg, heads_o, skip)
        normed(first)
        for copy in copies:
            copy.wait()
        for t in range(0, tiles, 2):
            project(t)
        project_step()
        advance()

    @pl.when(lax.rem(i, per_seq) == 0)
    def _():
        pbuf[:, 0:8, :] = jnp.zeros((tiles, 8, 128), f32)
        state[...] = jnp.zeros_like(state)

    nrm_o[...] = nbuf[...]
    z = zbuf[...]
    z_o[...] = z
    doc_row = seg[0].astype(f32)
    before_row = jnp.where(lax.rem(i, per_seq) == 0, -1.0, seg_before[0].astype(f32))
    doc, masks = documents(doc_row, before_row, docs)
    prev = docs[7:8, :]
    soft, a, b, reach, tail, keep = scan_factors(z, heads_o[1:2, :], doc, prev)
    factors = two_parts(jnp.concatenate([reach, tail, jnp.broadcast_to(keep, (8, 128))], axis=0))
    bt = b.T
    row = lax.broadcasted_iota(jnp.int32, (Q, Q), 0)
    lane = lax.broadcasted_iota(jnp.int32, (Q, Q), 1)
    joined = (row >= lane) & (doc == doc_row)
    low = lane < HD
    zero = jnp.zeros((Q, Q), bf16)

    def conv(t):
        cols = slice(128 * t, 128 * t + 128)
        here = pbuf[t, 8 : 8 + Q, :]
        cin_o[:, cols] = here.astype(bf16)
        half = cb[:, cols] + cw[3:4, cols] * here
        for k in range(3):
            half = half + cw[k : k + 1, cols] * (pbuf[t, 5 + k : 5 + k + Q, :] * masks[k])
        pbuf[t, 0:8, :] = pbuf[t, Q : Q + 8, :]
        th = jnp.tanh(half)
        dact_o[:, cols] = ((1.0 + th) * (1.0 + half * (1.0 - th))).astype(bf16)
        act = (half + half * th).astype(bf16)
        act_o[:, cols] = act
        return act

    normed(tok)
    bmat = conv(tiles - 2)
    cmat = conv(tiles - 1)
    bt_mat = bmat.astype(f32).T.astype(bf16)
    s = dot_nt(cmat, bmat)
    for p in range(heads // 2):
        cols = slice(128 * p, 128 * p + 128)
        half = slice(128 * (p % 2), 128 * (p % 2) + 128)
        if p % 2 == 0:
            group = slice(128 * p, 128 * p + 256)
            wide = dot(factors, onehot[:, group])
            st_low = state[:, group].astype(bf16)
            st_o[0, :, group] = st_low
            cs = dot(cmat, st_low)
        xp = conv(p)
        if p < tiles // 2:
            project(2 * p)
        if p == tiles // 2:
            project_step()
        parts = []
        for h in (2 * p, 2 * p + 1):
            spread = jnp.broadcast_to(a[:, h : h + 1], (Q, Q)) - bt[h : h + 1, :]
            parts.append((jnp.exp2(jnp.where(joined, spread, NEG)) * s).astype(bf16))
        xbd = jnp.concatenate([jnp.where(low, xp, zero), jnp.where(low, zero, xp)], axis=0)
        y = dot(jnp.concatenate(parts, axis=1), xbd)
        xf = xp.astype(f32)
        y = y + cs[:, half] * wide[0:Q, half] + xf * skip[:, cols]
        scan_o[:, cols] = y.astype(bf16)
        xw = (xf * wide[Q : 2 * Q, half]).astype(bf16)
        state[:, cols] = state[:, cols] * wide[2 * Q : 2 * Q + 1, half] + dot(bt_mat, xw)
    advance()


def forward_scan(tok, wc_a, wc_b, small, device, seg, seqs, ri, ro, share, heads):
    rows = tok.shape[0]
    n = rows // Q
    one = pl.Buffered(buffer_count=1)
    full = lambda arr: pl.BlockSpec(arr.shape, lambda i: (0,) * arr.ndim, pipeline_mode=one)
    blk = lambda w: pl.BlockSpec((Q, w), lambda i: (i, 0))
    hbm = pl.BlockSpec(memory_space=pl.ANY)
    low = lambda *shape: jax.ShapeDtypeStruct(shape, bf16)
    sides = [(1, D), (1, D), (8, CONV), (1, CONV), (1, DI), (8, 128), (1, DI)]
    side = lambda shape: pl.BlockSpec(shape, lambda i: (0, 0))
    return pl.pallas_call(
        functools.partial(forward_scan_kernel, heads, n // seqs, ri, ro, share),
        grid=(n,),
        in_specs=[pl.BlockSpec((Q, D), lambda i: (0, 0), pipeline_mode=one),
                  pl.BlockSpec((Q, D), lambda i: (jnp.minimum(i + 1, n - 1), 0)), hbm, hbm, full(small), full(device),
                  pl.BlockSpec((1, 1, Q), lambda i: (i, 0, 0)), pl.BlockSpec((1, 1, Q), lambda i: (jnp.maximum(i - 1, 0), 0, 0))],
        out_specs=[blk(CONV), blk(CONV), blk(CONV), blk(D), blk(DI), pl.BlockSpec((1, N, DI), lambda i: (i, 0, 0)), blk(128)]
        + [side(shape) for shape in sides],
        out_shape=[low(rows, CONV), low(rows, CONV), low(rows, CONV), low(rows, D), low(rows, DI), low(n, N, DI),
                   jax.ShapeDtypeStruct((rows, 128), f32)] + [jax.ShapeDtypeStruct(shape, f32) for shape in sides],
        scratch_shapes=[pltpu.VMEM((CONV // 128, Q + 8, 128), f32), pltpu.VMEM((Q, 128), f32), pltpu.VMEM((Q, D), bf16),
                        pltpu.VMEM((CONV // 128, Q, 128), f32), pltpu.VMEM((Q, 128), f32), pltpu.VMEM((Q, D), bf16),
                        pltpu.VMEM((N, DI), f32), pltpu.VMEM((Q + 8, 128), f32), pltpu.VMEM((256, DI), bf16),
                        pltpu.VMEM((D, CONV + 128), bf16), pltpu.SemaphoreType.DMA((2,))],
        compiler_params=pltpu.CompilerParams(vmem_limit_bytes=VM),
        name="forward_scan",
    )(tok, tok, wc_a, wc_b, small, device, seg, seg)


def block_order(ri):
    row = lax.broadcasted_iota(jnp.int32, (192, 192), 0)
    lane = lax.broadcasted_iota(jnp.int32, (192, 192), 1)
    second = lane >= 96
    at = jnp.where(second, lane - 96, lane)
    owner = lax.div(at, ri)
    target = owner * (2 * ri) + (at - owner * ri) + jnp.where(second, ri, 0)
    return (row == target).astype(bf16)


def gate_kernel(ri, tok, scan, cot, later, gain, gg, mixed_o, dscan_o, dgate_o, early_o, wo, acc_g, acc_o,
                nb_s, nbt_s, mixt_s, h_s, e_s, gated_s, eg_s):
    i = pl.program_id(0)
    bm, high = 256, 32
    blocks = tok.shape[0] // bm

    @pl.when(i == 0)
    def _():
        acc_g[...] = jnp.zeros_like(acc_g)
        acc_o[...] = jnp.zeros_like(acc_o)
        put = block_order(ri)
        for g in range(D // 96):
            at = slice(96 * g, 96 * g + 96)
            halves = jnp.concatenate([later[at, DI : DI + D], later[at, DI + D :]], axis=0)
            wo[192 * g : 192 * g + 192, :] = dot(put, halves).astype(bf16)

    x = tok[...].astype(f32)
    r = lax.rsqrt(jnp.mean(x * x, axis=-1, keepdims=True) + EPS)
    nb = (x * r * gain[...]).astype(bf16)
    nb_s[...] = nb * 0.5
    nbt_s[...] = nb.T

    def products(n):
        rows = slice(bm * n, bm * n + bm)
        for c in range(DI // 256):
            cols = slice(256 * c, 256 * c + 256)
            h_s[rows, cols] = dot(nb_s[rows, :], later[:, cols])
            yield
            e_s[rows, cols] = dot_nt(cot[rows, :], wo[cols, :])
            yield

    def sums(n):
        rows = slice(bm * n, bm * n + bm)
        for c in range(DI // 256):
            cols = slice(256 * c, 256 * c + 256)
            mixt_s[cols, :] = mixed_o[rows, cols].T
        for c in range(D // 256):
            cols = slice(256 * c, 256 * c + 256)
            acc_o[:, cols] += dot(mixt_s[...], cot[rows, cols])
            yield
        for c in range(DI // 256):
            cols = slice(256 * c, 256 * c + 256)
            acc_g[:, cols] += dot(nbt_s[:, rows], dgate_o[rows, cols])
            yield

    def elementwise(n, part):
        rows = slice(bm * n + part * high, bm * n + part * high + high)
        squares = jnp.zeros((high, 128), f32)
        cross = jnp.zeros((high, 128), f32)
        for t in range(DI // 128):
            cols = slice(128 * t, 128 * t + 128)
            h = h_s[rows, cols]
            gated = scan[rows, cols].astype(f32) * (h + h * jnp.tanh(h))
            eg = e_s[rows, cols] * gg[:, cols]
            squares = squares + gated * gated
            cross = cross + gated * eg
            gated_s[part, :, cols] = gated
            eg_s[part, :, cols] = eg
        rr = lax.rsqrt(jnp.sum(squares, axis=-1, keepdims=True) * (1.0 / DI) + EPS)
        pull = rr * rr * rr * (jnp.sum(cross, axis=-1, keepdims=True) * (1.0 / DI))
        rr = jnp.broadcast_to(rr, (high, 128))
        pull = jnp.broadcast_to(pull, (high, 128))
        yield
        for t in range(DI // 128):
            cols = slice(128 * t, 128 * t + 128)
            h = h_s[rows, cols]
            th = jnp.tanh(h)
            gated = gated_s[part, :, cols]
            mixed_o[rows, cols] = (gated * rr * gg[:, cols]).astype(bf16)
            dg = eg_s[part, :, cols] * rr - gated * pull
            act = h + h * th
            dscan_o[rows, cols] = (dg * act).astype(bf16)
            dg = dg * scan[rows, cols].astype(f32)
            dgate_o[rows, cols] = (dg * ((1.0 + th) + act * (1.0 - th))).astype(bf16)
        yield

    def both(n, matrix):
        vector = [step for part in range(bm // high) for step in [elementwise(n, part)] * 2]
        for step in vector:
            next(step)
            next(matrix, None)
        for _ in matrix:
            pass

    for _ in products(0):
        pass
    for n in range(blocks):
        both(n, products(n + 1) if n + 1 < blocks else sums(n - 1))
    for _ in sums(blocks - 1):
        pass

    @pl.when(i == pl.num_programs(0) - 1)
    def _():
        early_o[:, :DI] = (0.5 * acc_g[...]).astype(bf16)
        put = block_order(ri)
        for g in range(D // 96):
            at = slice(96 * g, 96 * g + 96)
            halves = dot_tn(put, acc_o[192 * g : 192 * g + 192, :].astype(bf16)).astype(bf16)
            early_o[at, DI : DI + D] = halves[:96]
            early_o[at, DI + D :] = halves[96:]


def gate_pass(tok, scan, cot, later, gain, gg, ri, bm=512):
    rows = tok.shape[0]
    one = pl.Buffered(buffer_count=1)
    full = lambda shape: pl.BlockSpec(shape, lambda i: (0,) * len(shape), pipeline_mode=one)
    blk = lambda w: pl.BlockSpec((bm, w), lambda i: (i, 0))
    low = lambda *shape: jax.ShapeDtypeStruct(shape, bf16)
    return pl.pallas_call(
        functools.partial(gate_kernel, ri),
        grid=(rows // bm,),
        in_specs=[blk(D), blk(DI), blk(D), full(later.shape), full(gain.shape), full(gg.shape)],
        out_specs=[blk(DI), blk(DI), blk(DI), full((D, 2 * DI)), full((DI, D))],
        out_shape=[low(rows, DI), low(rows, DI), low(rows, DI), low(D, 2 * DI), low(DI, D)],
        scratch_shapes=[pltpu.VMEM((D, DI), f32), pltpu.VMEM((DI, D), f32), pltpu.VMEM((bm, D), bf16), pltpu.VMEM((D, bm), bf16),
                        pltpu.VMEM((DI, 256), bf16),
                        pltpu.VMEM((bm, DI), f32), pltpu.VMEM((bm, DI), f32), pltpu.VMEM((8, 32, DI), f32),
                        pltpu.VMEM((8, 32, DI), f32)],
        compiler_params=pltpu.CompilerParams(vmem_limit_bytes=VM),
        name="gate_pass",
    )(tok, scan, cot, later, gain, gg)


def out_kernel(mixed, tok, wo, out_o):
    out_o[...] = (tok[...].astype(f32) + dot(mixed[...], wo[...])).astype(bf16)


def out_pass(mixed, tok, wo, bm=512):
    rows = tok.shape[0]
    blk = lambda w: pl.BlockSpec((bm, w), lambda i: (i, 0))
    return pl.pallas_call(
        out_kernel,
        grid=(rows // bm,),
        in_specs=[blk(DI), blk(D), pl.BlockSpec((DI, D), lambda i: (0, 0), pipeline_mode=pl.Buffered(buffer_count=1))],
        out_specs=blk(D),
        out_shape=jax.ShapeDtypeStruct((rows, D), bf16),
        compiler_params=pltpu.CompilerParams(vmem_limit_bytes=VM),
        cost_estimate=pl.CostEstimate(flops=0, bytes_accessed=0, transcendentals=0),
        name="out_pass",
    )(mixed, tok, wo)


def pack_grads(nf, share, tall, gcw, gcb, gsk, ghd, device, sums, rows, out_o):
    nd = device.shape[0]
    owner = device[...][:, 0:1]
    first_lane = nf * share

    def spread(values, width, who):
        total = values.shape[1]
        lane = lax.broadcasted_iota(jnp.int32, (128, total), 1).astype(f32)
        piece = jnp.floor((lane + 0.5) * (1.0 / width))
        place = lax.broadcasted_iota(jnp.int32, (128, total), 0).astype(f32) - first_lane
        pick = ((place == lane - piece * width) & (place < width)).astype(bf16)
        mine = piece[0:1, :] == who
        hi = values.astype(bf16).astype(f32)
        return [dot_nt(jnp.where(mine, part, 0.0).astype(bf16), pick) for part in (hi, values - hi)]

    rows[...] = jnp.zeros_like(rows)

    def put(n, values):
        rows[pl.ds(n, nd, stride=tall), :] = values

    for k in range(5):
        terms = gcw[8 * k : 8 * k + 8, :] if k < 4 else gcb[...]
        hi, lo = spread(0.5 * jnp.sum(terms, axis=0, keepdims=True), CONV // nd, owner)
        put(k, hi)
        put(5 + k, lo)
    group = owner - nf * jnp.floor((owner + 0.5) * (1.0 / nf))
    skips = two_parts(jnp.broadcast_to(jnp.sum(gsk[...], axis=0, keepdims=True), (8, DI)))
    skips = dot(skips[:, :DI], sums[...]) + dot(skips[:, DI:], sums[...])
    per_head = [jnp.sum(ghd[0:8, :], axis=0, keepdims=True), jnp.sum(ghd[8:16, :], axis=0, keepdims=True), skips[0:1, :]]
    for n in range(3):
        hi, lo = spread(per_head[n], share, group)
        put(10 + n, hi)
        put(13 + n, lo)
    out_o[...] = rows[...].astype(bf16)


def backward_scan_kernel(heads, per_seq, nf, share, tall, dscan, cin, act, dact, z_r, st, cw, head_terms, skip, seg, seg_before,
                         wc_a, wc_b, device, dproj_o, gproj_o, pack_o,
                         dstate, p1buf, qbuf, xwbuf, rowbuf, lastbuf, mbuf, onehot, sums, docs,
                         gcw_o, gcb_o, gsk_o, ghd_o, rows_s, wc, dlast, sems):
    i = pl.program_id(0)
    steps = pl.num_programs(0)

    @pl.when(i == 0)
    def _():
        half = wc_a.shape[0]
        copies = [pltpu.make_async_copy(wc_a.at[:, : CONV + 128], wc.at[0:half], sems.at[0]),
                  pltpu.make_async_copy(wc_b.at[:, : CONV + 128], wc.at[half : 2 * half], sems.at[1])]
        for copy in copies:
            copy.start()
        dlast[...] = jnp.zeros_like(dlast)
        gcw_o[...] = jnp.zeros_like(gcw_o)
        gcb_o[...] = jnp.zeros_like(gcb_o)
        gsk_o[...] = jnp.zeros_like(gsk_o)
        ghd_o[...] = jnp.zeros_like(ghd_o)
        rowbuf[...] = jnp.zeros_like(rowbuf)
        lastbuf[...] = jnp.zeros_like(lastbuf)
        onehot[...] = head_onehot(onehot.shape)
        head = lax.broadcasted_iota(jnp.int32, sums.shape, 0) >> 6
        sums[...] = (head == lax.broadcasted_iota(jnp.int32, sums.shape, 1)).astype(bf16)
        for copy in copies:
            copy.wait()

    @pl.when(lax.rem(i, per_seq) == 0)
    def _():
        mbuf[:, :, Q : Q + 8, :] = jnp.zeros((3, CONV // 128, 8, 128), f32)
        dstate[...] = jnp.zeros_like(dstate)

    z = z_r[...]
    rate = head_terms[1:2, :]
    doc_row = seg[0].astype(f32)
    before_row = jnp.where(lax.rem(i, per_seq) == per_seq - 1, -1.0, seg_before[0].astype(f32))
    doc, masks = documents(doc_row, before_row, docs)
    prev = docs[7:8, :]
    soft, a, b, reach, tail, keep = scan_factors(z, rate, doc, prev)
    factors = two_parts(jnp.concatenate([reach, tail, jnp.broadcast_to(keep, (8, 128))], axis=0))
    at = a.T
    row = lax.broadcasted_iota(jnp.int32, (Q, Q), 0)
    lane = lax.broadcasted_iota(jnp.int32, (Q, Q), 1)
    joined = (lane >= row) & (doc == doc_row)
    low = lane < HD
    bmat = act[:, DI : DI + N]
    cmat = act[:, DI + N :]
    ct_mat = cmat.astype(f32).T.astype(bf16)
    s = dot_nt(bmat, cmat)
    ds_low = dstate[...].astype(bf16)
    zero = jnp.zeros((Q, Q), bf16)
    dst = jnp.zeros((Q, Q), f32)

    def conv_back(t, grad):
        cols = slice(128 * t, 128 * t + 128)
        dpre = grad * dact[:, cols].astype(f32)
        for k in range(3):
            mbuf[k, t, 0:Q, :] = dpre * masks[k]
        cv = cin[:, cols].astype(f32)
        dcin = cw[3:4, cols] * dpre
        gcb_o[:, cols] += jnp.sum(dpre.reshape(-1, 8, 128), axis=0)
        gcw_o[24:32, cols] += jnp.sum((cv * dpre).reshape(-1, 8, 128), axis=0)
        for k in range(3):
            moved = mbuf[k, t, 3 - k : 3 - k + Q, :]
            dcin = dcin + cw[k : k + 1, cols] * moved
            gcw_o[8 * k : 8 * k + 8, cols] += jnp.sum((cv * moved).reshape(-1, 8, 128), axis=0)
        dproj_o[:, cols] = dcin.astype(bf16)
        mbuf[:, t, Q : Q + 8, :] = mbuf[:, t, 0:8, :]

    def project_back(given, block, part):
        cols = slice(256 * part, 256 * part + 256)
        gproj_o[pl.ds(block * Q, Q), cols] = dot_nt(given[...], wc[cols, :]).astype(bf16)

    block_before = steps - jnp.maximum(i, 1)
    for p in range(heads // 2):
        cols = slice(128 * p, 128 * p + 128)
        half = slice(128 * (p % 2), 128 * (p % 2) + 128)
        if p % 2 == 0:
            group = slice(128 * p, 128 * p + 256)
            wide = dot(factors, onehot[:, group])
            cs = dot(cmat, st[0, :, group])
            bd = dot(bmat, ds_low[:, group])
        if p % 4 == 1:
            project_back(dlast, block_before, p // 4)
        xp = act[:, cols]
        dy = dscan[:, cols]
        dybd = jnp.concatenate([jnp.where(low, dy, zero), jnp.where(low, zero, dy)], axis=0)
        dm = dot_nt(xp, dybd)
        parts = []
        for n, h in enumerate((2 * p, 2 * p + 1)):
            spread = at[h : h + 1, :] - jnp.broadcast_to(b[:, h : h + 1], (Q, Q))
            e = jnp.exp2(jnp.where(joined, spread, NEG))
            m = (e * s).astype(bf16)
            parts.append(m)
            dmh = dm[:, 128 * n : 128 * n + 128]
            dst = dst + dmh * e
            rowbuf[h : h + 1, :] = jnp.sum(dmh * m.astype(f32), axis=0, keepdims=True)
        xf = xp.astype(f32)
        dyf = dy.astype(f32)
        tail_p = wide[Q : 2 * Q, half]
        fresh = bd[:, half] * tail_p
        dx = dot(jnp.concatenate(parts, axis=1), dybd) + fresh
        p1 = xf * dx
        hi = p1.astype(bf16)
        p1buf[:, cols] = hi
        p1buf[:, DI + 128 * p : DI + 128 * p + 128] = (p1 - hi.astype(f32)).astype(bf16)
        dyr = dyf * wide[0:Q, half]
        qbuf[:, cols] = (dyr * cs[:, half]).astype(bf16)
        dyr = dyr.astype(bf16)
        ds = dstate[:, cols]
        lastbuf[0:1, cols] = jnp.sum(xf * fresh, axis=0, keepdims=True) + wide[2 * Q : 2 * Q + 1, half] * jnp.sum(
            ds * st[0, :, cols].astype(f32), axis=0, keepdims=True)
        gsk_o[:, cols] += jnp.sum((dyf * xf).reshape(-1, 8, 128), axis=0)
        xwbuf[:, cols] = (xf * tail_p).astype(bf16)
        xwbuf[:, DI + 128 * p : DI + 128 * p + 128] = dyr
        dstate[:, cols] = ds * wide[2 * Q : 2 * Q + 1, half] + dot(ct_mat, dyr)
        conv_back(p, dx + skip[:, cols] * dyf)
    dst_low = dst.astype(bf16)
    conv_back(DI // 128, dot(dst_low, cmat) + dot_nt(xwbuf[:, :DI], ds_low))
    conv_back(DI // 128 + 1, dot_tn(dst_low, bmat) + dot_nt(xwbuf[:, DI:], st[0]))
    hot = sums[...]
    p1 = dot(p1buf[:, :DI], hot) + dot(p1buf[:, DI:], hot)
    last = two_parts(lastbuf[...])
    last = (dot(last[:, :DI], hot) + dot(last[:, DI:], hot))[0:1, :]
    da = dot(qbuf[...], hot) - p1 + rowbuf[...].T
    g = cumsum_rows(da, reverse=True) + last
    sig = sigmoid(z)
    ratio = jnp.where(z < -15.0, 1.0, sig / jnp.where(z < -15.0, 1.0, soft))
    dz = g * rate * sig + p1 * ratio
    dproj_o[:, CONV:] = dz.astype(bf16)
    ghd_o[0:8, :] += jnp.sum(dz.reshape(-1, 8, 128), axis=0)
    ghd_o[8:16, :] += rate * jnp.sum((g * soft).reshape(-1, 8, 128), axis=0)
    dlast[...] = dproj_o[...]

    @pl.when(i == steps - 1)
    def _():
        for part in range(D // 256):
            project_back(dlast, 0, part)
        pack_grads(nf, share, tall, gcw_o, gcb_o, gsk_o, ghd_o, device, sums, rows_s, pack_o)


def backward_scan(dscan, cin, act, dact, z, st, cw, head_terms, skip, seg, wc_a, wc_b, device, heads, seqs, nf, share, tall):
    rows = dscan.shape[0]
    n = rows // Q
    nd = device.shape[0]
    one = pl.Buffered(buffer_count=1)
    full = lambda shape: pl.BlockSpec(shape, lambda i: (0,) * len(shape), pipeline_mode=one)
    blk = lambda w: pl.BlockSpec((Q, w), lambda i: (n - 1 - i, 0))
    blk3 = lambda s1, s2: pl.BlockSpec((1, s1, s2), lambda i: (n - 1 - i, 0, 0))
    hbm = pl.BlockSpec(memory_space=pl.ANY)
    return pl.pallas_call(
        functools.partial(backward_scan_kernel, heads, n // seqs, nf, share, tall),
        grid=(n,),
        in_specs=[blk(DI), blk(CONV), blk(CONV), blk(CONV), blk(128), blk3(N, DI), full(cw.shape), full(head_terms.shape),
                  full(skip.shape), blk3(1, Q), pl.BlockSpec((1, 1, Q), lambda i: (jnp.maximum(n - 2 - i, 0), 0, 0)),
                  hbm, hbm, full(device.shape)],
        out_specs=[blk(CONV + 128), full((rows, D)), full((nd * tall, 128))],
        out_shape=[jax.ShapeDtypeStruct((rows, CONV + 128), bf16), jax.ShapeDtypeStruct((rows, D), bf16),
                   jax.ShapeDtypeStruct((nd * tall, 128), bf16)],
        scratch_shapes=[pltpu.VMEM((N, DI), f32), pltpu.VMEM((Q, 2 * DI), bf16), pltpu.VMEM((Q, DI), bf16),
                        pltpu.VMEM((Q, 2 * DI), bf16), pltpu.VMEM((128, 128), f32), pltpu.VMEM((8, DI), f32),
                        pltpu.VMEM((3, CONV // 128, Q + 8, 128), f32), pltpu.VMEM((256, DI), bf16),
                        pltpu.VMEM((DI, 128), bf16), pltpu.VMEM((Q + 8, 128), f32), pltpu.VMEM((32, CONV), f32),
                        pltpu.VMEM((8, CONV), f32), pltpu.VMEM((8, DI), f32), pltpu.VMEM((16, 128), f32),
                        pltpu.VMEM((nd * tall, 128), f32), pltpu.VMEM((D, CONV + 128), bf16), pltpu.VMEM((Q, CONV + 128), bf16),
                        pltpu.SemaphoreType.DMA((2,))],
        compiler_params=pltpu.CompilerParams(vmem_limit_bytes=VM),
        cost_estimate=pl.CostEstimate(flops=0, bytes_accessed=0, transcendentals=0),
        name="backward_scan",
    )(dscan, cin, act, dact, z, st, cw, head_terms, skip, seg, seg, wc_a, wc_b, device)


def norm_back_kernel(ri, gproj, dgate, tok, cot, wg_abs, gain, device, out_o, wg, order):
    @pl.when(pl.program_id(0) == 0)
    def _():
        column = lax.broadcasted_iota(jnp.int32, (8, D), 1).astype(f32)
        slot = jnp.floor((column + 0.5) * (1.0 / ri))
        nd = device.shape[0]
        mine = lax.broadcasted_iota(jnp.int32, (nd, D), 0).astype(f32) == slot[0:1, :]
        feature = jnp.sum(jnp.where(mine, device[...][:, 0:1], 0.0), axis=0, keepdims=True) * ri + (column - slot * ri)[0:1, :]
        order[...] = (lax.broadcasted_iota(jnp.int32, (D, D), 0).astype(f32) == feature).astype(bf16)
        wg[...] = (0.5 * dot_tn(order[...], wg_abs[...])).astype(bf16)

    grad = dot_nt(dgate[...], wg[...]) + gproj[...].astype(f32)
    x = tok[...].astype(f32)
    r = lax.rsqrt(jnp.mean(x * x, axis=-1, keepdims=True) + EPS)
    unit = x * r
    e = gain[...] * grad
    back = r * (e - unit * jnp.mean(unit * e, axis=-1, keepdims=True))
    res = (cot[...].astype(f32) + back).astype(bf16)
    out_o[...] = dot_nt(res, order[...]).astype(bf16)


def norm_back(gproj, dgate, tok, cot, later, gain, device, ri, bm=512):
    rows = gproj.shape[0]
    one = pl.Buffered(buffer_count=1)
    full = lambda shape: pl.BlockSpec(shape, lambda i: (0,) * len(shape), pipeline_mode=one)
    blk = lambda w: pl.BlockSpec((bm, w), lambda i: (i, 0))
    return pl.pallas_call(
        functools.partial(norm_back_kernel, ri),
        grid=(rows // bm,),
        in_specs=[blk(D), blk(DI), blk(D), blk(D), full((D, DI)), full(gain.shape), full(device.shape)],
        out_specs=blk(D),
        out_shape=jax.ShapeDtypeStruct((rows, D), bf16),
        scratch_shapes=[pltpu.VMEM((D, DI), bf16), pltpu.VMEM((D, D), bf16)],
        compiler_params=pltpu.CompilerParams(vmem_limit_bytes=36 << 20),
        cost_estimate=pl.CostEstimate(flops=0, bytes_accessed=0, transcendentals=0),
        name="norm_back",
    )(gproj, dgate, tok, cot, later, gain, device)


def conv_weight_kernel(nrm, dproj, small, a_o, b_o):
    grad = lax.dot_general(dproj[...], nrm[...], (((0,), (0,)), ((), ())), preferred_element_type=f32)
    half = a_o.shape[0]
    out = grad.astype(bf16).T
    a_o[...] = out[:half]
    b_o[...] = out[half:]

    @pl.when(pl.program_id(0) == pl.num_programs(0) - 1)
    def _():
        last = slice(a_o.shape[1] - 128, a_o.shape[1])
        out = (grad[a_o.shape[1] - 128 :].T + small[...].astype(f32)).astype(bf16)
        a_o[:, last] = out[:half]
        b_o[:, last] = out[half:]


def conv_weight_grad(nrm, dproj, small, bn=640):
    rows = nrm.shape[0]
    one = pl.Buffered(buffer_count=1)
    return pl.pallas_call(
        conv_weight_kernel,
        grid=((CONV + 128) // bn,),
        in_specs=[pl.BlockSpec((rows, D), lambda i: (0, 0), pipeline_mode=one), pl.BlockSpec((rows, bn), lambda i: (0, i)),
                  pl.BlockSpec((D, 128), lambda i: (0, 0), pipeline_mode=one)],
        out_specs=[pl.BlockSpec((D // 2, bn), lambda i: (0, i))] * 2,
        out_shape=[jax.ShapeDtypeStruct((D // 2, CONV + 128), bf16)] * 2,
        compiler_params=pltpu.CompilerParams(vmem_limit_bytes=VM),
        cost_estimate=pl.CostEstimate(flops=0, bytes_accessed=0, transcendentals=0),
        name="conv_weight_grad",
    )(nrm, dproj, small)


def finish_kernel(heads, share, parts, early, w_in, w_out, in_gain, gate_gain, *refs):
    own, got = refs[0], refs[1:parts]
    in_o, out_o, in_gain_o, gate_gain_o, cw_o, cb_o, sb_o, dl_o, sg_o, total = refs[parts:]
    ri, ro, cc = w_in.shape[0], w_out.shape[0], cb_o.shape[1]
    value = own[...]
    for part in got:
        value = value + part[...].astype(f32)
    total[...] = value
    in_o[:, :DI] = early[:, :DI].astype(f32)
    in_o[:, DI:] = total[0:ri, : CONV + heads]
    out_o[0:ri, :] = early[:, DI : DI + D].astype(f32)
    out_o[ri:, :] = early[:, DI + D :].astype(f32)

    def across(column, count):
        spot = lax.broadcasted_iota(jnp.int32, (count, count), 0) == lax.broadcasted_iota(jnp.int32, (count, count), 1)
        return jnp.sum(jnp.where(spot, column, 0.0), axis=0, keepdims=True)

    in_gain_o[...] = across(jnp.sum(w_in[...].astype(f32) * in_o[...], axis=-1, keepdims=True), ri) / in_gain[...].astype(f32)
    gate_gain_o[...] = across(jnp.sum(w_out[...].astype(f32) * out_o[...], axis=-1, keepdims=True), ro) / gate_gain[...].astype(f32)
    at = CONV + heads
    cw_o[...] = total[0:4, at : at + cc] + total[5:9, at : at + cc]
    cb_o[...] = total[4:5, at : at + cc] + total[9:10, at : at + cc]
    for k, term in enumerate((sb_o, dl_o, sg_o)):
        term[...] = total[10 + k : 11 + k, at : at + share] + total[13 + k : 14 + k, at : at + share]


def finish(early, w_in, w_out, in_gain, gate_gain, own, got, heads, share, cc):
    ri, ro = w_in.shape[0], w_out.shape[0]
    shapes = [(ri, w_in.shape[1]), (ro, D), (1, ri), (1, ro), (4, cc), (1, cc)] + [(1, share)] * 3
    return pl.pallas_call(
        functools.partial(finish_kernel, heads, share, 1 + len(got)),
        out_shape=[jax.ShapeDtypeStruct(shape, f32) for shape in shapes],
        scratch_shapes=[pltpu.VMEM(own.shape, f32)],
        name="finish",
    )(early, w_in, w_out, in_gain, gate_gain, own, *got)


def stages_of(mesh):
    ndp, nf = mesh.shape["dp"], mesh.shape["fsdp"]
    out = []
    stride = 1
    while stride < nf:
        group = 2 if stride == 1 else min(4, nf // stride)
        out.append(("fsdp", stride, group, stride))
        stride *= group
    stride = 1
    while stride < ndp:
        group = min(4, ndp // stride)
        out.append(("dp", stride, group, stride * nf))
        stride *= group
    return out[::-1]


def pairs_of(stages):
    out = []
    for axis, stride, group, number in stages[::-1]:
        step = 1
        while step < group:
            out.append((axis, stride * step, 2, number * step))
            step *= 2
    return out


def slot_devices(stages):
    rel = np.zeros((1,), np.int32)
    for _, _, group, number in stages:
        rel = (np.arange(group, dtype=np.int32)[:, None] * number + rel[None, :]).reshape(-1)
    return jnp.asarray(rel)


def swap(arr, axis, size, offset):
    return lax.ppermute(arr, axis, [(i, i ^ offset) for i in range(size)])


def gather_stage(block, stage, sizes):
    axis, stride, group, _ = stage
    return jnp.stack([block] + [swap(block, axis, sizes[axis], k * stride) for k in range(1, group)])


def scatter_parts(kept, stage, sizes):
    axis, stride, group, _ = stage
    low = kept.astype(bf16)
    return [swap(low[k], axis, sizes[axis], k * stride) for k in range(1, group)]


def scatter_stage(kept, stage, sizes):
    total = kept[0]
    for part in scatter_parts(kept, stage, sizes):
        total = total + part.astype(f32)
    return total


def before(value, *others):
    return lax.optimization_barrier((value,) + others)


def local(mesh, tokens, cotangent, segments, in_gain, weight_in, conv_weight, conv_bias, step_bias, decay_log, skip_gain,
          gate_gain, weight_out):
    sizes = {"dp": mesh.shape["dp"], "fsdp": mesh.shape["fsdp"]}
    nf = sizes["fsdp"]
    nd = sizes["dp"] * nf
    axes = ("dp", "fsdp")
    stages = stages_of(mesh)
    me = lax.axis_index("dp") * nf + lax.axis_index("fsdp")
    seqs, length, _ = tokens.shape
    rows = seqs * length
    ri, ro, cc, share = weight_in.shape[0], weight_out.shape[0], conv_bias.shape[0], step_bias.shape[0]
    heads = share * nf

    device = slot_devices(stages) ^ me
    feature = (device[:, None] * ri + jnp.arange(ri)[None, :]).reshape(-1)
    order = (jnp.arange(D)[:, None] == feature[None, :]).astype(bf16)

    tall = max(ri, 16)
    wc, later = pack(weight_in, weight_out, in_gain[None], conv_weight, conv_bias[None], gate_gain[None],
                     step_bias[None], decay_log[None], skip_gain[None], ri, tall)
    later = lax.all_gather(later, axes, axis=0, tiled=True)
    tok = tokens.reshape(rows, D)
    up = cotangent.reshape(rows, D)
    wc = gather_stage(wc, stages[0], sizes)
    tok_s = jnp.dot(tok, order, preferred_element_type=bf16)
    device_rows = jnp.broadcast_to(device.astype(f32)[:, None], (nd, 128))
    seg = segments.reshape(rows // Q, 1, Q)
    wc, tok_s, device_rows, seg = before(wc, tok_s, device_rows, seg)
    for stage in stages[1:-1]:
        wc = gather_stage(wc, stage, sizes)
    up_s = jnp.dot(up, order, preferred_element_type=bf16)
    wc, up_s = before(wc, up_s)
    wc_b = swap(wc, stages[-1][0], sizes[stages[-1][0]], stages[-1][1])
    halves = [part.reshape(nd // 2, tall, CONV + 256) for part in (wc, wc_b)]
    small = jnp.concatenate([part[:, :16, CONV + 128 :] for part in halves], axis=0).transpose(1, 0, 2).astype(f32)
    wc_a, wc_b = [part[:, :ri].reshape(D // 2, CONV + 256) for part in halves]

    cin, act, dact, nrm, scan, st, z, gain, gain_abs, cw, cb, gg, head_terms, skip = forward_scan(
        tok_s, wc_a, wc_b, small, device_rows, seg, seqs, ri, ro, share, heads)
    mixed, dscan, dgate, early, wo = gate_pass(tok, scan, up, later, gain_abs, gg, ri)
    early = lax.psum_scatter(early, axes, scatter_dimension=0, tiled=True)

    dproj, gproj, small = backward_scan(
        dscan, cin, act, dact, z, st, cw, head_terms, skip, seg, wc_a, wc_b, device_rows, heads, seqs, nf, share, tall)
    if ri == tall:
        halves = conv_weight_grad(nrm, dproj, small)
        halves = [half.reshape(nd // 2, tall, CONV + 128) for half in halves]
    else:
        halves = conv_weight_grad(nrm, dproj, jnp.zeros((D, 128), bf16))
        halves = [jnp.pad(half.reshape(nd // 2, ri, CONV + 128), ((0, 0), (0, tall - ri), (0, 0))) for half in halves]
        small = jnp.pad(small.reshape(nd, tall, 128), ((0, 0), (0, 0), (CONV, 0)))
        halves = [half + part for half, part in zip(halves, (small[: nd // 2], small[nd // 2 :]))]

    axis, stride, group, _ = stages[-1]
    total = halves[0].astype(f32) + swap(halves[1], axis, sizes[axis], stride).astype(f32)
    total = total.reshape([g for _, _, g, _ in stages[-2::-1]] + [tall, CONV + 128])
    total, gain = before(total, gain)
    gtok = norm_back(gproj, dgate, tok_s, up_s, later, gain, device_rows, ri)
    for stage in stages[-2:0:-1]:
        total = scatter_stage(total, stage, sizes)
    total, gtok, wo = before(total, gtok, wo)
    got = scatter_parts(total, stages[0], sizes)
    out = out_pass(mixed, tok, wo)
    early, out = before(early, out)
    g_in, g_out, g_in_gain, g_gate_gain, g_cw, g_cb, g_sb, g_dl, g_sg = finish(
        early, weight_in, weight_out, in_gain[None], gate_gain[None], total[0], got, heads, share, cc)
    return (out.reshape(tokens.shape), gtok.reshape(tokens.shape), g_in_gain[0], g_in, g_cw, g_cb[0],
            g_sb[0], g_dl[0], g_sg[0], g_gate_gain[0], g_out)


def solution(mesh):
    every = ("dp", "fsdp")
    return jax.shard_map(
        functools.partial(local, mesh),
        mesh=mesh,
        in_specs=(P(every, None, None), P(every, None, None), P(every, None), P(every), P(every, None), P(None, every),
                  P(every), P("fsdp"), P("fsdp"), P("fsdp"), P(every), P(every, None)),
        out_specs=(P(every, None, None), P(every, None, None), P(every), P(every, None), P(None, every), P(every),
                   P("fsdp"), P("fsdp"), P("fsdp"), P(every), P(every, None)),
        check_vma=False,
    )
```

```python
import functools

import jax
import jax.numpy as jnp
import numpy as np
from jax import lax
from jax.experimental import pallas as pl
from jax.experimental.pallas import tpu as pltpu
from jax.sharding import PartitionSpec as P

EPS = 1e-05
LOG2E = 1.4426950408889634
NEG = -1e30
f32, bf16 = jnp.float32, jnp.bfloat16
Q = 128
VM = 60 * 1024 * 1024

D, DI, CONV, N, HD = 768, 1536, 1792, 128, 64


def dot(a, b):
    return lax.dot_general(a, b, (((1,), (0,)), ((), ())), preferred_element_type=f32)


def dot_nt(a, b):
    return lax.dot_general(a, b, (((1,), (1,)), ((), ())), preferred_element_type=f32)


def dot_tn(a, b):
    return lax.dot_general(a, b, (((0,), (0,)), ((), ())), preferred_element_type=f32)


def sigmoid(v):
    return 1.0 / (1.0 + jnp.exp(-v))


def cumsum_rows(v, reverse=False):
    rows = lax.broadcasted_iota(jnp.int32, v.shape, 0)
    count = v.shape[0]
    shift = 1
    while shift < count:
        if reverse:
            moved = pltpu.roll(v, count - shift, 0)
            v = v + jnp.where(rows < count - shift, moved, 0.0)
        else:
            moved = pltpu.roll(v, shift, 0)
            v = v + jnp.where(rows >= shift, moved, 0.0)
        shift *= 2
    return v


def step_terms(z):
    e = jnp.exp(-jnp.abs(z))
    soft = jnp.maximum(z, 0.0) + jnp.log1p(e)
    tiny = z < -15.0
    log_soft = jnp.where(tiny, z, jnp.log(jnp.where(tiny, 1.0, soft)))
    return soft, log_soft


def columns(row):
    return jnp.broadcast_to(row, (Q, 128)).T


def documents(row, before_row, docs):
    doc = columns(row)
    docs[0:8, :] = columns(before_row)[Q - 8 : Q, :]
    docs[8 : 8 + Q, :] = doc
    return doc, [(docs[8 - s : 8 - s + Q, :] == doc).astype(f32) for s in (3, 2, 1)]


def scan_factors(z, rate, doc, prev_doc):
    soft, log_soft = step_terms(z)
    a = cumsum_rows(soft * (rate * LOG2E))
    b = a - log_soft * LOG2E
    last = a[Q - 1 : Q, :]
    last_doc = doc[Q - 1 : Q, :]
    reach = jnp.where(doc == prev_doc, jnp.exp2(a), 0.0)
    tail = jnp.where(doc == last_doc, jnp.exp2(last - b), 0.0)
    keep = jnp.where(last_doc == prev_doc, jnp.exp2(last), 0.0)
    return soft, a, b, reach, tail, keep


def pair_of(cols, p, low):
    left = jnp.broadcast_to(cols[:, 2 * p : 2 * p + 1], low.shape)
    right = jnp.broadcast_to(cols[:, 2 * p + 1 : 2 * p + 2], low.shape)
    return jnp.where(low, left, right)


def two_parts(cols):
    hi = cols.astype(bf16)
    return jnp.concatenate([hi, (cols - hi.astype(f32)).astype(bf16)], axis=1)


def head_onehot(shape):
    head = lax.broadcasted_iota(jnp.int32, shape, 1) >> 6
    return (lax.broadcasted_iota(jnp.int32, shape, 0) & 127 == head).astype(bf16)


def pack_kernel(ri, w_in, w_out, in_gain, cw, cb, gg, sb, dl, sg, wc_o, later_o, rows):
    wc_o[...] = jnp.zeros_like(wc_o)
    wc_o[0:ri, : w_in.shape[1] - DI] = w_in[:, DI:]
    rows[...] = jnp.zeros_like(rows)
    at = w_in.shape[1] - DI - CONV

    def put(n, value):
        rows[n : n + value.shape[0], at : at + value.shape[1]] = value.astype(f32)

    put(0, in_gain[...])
    put(1, cw[...])
    put(5, cb[...])
    put(6, gg[...])
    for k, term in enumerate((sb, dl, sg)):
        value = term[...]
        for n in range(3):
            part = value.astype(bf16).astype(f32)
            put(7 + 3 * n + k, part)
            value = value - part
    wc_o[0:16, CONV:] = (wc_o[0:16, CONV:].astype(f32) + rows[...]).astype(bf16)
    later_o[:, :DI] = w_in[:, :DI]
    later_o[:, DI : DI + D] = w_out[0:ri, :]
    later_o[:, DI + D :] = w_out[ri:, :]


def pack(w_in, w_out, in_gain, cw, cb, gg, sb, dl, sg, ri, tall):
    return pl.pallas_call(
        functools.partial(pack_kernel, ri),
        out_shape=[jax.ShapeDtypeStruct((tall, CONV + 128), bf16), jax.ShapeDtypeStruct((ri, 2 * DI), bf16)],
        scratch_shapes=[pltpu.VMEM((16, 128), f32)],
        name="pack",
    )(w_in, w_out, in_gain, cw, cb, gg, sb, dl, sg)


def unpack_small(ri, ro, share, first_lane, small, device, onehot, gain, gain_abs, cw, cb, gg, heads_o, skip):
    nd = small.shape[1]
    slot = lax.broadcasted_iota(jnp.int32, (nd, 128), 0).astype(f32)[:, 0:1]
    owner = device[...][:, 0:1]

    def spread(rows, width, total, who):
        lane = lax.broadcasted_iota(jnp.int32, (128, total), 1).astype(f32)
        piece = jnp.floor((lane + 0.5) * (1.0 / width))
        inner = lane - piece * width
        pick = (lax.broadcasted_iota(jnp.int32, (128, total), 0).astype(f32) - first_lane == inner).astype(bf16)
        mine = piece[0:1, :] == who
        out = dot(jnp.concatenate([small[r].astype(bf16) for r in rows], axis=0), pick)
        return [jnp.sum(jnp.where(mine, out[nd * n : nd * n + nd], 0.0), axis=0, keepdims=True) for n in range(len(rows))]

    gain[...] = spread([0], ri, D, slot)[0]
    gain_abs[...] = spread([0], ri, D, owner)[0]
    taps = spread(range(1, 6), CONV // nd, CONV, owner)
    for k in range(4):
        cw[k : k + 1, :] = 0.5 * taps[k]
    cw[4:8, :] = jnp.zeros((4, CONV), f32)
    cb[...] = 0.5 * taps[4]
    gg[...] = spread([6], ro, DI, owner)[0]
    parts = spread(range(7, 16), share, 128, owner)
    per_head = [parts[n] + parts[n + 3] + parts[n + 6] for n in range(3)]
    heads_o[0:1, :] = per_head[0]
    heads_o[1:2, :] = -jnp.exp(per_head[1])
    skip[...] = dot(two_parts(jnp.broadcast_to(per_head[2], (8, 128))), onehot[...])[0:1, :]


def clear_free(wc, heads):
    last = wc[:, CONV:]
    wc[:, CONV:] = jnp.where(lax.broadcasted_iota(jnp.int32, last.shape, 1) < heads, last, jnp.zeros_like(last))


def forward_scan_kernel(heads, per_seq, ri, ro, share, first, tok, wc_a, wc_b, small, device, seg, seg_before,
                        cin_o, act_o, dact_o, nrm_o, scan_o, st_o, z_o, gain, gain_abs, cw, cb, gg, heads_o, skip,
                        pbuf, zbuf, nbuf, pnext, znext, nnext, state, docs, onehot, wc, sems):
    i = pl.program_id(0)
    tiles = CONV // 128

    def normed(block):
        x = block[...].astype(f32)
        r = lax.rsqrt(jnp.mean(x * x, axis=-1, keepdims=True) + EPS)
        nnext[...] = (x * r * gain[...]).astype(bf16)

    def project(t):
        part = dot(nnext[...], wc[:, 128 * t : 128 * t + 256])
        pnext[t] = part[:, :128]
        pnext[t + 1] = part[:, 128:]

    def project_step():
        znext[...] = dot(nnext[...], wc[:, CONV:]) + heads_o[0:1, :]

    def advance():
        pbuf[:, 8 : 8 + Q, :] = pnext[...]
        zbuf[...] = znext[...]
        nbuf[...] = nnext[...]

    @pl.when(i == 0)
    def _():
        rows = wc_a.shape[0]
        copies = [pltpu.make_async_copy(wc_a, wc.at[0:rows], sems.at[0]),
                  pltpu.make_async_copy(wc_b, wc.at[rows : 2 * rows], sems.at[1])]
        for copy in copies:
            copy.start()
        onehot[...] = head_onehot(onehot.shape)
        unpack_small(ri, ro, share, heads, small, device, onehot, gain, gain_abs, cw, cb, gg, heads_o, skip)
        normed(first)
        for copy in copies:
            copy.wait()
        clear_free(wc, heads)
        for t in range(0, tiles, 2):
            project(t)
        project_step()
        advance()

    @pl.when(lax.rem(i, per_seq) == 0)
    def _():
        pbuf[:, 0:8, :] = jnp.zeros((tiles, 8, 128), f32)
        state[...] = jnp.zeros_like(state)

    nrm_o[...] = nbuf[...]
    z = zbuf[...]
    z_o[...] = z
    doc_row = seg[0].astype(f32)
    before_row = jnp.where(lax.rem(i, per_seq) == 0, -1.0, seg_before[0].astype(f32))
    doc, masks = documents(doc_row, before_row, docs)
    prev = docs[7:8, :]
    soft, a, b, reach, tail, keep = scan_factors(z, heads_o[1:2, :], doc, prev)
    factors = two_parts(jnp.concatenate([reach, tail, jnp.broadcast_to(keep, (8, 128))], axis=0))
    bt = b.T
    row = lax.broadcasted_iota(jnp.int32, (Q, Q), 0)
    lane = lax.broadcasted_iota(jnp.int32, (Q, Q), 1)
    joined = (row >= lane) & (doc == doc_row)
    low = lane < HD
    zero = jnp.zeros((Q, Q), bf16)

    def conv(t):
        cols = slice(128 * t, 128 * t + 128)
        here = pbuf[t, 8 : 8 + Q, :]
        cin_o[:, cols] = here.astype(bf16)
        half = cb[:, cols] + cw[3:4, cols] * here
        for k in range(3):
            half = half + cw[k : k + 1, cols] * (pbuf[t, 5 + k : 5 + k + Q, :] * masks[k])
        pbuf[t, 0:8, :] = pbuf[t, Q : Q + 8, :]
        up = 1.0 + jnp.tanh(half)
        act = half * up
        dact_o[:, cols] = (up + act * (2.0 - up)).astype(bf16)
        act = act.astype(bf16)
        act_o[:, cols] = act
        return act

    normed(tok)
    bmat = conv(tiles - 2)
    cmat = conv(tiles - 1)
    bt_mat = bmat.astype(f32).T.astype(bf16)
    s = dot_nt(cmat, bmat)
    for p in range(heads // 2):
        cols = slice(128 * p, 128 * p + 128)
        half = slice(128 * (p % 2), 128 * (p % 2) + 128)
        if p % 2 == 0:
            group = slice(128 * p, 128 * p + 256)
            wide = dot(factors, onehot[:, group])
            st_low = state[:, group].astype(bf16)
            st_o[0, :, group] = st_low
            cs = dot(cmat, st_low)
        xp = conv(p)
        if p < tiles // 2:
            project(2 * p)
        if p == tiles // 2:
            project_step()
        parts = []
        for h in (2 * p, 2 * p + 1):
            spread = jnp.broadcast_to(a[:, h : h + 1], (Q, Q)) - bt[h : h + 1, :]
            parts.append((jnp.exp2(jnp.where(joined, spread, NEG)) * s).astype(bf16))
        xbd = jnp.concatenate([jnp.where(low, xp, zero), jnp.where(low, zero, xp)], axis=0)
        y = dot(jnp.concatenate(parts, axis=1), xbd)
        xf = xp.astype(f32)
        y = y + cs[:, half] * wide[0:Q, half] + xf * skip[:, cols]
        scan_o[:, cols] = y.astype(bf16)
        xw = (xf * wide[Q : 2 * Q, half]).astype(bf16)
        state[:, cols] = state[:, cols] * wide[2 * Q : 2 * Q + 1, half] + dot(bt_mat, xw)
    advance()


def forward_scan(tok, wc_a, wc_b, small, device, seg, seqs, ri, ro, share, heads):
    rows = tok.shape[0]
    n = rows // Q
    one = pl.Buffered(buffer_count=1)
    full = lambda arr: pl.BlockSpec(arr.shape, lambda i: (0,) * arr.ndim, pipeline_mode=one)
    blk = lambda w: pl.BlockSpec((Q, w), lambda i: (i, 0))
    hbm = pl.BlockSpec(memory_space=pl.ANY)
    low = lambda *shape: jax.ShapeDtypeStruct(shape, bf16)
    sides = [(1, D), (1, D), (8, CONV), (1, CONV), (1, DI), (8, 128), (1, DI)]
    side = lambda shape: pl.BlockSpec(shape, lambda i: (0, 0))
    return pl.pallas_call(
        functools.partial(forward_scan_kernel, heads, n // seqs, ri, ro, share),
        grid=(n,),
        in_specs=[pl.BlockSpec((Q, D), lambda i: (0, 0), pipeline_mode=one),
                  pl.BlockSpec((Q, D), lambda i: (jnp.minimum(i + 1, n - 1), 0)), hbm, hbm, full(small), full(device),
                  pl.BlockSpec((1, 1, Q), lambda i: (i, 0, 0)), pl.BlockSpec((1, 1, Q), lambda i: (jnp.maximum(i - 1, 0), 0, 0))],
        out_specs=[blk(CONV), blk(CONV), blk(CONV), blk(D), blk(DI), pl.BlockSpec((1, N, DI), lambda i: (i, 0, 0)), blk(128)]
        + [side(shape) for shape in sides],
        out_shape=[low(rows, CONV), low(rows, CONV), low(rows, CONV), low(rows, D), low(rows, DI), low(n, N, DI),
                   jax.ShapeDtypeStruct((rows, 128), f32)] + [jax.ShapeDtypeStruct(shape, f32) for shape in sides],
        scratch_shapes=[pltpu.VMEM((CONV // 128, Q + 8, 128), f32), pltpu.VMEM((Q, 128), f32), pltpu.VMEM((Q, D), bf16),
                        pltpu.VMEM((CONV // 128, Q, 128), f32), pltpu.VMEM((Q, 128), f32), pltpu.VMEM((Q, D), bf16),
                        pltpu.VMEM((N, DI), f32), pltpu.VMEM((Q + 8, 128), f32), pltpu.VMEM((256, DI), bf16),
                        pltpu.VMEM((D, CONV + 128), bf16), pltpu.SemaphoreType.DMA((2,))],
        compiler_params=pltpu.CompilerParams(vmem_limit_bytes=56 << 20),
        name="forward_scan",
    )(tok, tok, wc_a, wc_b, small, device, seg, seg)


def block_order(ri):
    row = lax.broadcasted_iota(jnp.int32, (192, 192), 0)
    lane = lax.broadcasted_iota(jnp.int32, (192, 192), 1)
    second = lane >= 96
    at = jnp.where(second, lane - 96, lane)
    owner = lax.div(at, ri)
    target = owner * (2 * ri) + (at - owner * ri) + jnp.where(second, ri, 0)
    return (row == target).astype(bf16)


def gate_kernel(ri, tok, scan, cot, later_in, gain, gg, mixed_o, dscan_o, dgate_o, early_o, wo_o, later, wo, early, sems,
                acc_g, acc_o, nb_s, nbt_s, mixt_s, h_s, e_s, gated_s, eg_s):
    i = pl.program_id(0)
    bm, high = 256, 32
    blocks = tok.shape[0] // bm

    wo_copy = pltpu.make_async_copy(wo, wo_o, sems.at[2])

    @pl.when(i == 0)
    def _():
        copies = [pltpu.make_async_copy(later_in.at[:, cols], later.at[:, cols], sems.at[n])
                  for n, cols in enumerate((slice(DI, 2 * DI), slice(0, DI)))]
        for copy in copies:
            copy.start()
        acc_g[...] = jnp.zeros_like(acc_g)
        acc_o[...] = jnp.zeros_like(acc_o)
        copies[0].wait()
        put = block_order(ri)
        for g in range(D // 96):
            at = slice(96 * g, 96 * g + 96)
            halves = jnp.concatenate([later[at, DI : DI + D], later[at, DI + D :]], axis=0)
            wo[192 * g : 192 * g + 192, :] = dot(put, halves).astype(bf16)
        wo_copy.start()
        copies[1].wait()

    x = tok[...].astype(f32)
    r = lax.rsqrt(jnp.mean(x * x, axis=-1, keepdims=True) + EPS)
    nb = (x * r * gain[...]).astype(bf16)
    nb_s[...] = nb * 0.5
    nbt_s[...] = nb.T

    def products(n):
        rows = slice(bm * n, bm * n + bm)
        for c in range(DI // 256):
            cols = slice(256 * c, 256 * c + 256)
            h_s[rows, cols] = dot(nb_s[rows, :], later[:, cols])
            yield
            e_s[rows, cols] = dot_nt(cot[rows, :], wo[cols, :])
            yield

    def sums(n):
        rows = slice(bm * n, bm * n + bm)
        for c in range(DI // 256):
            cols = slice(256 * c, 256 * c + 256)
            mixt_s[cols, :] = mixed_o[rows, cols].T
        for c in range(D // 256):
            cols = slice(256 * c, 256 * c + 256)
            acc_o[:, cols] += dot(mixt_s[...], cot[rows, cols])
            yield
        for c in range(DI // 256):
            cols = slice(256 * c, 256 * c + 256)
            acc_g[:, cols] += dot(nbt_s[:, rows], dgate_o[rows, cols])
            yield

    def elementwise(n, part):
        rows = slice(bm * n + part * high, bm * n + part * high + high)
        squares = jnp.zeros((high, 128), f32)
        cross = jnp.zeros((high, 128), f32)
        for t in range(DI // 128):
            cols = slice(128 * t, 128 * t + 128)
            h = h_s[rows, cols]
            gated = scan[rows, cols].astype(f32) * (h + h * jnp.tanh(h))
            eg = e_s[rows, cols] * gg[:, cols]
            squares = squares + gated * gated
            cross = cross + gated * eg
            gated_s[part, :, cols] = gated
            eg_s[part, :, cols] = eg
        rr = lax.rsqrt(jnp.sum(squares, axis=-1, keepdims=True) * (1.0 / DI) + EPS)
        pull = rr * rr * rr * (jnp.sum(cross, axis=-1, keepdims=True) * (1.0 / DI))
        rr = jnp.broadcast_to(rr, (high, 128))
        pull = jnp.broadcast_to(pull, (high, 128))
        yield
        for t in range(DI // 128):
            cols = slice(128 * t, 128 * t + 128)
            h = h_s[rows, cols]
            th = jnp.tanh(h)
            gated = gated_s[part, :, cols]
            mixed_o[rows, cols] = (gated * rr * gg[:, cols]).astype(bf16)
            dg = eg_s[part, :, cols] * rr - gated * pull
            act = h + h * th
            dscan_o[rows, cols] = (dg * act).astype(bf16)
            dg = dg * scan[rows, cols].astype(f32)
            dgate_o[rows, cols] = (dg * ((1.0 + th) + act * (1.0 - th))).astype(bf16)
        yield

    def both(n, matrix):
        vector = [step for part in range(bm // high) for step in [elementwise(n, part)] * 2]
        for step in vector:
            next(step)
            next(matrix, None)
        for _ in matrix:
            pass

    for _ in products(0):
        pass
    for n in range(blocks):
        both(n, products(n + 1) if n + 1 < blocks else sums(n - 1))
    for _ in sums(blocks - 1):
        pass

    @pl.when(i == pl.num_programs(0) - 1)
    def _():
        put = block_order(ri)
        for g in range(D // 96):
            at = slice(96 * g, 96 * g + 96)
            early[at, :DI] = (0.5 * acc_g[at, :]).astype(bf16)
            halves = dot_tn(put, acc_o[192 * g : 192 * g + 192, :].astype(bf16)).astype(bf16)
            early[at, DI : DI + D] = halves[:96]
            early[at, DI + D :] = halves[96:]
            pltpu.make_async_copy(early.at[at], early_o.at[at], sems.at[3 + g]).start()
        for g in range(D // 96):
            at = slice(96 * g, 96 * g + 96)
            pltpu.make_async_copy(early.at[at], early_o.at[at], sems.at[3 + g]).wait()
        wo_copy.wait()


def gate_pass(tok, scan, cot, later, gain, gg, ri, bm=512):
    rows = tok.shape[0]
    one = pl.Buffered(buffer_count=1)
    full = lambda shape: pl.BlockSpec(shape, lambda i: (0,) * len(shape), pipeline_mode=one)
    blk = lambda w: pl.BlockSpec((bm, w), lambda i: (i, 0))
    hbm = pl.BlockSpec(memory_space=pl.ANY)
    low = lambda *shape: jax.ShapeDtypeStruct(shape, bf16)
    return pl.pallas_call(
        functools.partial(gate_kernel, ri),
        grid=(rows // bm,),
        in_specs=[blk(D), blk(DI), blk(D), hbm, full(gain.shape), full(gg.shape)],
        out_specs=[blk(DI), blk(DI), blk(DI), hbm, hbm],
        out_shape=[low(rows, DI), low(rows, DI), low(rows, DI), low(D, 2 * DI), low(DI, D)],
        scratch_shapes=[pltpu.VMEM((D, 2 * DI), bf16), pltpu.VMEM((DI, D), bf16), pltpu.VMEM((D, 2 * DI), bf16),
                        pltpu.SemaphoreType.DMA((3 + D // 96,)), pltpu.VMEM((D, DI), f32), pltpu.VMEM((DI, D), f32), pltpu.VMEM((bm, D), bf16), pltpu.VMEM((D, bm), bf16),
                        pltpu.VMEM((DI, 256), bf16),
                        pltpu.VMEM((bm, DI), f32), pltpu.VMEM((bm, DI), f32), pltpu.VMEM((8, 32, DI), f32),
                        pltpu.VMEM((8, 32, DI), f32)],
        compiler_params=pltpu.CompilerParams(vmem_limit_bytes=VM),
        name="gate_pass",
    )(tok, scan, cot, later, gain, gg)


def out_kernel(mixed, tok, wo, out_o):
    out_o[...] = (tok[...].astype(f32) + dot(mixed[...], wo[...])).astype(bf16)


def out_pass(mixed, tok, wo, bm=512):
    rows = tok.shape[0]
    blk = lambda w: pl.BlockSpec((bm, w), lambda i: (i, 0))
    return pl.pallas_call(
        out_kernel,
        grid=(rows // bm,),
        in_specs=[blk(DI), blk(D), pl.BlockSpec((DI, D), lambda i: (0, 0), pipeline_mode=pl.Buffered(buffer_count=1))],
        out_specs=blk(D),
        out_shape=jax.ShapeDtypeStruct((rows, D), bf16),
        compiler_params=pltpu.CompilerParams(vmem_limit_bytes=50 << 20),
        cost_estimate=pl.CostEstimate(flops=0, bytes_accessed=0, transcendentals=0),
        name="out_pass",
    )(mixed, tok, wo)


def pack_grads(nf, share, tall, gcw, gcb, gsk, ghd, device, sums, rows, out_o):
    nd = device.shape[0]
    owner = device[...][:, 0:1]
    first_lane = nf * share

    def spread(values, width, who):
        total = values[0].shape[1]
        lane = lax.broadcasted_iota(jnp.int32, (128, total), 1).astype(f32)
        piece = jnp.floor((lane + 0.5) * (1.0 / width))
        place = lax.broadcasted_iota(jnp.int32, (128, total), 0).astype(f32) - first_lane
        pick = ((place == lane - piece * width) & (place < width)).astype(bf16)
        mine = piece[0:1, :] == who
        terms = []
        for value in values:
            hi = value.astype(bf16).astype(f32)
            terms += [jnp.where(mine, part, 0.0).astype(bf16) for part in (hi, value - hi)]
        out = dot_nt(jnp.concatenate(terms, axis=0), pick)
        return [out[nd * k : nd * k + nd] for k in range(len(terms))]

    rows[...] = jnp.zeros_like(rows)

    def put(n, values):
        rows[pl.ds(n, nd, stride=tall), :] = values

    taps = [0.5 * jnp.sum(gcw[8 * k : 8 * k + 8, :], axis=0, keepdims=True) for k in range(4)]
    taps.append(0.5 * jnp.sum(gcb[...], axis=0, keepdims=True))
    for k, part in enumerate(spread(taps, CONV // nd, owner)):
        put(k // 2 + 5 * (k % 2), part)
    group = owner - nf * jnp.floor((owner + 0.5) * (1.0 / nf))
    skips = two_parts(jnp.broadcast_to(jnp.sum(gsk[...], axis=0, keepdims=True), (8, DI)))
    skips = dot(skips[:, :DI], sums[...]) + dot(skips[:, DI:], sums[...])
    per_head = [jnp.sum(ghd[0:8, :], axis=0, keepdims=True), jnp.sum(ghd[8:16, :], axis=0, keepdims=True), skips[0:1, :]]
    for k, part in enumerate(spread(per_head, share, group)):
        put(10 + k // 2 + 3 * (k % 2), part)
    out_o[...] = rows[...].astype(bf16)


def backward_scan_kernel(heads, per_seq, nf, share, tall, dscan, cin, act, dact, z_r, st, cw, head_terms, skip, seg, seg_before,
                         wc_a, wc_b, device, dproj_o, gproj_o, pack_o, gproj,
                         dstate, p1buf, qbuf, xwbuf, rowbuf, lastbuf, mbuf, onehot, sums, docs,
                         gcw_o, gcb_o, gsk_o, ghd_o, rows_s, wc, dlast, sems):
    i = pl.program_id(0)
    steps = pl.num_programs(0)

    @pl.when(i == 0)
    def _():
        half = wc_a.shape[0]
        copies = [pltpu.make_async_copy(wc_a, wc.at[0:half], sems.at[0]),
                  pltpu.make_async_copy(wc_b, wc.at[half : 2 * half], sems.at[1])]
        for copy in copies:
            copy.start()
        dlast[...] = jnp.zeros_like(dlast)
        gcw_o[...] = jnp.zeros_like(gcw_o)
        gcb_o[...] = jnp.zeros_like(gcb_o)
        gsk_o[...] = jnp.zeros_like(gsk_o)
        ghd_o[...] = jnp.zeros_like(ghd_o)
        rowbuf[...] = jnp.zeros_like(rowbuf)
        lastbuf[...] = jnp.zeros_like(lastbuf)
        onehot[...] = head_onehot(onehot.shape)
        head = lax.broadcasted_iota(jnp.int32, sums.shape, 0) >> 6
        sums[...] = (head == lax.broadcasted_iota(jnp.int32, sums.shape, 1)).astype(bf16)
        for copy in copies:
            copy.wait()
        clear_free(wc, heads)

    @pl.when(lax.rem(i, per_seq) == 0)
    def _():
        mbuf[:, :, Q : Q + 8, :] = jnp.zeros((3, CONV // 128, 8, 128), f32)
        dstate[...] = jnp.zeros_like(dstate)

    z = z_r[...]
    rate = head_terms[1:2, :]
    doc_row = seg[0].astype(f32)
    before_row = jnp.where(lax.rem(i, per_seq) == per_seq - 1, -1.0, seg_before[0].astype(f32))
    doc, masks = documents(doc_row, before_row, docs)
    prev = docs[7:8, :]
    soft, a, b, reach, tail, keep = scan_factors(z, rate, doc, prev)
    factors = two_parts(jnp.concatenate([reach, tail, jnp.broadcast_to(keep, (8, 128))], axis=0))
    at = a.T
    row = lax.broadcasted_iota(jnp.int32, (Q, Q), 0)
    lane = lax.broadcasted_iota(jnp.int32, (Q, Q), 1)
    joined = (lane >= row) & (doc == doc_row)
    low = lane < HD
    bmat = act[:, DI : DI + N]
    cmat = act[:, DI + N :]
    ct_mat = cmat.astype(f32).T.astype(bf16)
    s = dot_nt(bmat, cmat)
    ds_low = dstate[...].astype(bf16)
    zero = jnp.zeros((Q, Q), bf16)
    dst = jnp.zeros((Q, Q), f32)

    def conv_back(t, grad):
        cols = slice(128 * t, 128 * t + 128)
        dpre = grad * dact[:, cols].astype(f32)
        for k in range(3):
            mbuf[k, t, 0:Q, :] = dpre * masks[k]
        cv = cin[:, cols].astype(f32)
        dcin = cw[3:4, cols] * dpre
        gcb_o[:, cols] += jnp.sum(dpre.reshape(-1, 8, 128), axis=0)
        gcw_o[24:32, cols] += jnp.sum((cv * dpre).reshape(-1, 8, 128), axis=0)
        for k in range(3):
            moved = mbuf[k, t, 3 - k : 3 - k + Q, :]
            dcin = dcin + cw[k : k + 1, cols] * moved
            gcw_o[8 * k : 8 * k + 8, cols] += jnp.sum((cv * moved).reshape(-1, 8, 128), axis=0)
        dproj_o[:, cols] = dcin.astype(bf16)
        mbuf[:, t, Q : Q + 8, :] = mbuf[:, t, 0:8, :]

    def project_back(given, block, part):
        cols = slice(256 * part, 256 * part + 256)
        gproj[pl.ds(block * Q, Q), cols] = dot_nt(given[...], wc[cols, :]).astype(bf16)

    block_before = steps - jnp.maximum(i, 1)
    for p in range(heads // 2):
        cols = slice(128 * p, 128 * p + 128)
        half = slice(128 * (p % 2), 128 * (p % 2) + 128)
        if p % 2 == 0:
            group = slice(128 * p, 128 * p + 256)
            wide = dot(factors, onehot[:, group])
            cs = dot(cmat, st[0, :, group])
            bd = dot(bmat, ds_low[:, group])
        if p % 4 == 1:
            project_back(dlast, block_before, p // 4)
        xp = act[:, cols]
        dy = dscan[:, cols]
        dybd = jnp.concatenate([jnp.where(low, dy, zero), jnp.where(low, zero, dy)], axis=0)
        dm = dot_nt(xp, dybd)
        parts = []
        for n, h in enumerate((2 * p, 2 * p + 1)):
            spread = at[h : h + 1, :] - jnp.broadcast_to(b[:, h : h + 1], (Q, Q))
            e = jnp.exp2(jnp.where(joined, spread, NEG))
            m = (e * s).astype(bf16)
            parts.append(m)
            dmh = dm[:, 128 * n : 128 * n + 128]
            dst = dst + dmh * e
            rowbuf[h : h + 1, :] = jnp.sum(dmh * m.astype(f32), axis=0, keepdims=True)
        xf = xp.astype(f32)
        dyf = dy.astype(f32)
        tail_p = wide[Q : 2 * Q, half]
        fresh = bd[:, half] * tail_p
        dx = dot(jnp.concatenate(parts, axis=1), dybd) + fresh
        p1 = xf * dx
        hi = p1.astype(bf16)
        p1buf[:, cols] = hi
        p1buf[:, DI + 128 * p : DI + 128 * p + 128] = (p1 - hi.astype(f32)).astype(bf16)
        dyr = dyf * wide[0:Q, half]
        qbuf[:, cols] = (dyr * cs[:, half]).astype(bf16)
        dyr = dyr.astype(bf16)
        ds = dstate[:, cols]
        lastbuf[0:1, cols] = jnp.sum(xf * fresh, axis=0, keepdims=True) + wide[2 * Q : 2 * Q + 1, half] * jnp.sum(
            ds * st[0, :, cols].astype(f32), axis=0, keepdims=True)
        gsk_o[:, cols] += jnp.sum((dyf * xf).reshape(-1, 8, 128), axis=0)
        xwbuf[:, cols] = (xf * tail_p).astype(bf16)
        xwbuf[:, DI + 128 * p : DI + 128 * p + 128] = dyr
        dstate[:, cols] = ds * wide[2 * Q : 2 * Q + 1, half] + dot(ct_mat, dyr)
        conv_back(p, dx + skip[:, cols] * dyf)
    dst_low = dst.astype(bf16)
    conv_back(DI // 128, dot(dst_low, cmat) + dot_nt(xwbuf[:, :DI], ds_low))
    conv_back(DI // 128 + 1, dot_tn(dst_low, bmat) + dot_nt(xwbuf[:, DI:], st[0]))
    hot = sums[...]
    p1 = dot(p1buf[:, :DI], hot) + dot(p1buf[:, DI:], hot)
    last = two_parts(lastbuf[...])
    last = (dot(last[:, :DI], hot) + dot(last[:, DI:], hot))[0:1, :]
    da = dot(qbuf[...], hot) - p1 + rowbuf[...].T
    g = cumsum_rows(da, reverse=True) + last
    sig = sigmoid(z)
    ratio = jnp.where(z < -15.0, 1.0, sig / jnp.where(z < -15.0, 1.0, soft))
    dz = g * rate * sig + p1 * ratio
    dproj_o[:, CONV:] = dz.astype(bf16)
    ghd_o[0:8, :] += jnp.sum(dz.reshape(-1, 8, 128), axis=0)
    ghd_o[8:16, :] += rate * jnp.sum((g * soft).reshape(-1, 8, 128), axis=0)
    dlast[...] = dproj_o[...]

    def copy_out(block):
        at = pl.ds(block * Q, Q)
        return pltpu.make_async_copy(gproj.at[at], gproj_o.at[at], sems.at[2])

    @pl.when(i > 0)
    def _():
        copy_out(block_before).start()

    @pl.when(i == steps - 1)
    def _():
        for part in range(D // 256):
            project_back(dlast, 0, part)
        copy_out(0).start()
        pack_grads(nf, share, tall, gcw_o, gcb_o, gsk_o, ghd_o, device, sums, rows_s, pack_o)
        pltpu.make_async_copy(gproj, gproj_o, sems.at[2]).wait()


def backward_scan(dscan, cin, act, dact, z, st, cw, head_terms, skip, seg, wc_a, wc_b, device, heads, seqs, nf, share, tall):
    rows = dscan.shape[0]
    n = rows // Q
    nd = device.shape[0]
    one = pl.Buffered(buffer_count=1)
    full = lambda shape: pl.BlockSpec(shape, lambda i: (0,) * len(shape), pipeline_mode=one)
    blk = lambda w: pl.BlockSpec((Q, w), lambda i: (n - 1 - i, 0))
    blk3 = lambda s1, s2: pl.BlockSpec((1, s1, s2), lambda i: (n - 1 - i, 0, 0))
    hbm = pl.BlockSpec(memory_space=pl.ANY)
    return pl.pallas_call(
        functools.partial(backward_scan_kernel, heads, n // seqs, nf, share, tall),
        grid=(n,),
        in_specs=[blk(DI), blk(CONV), blk(CONV), blk(CONV), blk(128), blk3(N, DI), full(cw.shape), full(head_terms.shape),
                  full(skip.shape), blk3(1, Q), pl.BlockSpec((1, 1, Q), lambda i: (jnp.maximum(n - 2 - i, 0), 0, 0)),
                  hbm, hbm, full(device.shape)],
        out_specs=[blk(CONV + 128), hbm, full((nd * tall, 128))],
        out_shape=[jax.ShapeDtypeStruct((rows, CONV + 128), bf16), jax.ShapeDtypeStruct((rows, D), bf16),
                   jax.ShapeDtypeStruct((nd * tall, 128), bf16)],
        scratch_shapes=[pltpu.VMEM((rows, D), bf16), pltpu.VMEM((N, DI), f32), pltpu.VMEM((Q, 2 * DI), bf16), pltpu.VMEM((Q, DI), bf16),
                        pltpu.VMEM((Q, 2 * DI), bf16), pltpu.VMEM((128, 128), f32), pltpu.VMEM((8, DI), f32),
                        pltpu.VMEM((3, CONV // 128, Q + 8, 128), f32), pltpu.VMEM((256, DI), bf16),
                        pltpu.VMEM((DI, 128), bf16), pltpu.VMEM((Q + 8, 128), f32), pltpu.VMEM((32, CONV), f32),
                        pltpu.VMEM((8, CONV), f32), pltpu.VMEM((8, DI), f32), pltpu.VMEM((16, 128), f32),
                        pltpu.VMEM((nd * tall, 128), f32), pltpu.VMEM((D, CONV + 128), bf16), pltpu.VMEM((Q, CONV + 128), bf16),
                        pltpu.SemaphoreType.DMA((3,))],
        compiler_params=pltpu.CompilerParams(vmem_limit_bytes=VM),
        cost_estimate=pl.CostEstimate(flops=0, bytes_accessed=0, transcendentals=0),
        name="backward_scan",
    )(dscan, cin, act, dact, z, st, cw, head_terms, skip, seg, seg, wc_a, wc_b, device)


def norm_back_kernel(ri, gproj, dgate, tok, cot, wg_abs, gain, device, out_o, wg, order):
    @pl.when(pl.program_id(0) == 0)
    def _():
        column = lax.broadcasted_iota(jnp.int32, (8, D), 1).astype(f32)
        slot = jnp.floor((column + 0.5) * (1.0 / ri))
        nd = device.shape[0]
        mine = lax.broadcasted_iota(jnp.int32, (nd, D), 0).astype(f32) == slot[0:1, :]
        feature = jnp.sum(jnp.where(mine, device[...][:, 0:1], 0.0), axis=0, keepdims=True) * ri + (column - slot * ri)[0:1, :]
        order[...] = (lax.broadcasted_iota(jnp.int32, (D, D), 0).astype(f32) == feature).astype(bf16)
        wg[...] = (0.5 * dot_tn(order[...], wg_abs[...])).astype(bf16)

    grad = dot_nt(dgate[...], wg[...]) + gproj[...].astype(f32)
    x = tok[...].astype(f32)
    r = lax.rsqrt(jnp.mean(x * x, axis=-1, keepdims=True) + EPS)
    unit = x * r
    e = gain[...] * grad
    back = r * (e - unit * jnp.mean(unit * e, axis=-1, keepdims=True))
    res = (cot[...].astype(f32) + back).astype(bf16)
    out_o[...] = dot_nt(res, order[...]).astype(bf16)


def norm_back(gproj, dgate, tok, cot, later, gain, device, ri, bm=512):
    rows = gproj.shape[0]
    one = pl.Buffered(buffer_count=1)
    full = lambda shape: pl.BlockSpec(shape, lambda i: (0,) * len(shape), pipeline_mode=one)
    blk = lambda w: pl.BlockSpec((bm, w), lambda i: (i, 0))
    return pl.pallas_call(
        functools.partial(norm_back_kernel, ri),
        grid=(rows // bm,),
        in_specs=[blk(D), blk(DI), blk(D), blk(D), full((D, DI)), full(gain.shape), full(device.shape)],
        out_specs=blk(D),
        out_shape=jax.ShapeDtypeStruct((rows, D), bf16),
        scratch_shapes=[pltpu.VMEM((D, DI), bf16), pltpu.VMEM((D, D), bf16)],
        compiler_params=pltpu.CompilerParams(vmem_limit_bytes=46 << 20),
        cost_estimate=pl.CostEstimate(flops=0, bytes_accessed=0, transcendentals=0),
        name="norm_back",
    )(gproj, dgate, tok, cot, later, gain, device)


def conv_weight_kernel(nrm, dproj, small, a_o, b_o):
    grad = lax.dot_general(dproj[...], nrm[...], (((0,), (0,)), ((), ())), preferred_element_type=f32)
    half = a_o.shape[0]
    out = grad.astype(bf16).T
    a_o[...] = out[:half]
    b_o[...] = out[half:]

    @pl.when(pl.program_id(0) == pl.num_programs(0) - 1)
    def _():
        last = slice(a_o.shape[1] - 128, a_o.shape[1])
        out = (grad[a_o.shape[1] - 128 :].T + small[...].astype(f32)).astype(bf16)
        a_o[:, last] = out[:half]
        b_o[:, last] = out[half:]


def conv_weight_grad(nrm, dproj, small, bn=640):
    rows = nrm.shape[0]
    one = pl.Buffered(buffer_count=1)
    return pl.pallas_call(
        conv_weight_kernel,
        grid=((CONV + 128) // bn,),
        in_specs=[pl.BlockSpec((rows, D), lambda i: (0, 0), pipeline_mode=one), pl.BlockSpec((rows, bn), lambda i: (0, i)),
                  pl.BlockSpec((D, 128), lambda i: (0, 0), pipeline_mode=one)],
        out_specs=[pl.BlockSpec((D // 2, bn), lambda i: (0, i))] * 2,
        out_shape=[jax.ShapeDtypeStruct((D // 2, CONV + 128), bf16)] * 2,
        compiler_params=pltpu.CompilerParams(vmem_limit_bytes=VM),
        cost_estimate=pl.CostEstimate(flops=0, bytes_accessed=0, transcendentals=0),
        name="conv_weight_grad",
    )(nrm, dproj, small)


def finish_kernel(heads, share, parts, early, w_in, w_out, in_gain, gate_gain, *refs):
    own, got = refs[0], refs[1:parts]
    in_o, out_o, in_gain_o, gate_gain_o, cw_o, cb_o, sb_o, dl_o, sg_o, total = refs[parts:]
    ri, ro, cc = w_in.shape[0], w_out.shape[0], cb_o.shape[1]
    value = own[...]
    for part in got:
        value = value + part[...].astype(f32)
    total[...] = value
    in_o[:, :DI] = early[:, :DI].astype(f32)
    in_o[:, DI:] = total[0:ri, : CONV + heads]
    out_o[0:ri, :] = early[:, DI : DI + D].astype(f32)
    out_o[ri:, :] = early[:, DI + D :].astype(f32)

    def across(column, count):
        spot = lax.broadcasted_iota(jnp.int32, (count, count), 0) == lax.broadcasted_iota(jnp.int32, (count, count), 1)
        return jnp.sum(jnp.where(spot, column, 0.0), axis=0, keepdims=True)

    in_gain_o[...] = across(jnp.sum(w_in[...].astype(f32) * in_o[...], axis=-1, keepdims=True), ri) / in_gain[...].astype(f32)
    gate_gain_o[...] = across(jnp.sum(w_out[...].astype(f32) * out_o[...], axis=-1, keepdims=True), ro) / gate_gain[...].astype(f32)
    at = CONV + heads
    cw_o[...] = total[0:4, at : at + cc] + total[5:9, at : at + cc]
    cb_o[...] = total[4:5, at : at + cc] + total[9:10, at : at + cc]
    for k, term in enumerate((sb_o, dl_o, sg_o)):
        term[...] = total[10 + k : 11 + k, at : at + share] + total[13 + k : 14 + k, at : at + share]


def finish(early, w_in, w_out, in_gain, gate_gain, own, got, heads, share, cc):
    ri, ro = w_in.shape[0], w_out.shape[0]
    shapes = [(ri, w_in.shape[1]), (ro, D), (1, ri), (1, ro), (4, cc), (1, cc)] + [(1, share)] * 3
    return pl.pallas_call(
        functools.partial(finish_kernel, heads, share, 1 + len(got)),
        out_shape=[jax.ShapeDtypeStruct(shape, f32) for shape in shapes],
        scratch_shapes=[pltpu.VMEM(own.shape, f32)],
        name="finish",
    )(early, w_in, w_out, in_gain, gate_gain, own, *got)


def stages_of(mesh):
    ndp, nf = mesh.shape["dp"], mesh.shape["fsdp"]
    out = []
    stride = 1
    while stride < nf:
        group = 2 if stride == 1 else min(4, nf // stride)
        out.append(("fsdp", stride, group, stride))
        stride *= group
    stride = 1
    while stride < ndp:
        group = min(4, ndp // stride)
        out.append(("dp", stride, group, stride * nf))
        stride *= group
    return out[::-1]


def pairs_of(stages):
    out = []
    for axis, stride, group, number in stages[::-1]:
        step = 1
        while step < group:
            out.append((axis, stride * step, 2, number * step))
            step *= 2
    return out


def slot_devices(stages):
    rel = np.zeros((1,), np.int32)
    for _, _, group, number in stages:
        rel = (np.arange(group, dtype=np.int32)[:, None] * number + rel[None, :]).reshape(-1)
    return jnp.asarray(rel)


def swap(arr, axis, size, offset):
    return lax.ppermute(arr, axis, [(i, i ^ offset) for i in range(size)])


def gather_stage(block, stage, sizes):
    axis, stride, group, _ = stage
    return jnp.stack([block] + [swap(block, axis, sizes[axis], k * stride) for k in range(1, group)])


def scatter_parts(kept, stage, sizes):
    axis, stride, group, _ = stage
    return [swap(kept[k].astype(bf16), axis, sizes[axis], k * stride) for k in range(1, group)]


def scatter_stage(kept, stage, sizes):
    total = kept[0]
    for part in scatter_parts(kept, stage, sizes):
        total = total + part.astype(f32)
    return total


def before(value, *others):
    return lax.optimization_barrier((value,) + others)


def local(mesh, tokens, cotangent, segments, in_gain, weight_in, conv_weight, conv_bias, step_bias, decay_log, skip_gain,
          gate_gain, weight_out):
    sizes = {"dp": mesh.shape["dp"], "fsdp": mesh.shape["fsdp"]}
    nf = sizes["fsdp"]
    nd = sizes["dp"] * nf
    axes = ("dp", "fsdp")
    stages = stages_of(mesh)
    me = lax.axis_index("dp") * nf + lax.axis_index("fsdp")
    seqs, length, _ = tokens.shape
    rows = seqs * length
    ri, ro, cc, share = weight_in.shape[0], weight_out.shape[0], conv_bias.shape[0], step_bias.shape[0]
    heads = share * nf

    device = slot_devices(stages) ^ me
    feature = (device[:, None] * ri + jnp.arange(ri)[None, :]).reshape(-1)
    order = (jnp.arange(D)[:, None] == feature[None, :]).astype(bf16)

    tall = max(ri, 16)
    wc, later = pack(weight_in, weight_out, in_gain[None], conv_weight, conv_bias[None], gate_gain[None],
                     step_bias[None], decay_log[None], skip_gain[None], ri, tall)
    later = lax.all_gather(later, axes, axis=0, tiled=True)
    tok = tokens.reshape(rows, D)
    up = cotangent.reshape(rows, D)
    wc = gather_stage(wc, stages[0], sizes)
    tok_s = jnp.dot(tok, order, preferred_element_type=bf16)
    device_rows = jnp.broadcast_to(device.astype(f32)[:, None], (nd, 128))
    seg = segments.reshape(rows // Q, 1, Q)
    wc, tok_s, device_rows, seg = before(wc, tok_s, device_rows, seg)
    for stage in stages[1:-1]:
        wc = gather_stage(wc, stage, sizes)
    up_s = jnp.dot(up, order, preferred_element_type=bf16)
    wc, up_s = before(wc, up_s)
    wc_b = swap(wc, stages[-1][0], sizes[stages[-1][0]], stages[-1][1])
    halves = [part.reshape(nd // 2, tall, CONV + 128) for part in (wc, wc_b)]
    small = jnp.concatenate([part[:, :16, CONV:] for part in halves], axis=0).transpose(1, 0, 2).astype(f32)
    wc_a, wc_b = [part[:, :ri].reshape(D // 2, CONV + 128) for part in halves]

    cin, act, dact, nrm, scan, st, z, gain, gain_abs, cw, cb, gg, head_terms, skip = forward_scan(
        tok_s, wc_a, wc_b, small, device_rows, seg, seqs, ri, ro, share, heads)
    mixed, dscan, dgate, early, wo = gate_pass(tok, scan, up, later, gain_abs, gg, ri)
    early = lax.psum_scatter(early, axes, scatter_dimension=0, tiled=True)

    dproj, gproj, small = backward_scan(
        dscan, cin, act, dact, z, st, cw, head_terms, skip, seg, wc_a, wc_b, device_rows, heads, seqs, nf, share, tall)
    if ri == tall:
        halves = conv_weight_grad(nrm, dproj, small)
        halves = [half.reshape(nd // 2, tall, CONV + 128) for half in halves]
    else:
        halves = conv_weight_grad(nrm, dproj, jnp.zeros((D, 128), bf16))
        halves = [jnp.pad(half.reshape(nd // 2, ri, CONV + 128), ((0, 0), (0, tall - ri), (0, 0))) for half in halves]
        small = jnp.pad(small.reshape(nd, tall, 128), ((0, 0), (0, 0), (CONV, 0)))
        halves = [half + part for half, part in zip(halves, (small[: nd // 2], small[nd // 2 :]))]

    axis, stride, group, _ = stages[-1]
    got = swap(halves[1], axis, sizes[axis], stride)
    shape = [g for _, _, g, _ in stages[-2::-1]] + [tall, CONV + 128]
    pieces = zip(halves[0].reshape(shape), got.reshape(shape))
    total = [mine.astype(f32) + part.astype(f32) for mine, part in pieces]
    total[0], gain = before(total[0], gain)
    gtok = norm_back(gproj, dgate, tok_s, up_s, later, gain, device_rows, ri)
    for stage in stages[-2:0:-1]:
        total = scatter_stage(total, stage, sizes)
    total, gtok, wo = before(total, gtok, wo)
    got = scatter_parts(total, stages[0], sizes)
    out = out_pass(mixed, tok, wo)
    early, out = before(early, out)
    g_in, g_out, g_in_gain, g_gate_gain, g_cw, g_cb, g_sb, g_dl, g_sg = finish(
        early, weight_in, weight_out, in_gain[None], gate_gain[None], total[0], got, heads, share, cc)
    return (out.reshape(tokens.shape), gtok.reshape(tokens.shape), g_in_gain[0], g_in, g_cw, g_cb[0],
            g_sb[0], g_dl[0], g_sg[0], g_gate_gain[0], g_out)


def solution(mesh):
    every = ("dp", "fsdp")
    return jax.shard_map(
        functools.partial(local, mesh),
        mesh=mesh,
        in_specs=(P(every, None, None), P(every, None, None), P(every, None), P(every), P(every, None), P(None, every),
                  P(every), P("fsdp"), P("fsdp"), P("fsdp"), P(every), P(every, None)),
        out_specs=(P(every, None, None), P(every, None, None), P(every), P(every, None), P(None, every), P(every),
                   P("fsdp"), P("fsdp"), P("fsdp"), P(every), P(every, None)),
        check_vma=False,
    )
```

```python
import functools

import jax
import jax.numpy as jnp
import numpy as np
from jax import lax
from jax.experimental import pallas as pl
from jax.experimental.pallas import tpu as pltpu
from jax.sharding import PartitionSpec as P

EPS = 1e-05
LOG2E = 1.4426950408889634
NEG = -1e30
f32, bf16 = jnp.float32, jnp.bfloat16
Q = 128
VM = 60 * 1024 * 1024

D, DI, CONV, N, HD = 768, 1536, 1792, 128, 64
SPLIT = 1024


def dot(a, b):
    return lax.dot_general(a, b, (((1,), (0,)), ((), ())), preferred_element_type=f32)


def dot_nt(a, b):
    return lax.dot_general(a, b, (((1,), (1,)), ((), ())), preferred_element_type=f32)


def dot_tn(a, b):
    return lax.dot_general(a, b, (((0,), (0,)), ((), ())), preferred_element_type=f32)


def sigmoid(v):
    return 1.0 / (1.0 + jnp.exp(-v))


def cumsum_rows(v, reverse=False):
    rows = lax.broadcasted_iota(jnp.int32, v.shape, 0)
    count = v.shape[0]
    shift = 1
    while shift < count:
        if reverse:
            moved = pltpu.roll(v, count - shift, 0)
            v = v + jnp.where(rows < count - shift, moved, 0.0)
        else:
            moved = pltpu.roll(v, shift, 0)
            v = v + jnp.where(rows >= shift, moved, 0.0)
        shift *= 2
    return v


def step_terms(z):
    e = jnp.exp(-jnp.abs(z))
    soft = jnp.maximum(z, 0.0) + jnp.log1p(e)
    tiny = z < -15.0
    log_soft = jnp.where(tiny, z, jnp.log(jnp.where(tiny, 1.0, soft)))
    return soft, log_soft


def columns(row):
    return jnp.broadcast_to(row, (Q, 128)).T


def documents(row, before_row, docs):
    doc = columns(row)
    docs[0:8, :] = columns(before_row)[Q - 8 : Q, :]
    docs[8 : 8 + Q, :] = doc
    return doc, [(docs[8 - s : 8 - s + Q, :] == doc).astype(f32) for s in (3, 2, 1)]


def scan_factors(z, rate, doc, prev_doc):
    soft, log_soft = step_terms(z)
    a = cumsum_rows(soft * (rate * LOG2E))
    b = a - log_soft * LOG2E
    last = a[Q - 1 : Q, :]
    last_doc = doc[Q - 1 : Q, :]
    reach = jnp.where(doc == prev_doc, jnp.exp2(a), 0.0)
    tail = jnp.where(doc == last_doc, jnp.exp2(last - b), 0.0)
    keep = jnp.where(last_doc == prev_doc, jnp.exp2(last), 0.0)
    return soft, a, b, reach, tail, keep


def pair_of(cols, p, low):
    left = jnp.broadcast_to(cols[:, 2 * p : 2 * p + 1], low.shape)
    right = jnp.broadcast_to(cols[:, 2 * p + 1 : 2 * p + 2], low.shape)
    return jnp.where(low, left, right)


def two_parts(cols):
    hi = cols.astype(bf16)
    return jnp.concatenate([hi, (cols - hi.astype(f32)).astype(bf16)], axis=1)


def head_onehot(shape):
    head = lax.broadcasted_iota(jnp.int32, shape, 1) >> 6
    return (lax.broadcasted_iota(jnp.int32, shape, 0) & 127 == head).astype(bf16)


def pack_kernel(ri, w_in, w_out, in_gain, cw, cb, gg, sb, dl, sg, wc_o, later_o, rows):
    wc_o[...] = jnp.zeros_like(wc_o)
    wc_o[0:ri, : w_in.shape[1] - DI] = w_in[:, DI:]
    rows[...] = jnp.zeros_like(rows)
    at = w_in.shape[1] - DI - CONV

    def put(n, value):
        rows[n : n + value.shape[0], at : at + value.shape[1]] = value.astype(f32)

    put(0, in_gain[...])
    put(1, cw[...])
    put(5, cb[...])
    put(6, gg[...])
    for k, term in enumerate((sb, dl, sg)):
        value = term[...]
        for n in range(3):
            part = value.astype(bf16).astype(f32)
            put(7 + 3 * n + k, part)
            value = value - part
    wc_o[0:16, CONV:] = (wc_o[0:16, CONV:].astype(f32) + rows[...]).astype(bf16)
    later_o[:, :DI] = w_in[:, :DI]
    later_o[:, DI : DI + D] = w_out[0:ri, :]
    later_o[:, DI + D :] = w_out[ri:, :]


def pack(w_in, w_out, in_gain, cw, cb, gg, sb, dl, sg, ri, tall):
    return pl.pallas_call(
        functools.partial(pack_kernel, ri),
        out_shape=[jax.ShapeDtypeStruct((tall, CONV + 128), bf16), jax.ShapeDtypeStruct((ri, 2 * DI), bf16)],
        scratch_shapes=[pltpu.VMEM((16, 128), f32)],
        name="pack",
    )(w_in, w_out, in_gain, cw, cb, gg, sb, dl, sg)


def unpack_small(ri, ro, share, first_lane, small, device, onehot, gain, gain_abs, cw, cb, gg, heads_o, skip):
    nd = small.shape[1]
    slot = lax.broadcasted_iota(jnp.int32, (nd, 128), 0).astype(f32)[:, 0:1]
    owner = device[...][:, 0:1]

    def spread(rows, width, total, who):
        lane = lax.broadcasted_iota(jnp.int32, (128, total), 1).astype(f32)
        piece = jnp.floor((lane + 0.5) * (1.0 / width))
        inner = lane - piece * width
        pick = (lax.broadcasted_iota(jnp.int32, (128, total), 0).astype(f32) - first_lane == inner).astype(bf16)
        mine = piece[0:1, :] == who
        out = dot(jnp.concatenate([small[r].astype(bf16) for r in rows], axis=0), pick)
        return [jnp.sum(jnp.where(mine, out[nd * n : nd * n + nd], 0.0), axis=0, keepdims=True) for n in range(len(rows))]

    gain[...] = spread([0], ri, D, slot)[0]
    gain_abs[...] = spread([0], ri, D, owner)[0]
    taps = spread(range(1, 6), CONV // nd, CONV, owner)
    for k in range(4):
        cw[k : k + 1, :] = 0.5 * taps[k]
    cw[4:8, :] = jnp.zeros((4, CONV), f32)
    cb[...] = 0.5 * taps[4]
    gg[...] = spread([6], ro, DI, owner)[0]
    parts = spread(range(7, 16), share, 128, owner)
    per_head = [parts[n] + parts[n + 3] + parts[n + 6] for n in range(3)]
    heads_o[0:1, :] = per_head[0]
    heads_o[1:2, :] = -jnp.exp(per_head[1])
    skip[...] = dot(two_parts(jnp.broadcast_to(per_head[2], (8, 128))), onehot[...])[0:1, :]


def copies_of(pieces, wc, sems):
    rows = pieces[0].shape[0]
    spots = [(n // 2, slice(0, SPLIT) if n % 2 == 0 else slice(SPLIT, CONV + 128)) for n in range(4)]
    return [pltpu.make_async_copy(piece, wc.at[rows * r : rows * r + rows, cols], sems.at[n])
            for n, (piece, (r, cols)) in enumerate(zip(pieces, spots))]


def clear_free(wc, heads):
    last = wc[:, CONV:]
    wc[:, CONV:] = jnp.where(lax.broadcasted_iota(jnp.int32, last.shape, 1) < heads, last, jnp.zeros_like(last))


def forward_scan_kernel(heads, per_seq, ri, ro, share, first, tok, wc_0, wc_1, wc_2, wc_3, small, device, seg, seg_before,
                        cin_o, act_o, dact_o, nrm_o, scan_o, st_o, z_o, gain, gain_abs, cw, cb, gg, heads_o, skip,
                        pbuf, zbuf, nbuf, pnext, znext, nnext, state, docs, onehot, wc, sems):
    i = pl.program_id(0)
    tiles = CONV // 128

    def normed(block):
        x = block[...].astype(f32)
        r = lax.rsqrt(jnp.mean(x * x, axis=-1, keepdims=True) + EPS)
        nnext[...] = (x * r * gain[...]).astype(bf16)

    def project(t):
        part = dot(nnext[...], wc[:, 128 * t : 128 * t + 256])
        pnext[t] = part[:, :128]
        pnext[t + 1] = part[:, 128:]

    def project_step():
        znext[...] = dot(nnext[...], wc[:, CONV:]) + heads_o[0:1, :]

    def advance():
        pbuf[:, 8 : 8 + Q, :] = pnext[...]
        zbuf[...] = znext[...]
        nbuf[...] = nnext[...]

    @pl.when(i == 0)
    def _():
        copies = copies_of((wc_0, wc_1, wc_2, wc_3), wc, sems)
        for copy in copies:
            copy.start()
        onehot[...] = head_onehot(onehot.shape)
        unpack_small(ri, ro, share, heads, small, device, onehot, gain, gain_abs, cw, cb, gg, heads_o, skip)
        normed(first)
        for copy in copies:
            copy.wait()
        clear_free(wc, heads)
        for t in range(0, tiles, 2):
            project(t)
        project_step()
        advance()

    @pl.when(lax.rem(i, per_seq) == 0)
    def _():
        pbuf[:, 0:8, :] = jnp.zeros((tiles, 8, 128), f32)
        state[...] = jnp.zeros_like(state)

    nrm_o[...] = nbuf[...]
    z = zbuf[...]
    z_o[...] = z
    doc_row = seg[0].astype(f32)
    before_row = jnp.where(lax.rem(i, per_seq) == 0, -1.0, seg_before[0].astype(f32))
    doc, masks = documents(doc_row, before_row, docs)
    prev = docs[7:8, :]
    soft, a, b, reach, tail, keep = scan_factors(z, heads_o[1:2, :], doc, prev)
    factors = two_parts(jnp.concatenate([reach, tail, jnp.broadcast_to(keep, (8, 128))], axis=0))
    bt = b.T
    row = lax.broadcasted_iota(jnp.int32, (Q, Q), 0)
    lane = lax.broadcasted_iota(jnp.int32, (Q, Q), 1)
    joined = (row >= lane) & (doc == doc_row)
    low = lane < HD
    zero = jnp.zeros((Q, Q), bf16)

    def conv(t):
        cols = slice(128 * t, 128 * t + 128)
        here = pbuf[t, 8 : 8 + Q, :]
        cin_o[:, cols] = here.astype(bf16)
        half = cb[:, cols] + cw[3:4, cols] * here
        for k in range(3):
            half = half + cw[k : k + 1, cols] * (pbuf[t, 5 + k : 5 + k + Q, :] * masks[k])
        pbuf[t, 0:8, :] = pbuf[t, Q : Q + 8, :]
        up = 1.0 + jnp.tanh(half)
        act = half * up
        dact_o[:, cols] = (up + act * (2.0 - up)).astype(bf16)
        act = act.astype(bf16)
        act_o[:, cols] = act
        return act

    normed(tok)
    bmat = conv(tiles - 2)
    cmat = conv(tiles - 1)
    bt_mat = bmat.astype(f32).T.astype(bf16)
    s = dot_nt(cmat, bmat)
    for p in range(heads // 2):
        cols = slice(128 * p, 128 * p + 128)
        half = slice(128 * (p % 2), 128 * (p % 2) + 128)
        if p % 2 == 0:
            group = slice(128 * p, 128 * p + 256)
            wide = dot(factors, onehot[:, group])
            st_low = state[:, group].astype(bf16)
            st_o[0, :, group] = st_low
            cs = dot(cmat, st_low)
        xp = conv(p)
        if p < tiles // 2:
            project(2 * p)
        if p == tiles // 2:
            project_step()
        parts = []
        for h in (2 * p, 2 * p + 1):
            spread = jnp.broadcast_to(a[:, h : h + 1], (Q, Q)) - bt[h : h + 1, :]
            parts.append((jnp.exp2(jnp.where(joined, spread, NEG)) * s).astype(bf16))
        xbd = jnp.concatenate([jnp.where(low, xp, zero), jnp.where(low, zero, xp)], axis=0)
        y = dot(jnp.concatenate(parts, axis=1), xbd)
        xf = xp.astype(f32)
        y = y + cs[:, half] * wide[0:Q, half] + xf * skip[:, cols]
        scan_o[:, cols] = y.astype(bf16)
        xw = (xf * wide[Q : 2 * Q, half]).astype(bf16)
        state[:, cols] = state[:, cols] * wide[2 * Q : 2 * Q + 1, half] + dot(bt_mat, xw)
    advance()


def forward_scan(tok, wc, small, device, seg, seqs, ri, ro, share, heads):
    rows = tok.shape[0]
    n = rows // Q
    one = pl.Buffered(buffer_count=1)
    full = lambda arr: pl.BlockSpec(arr.shape, lambda i: (0,) * arr.ndim, pipeline_mode=one)
    blk = lambda w: pl.BlockSpec((Q, w), lambda i: (i, 0))
    hbm = pl.BlockSpec(memory_space=pl.ANY)
    low = lambda *shape: jax.ShapeDtypeStruct(shape, bf16)
    sides = [(1, D), (1, D), (8, CONV), (1, CONV), (1, DI), (8, 128), (1, DI)]
    side = lambda shape: pl.BlockSpec(shape, lambda i: (0, 0))
    return pl.pallas_call(
        functools.partial(forward_scan_kernel, heads, n // seqs, ri, ro, share),
        grid=(n,),
        in_specs=[pl.BlockSpec((Q, D), lambda i: (0, 0), pipeline_mode=one),
                  pl.BlockSpec((Q, D), lambda i: (jnp.minimum(i + 1, n - 1), 0)), hbm, hbm, hbm, hbm, full(small), full(device),
                  pl.BlockSpec((1, 1, Q), lambda i: (i, 0, 0)), pl.BlockSpec((1, 1, Q), lambda i: (jnp.maximum(i - 1, 0), 0, 0))],
        out_specs=[blk(CONV), blk(CONV), blk(CONV), blk(D), blk(DI), pl.BlockSpec((1, N, DI), lambda i: (i, 0, 0)), blk(128)]
        + [side(shape) for shape in sides],
        out_shape=[low(rows, CONV), low(rows, CONV), low(rows, CONV), low(rows, D), low(rows, DI), low(n, N, DI),
                   jax.ShapeDtypeStruct((rows, 128), f32)] + [jax.ShapeDtypeStruct(shape, f32) for shape in sides],
        scratch_shapes=[pltpu.VMEM((CONV // 128, Q + 8, 128), f32), pltpu.VMEM((Q, 128), f32), pltpu.VMEM((Q, D), bf16),
                        pltpu.VMEM((CONV // 128, Q, 128), f32), pltpu.VMEM((Q, 128), f32), pltpu.VMEM((Q, D), bf16),
                        pltpu.VMEM((N, DI), f32), pltpu.VMEM((Q + 8, 128), f32), pltpu.VMEM((256, DI), bf16),
                        pltpu.VMEM((D, CONV + 128), bf16), pltpu.SemaphoreType.DMA((4,))],
        compiler_params=pltpu.CompilerParams(vmem_limit_bytes=56 << 20),
        name="forward_scan",
    )(tok, tok, *wc, small, device, seg, seg)


def block_order(ri):
    row = lax.broadcasted_iota(jnp.int32, (192, 192), 0)
    lane = lax.broadcasted_iota(jnp.int32, (192, 192), 1)
    second = lane >= 96
    at = jnp.where(second, lane - 96, lane)
    owner = lax.div(at, ri)
    target = owner * (2 * ri) + (at - owner * ri) + jnp.where(second, ri, 0)
    return (row == target).astype(bf16)


def gate_kernel(ri, tok, scan, cot, later_in, gain, gg, mixed_o, dscan_o, dgate_o, early_o, wo_o, later, wo, early, sems,
                acc_g, acc_o, nb_s, nbt_s, mixt_s, h_s, e_s, gated_s, eg_s):
    i = pl.program_id(0)
    bm, high = 256, 32
    blocks = tok.shape[0] // bm

    wo_copy = pltpu.make_async_copy(wo, wo_o, sems.at[2])

    @pl.when(i == 0)
    def _():
        copies = [pltpu.make_async_copy(later_in.at[:, cols], later.at[:, cols], sems.at[n])
                  for n, cols in enumerate((slice(DI, 2 * DI), slice(0, DI)))]
        for copy in copies:
            copy.start()
        acc_g[...] = jnp.zeros_like(acc_g)
        acc_o[...] = jnp.zeros_like(acc_o)
        copies[0].wait()
        put = block_order(ri)
        for g in range(D // 96):
            at = slice(96 * g, 96 * g + 96)
            halves = jnp.concatenate([later[at, DI : DI + D], later[at, DI + D :]], axis=0)
            wo[192 * g : 192 * g + 192, :] = dot(put, halves).astype(bf16)
        wo_copy.start()
        copies[1].wait()

    x = tok[...].astype(f32)
    r = lax.rsqrt(jnp.mean(x * x, axis=-1, keepdims=True) + EPS)
    nb = (x * r * gain[...]).astype(bf16)
    nb_s[...] = nb * 0.5
    nbt_s[...] = nb.T

    def products(n):
        rows = slice(bm * n, bm * n + bm)
        for c in range(DI // 256):
            cols = slice(256 * c, 256 * c + 256)
            h_s[rows, cols] = dot(nb_s[rows, :], later[:, cols])
            yield
            e_s[rows, cols] = dot_nt(cot[rows, :], wo[cols, :])
            yield

    def sums(n):
        rows = slice(bm * n, bm * n + bm)
        for c in range(DI // 256):
            cols = slice(256 * c, 256 * c + 256)
            mixt_s[cols, :] = mixed_o[rows, cols].T
        for c in range(D // 256):
            cols = slice(256 * c, 256 * c + 256)
            acc_o[:, cols] += dot(mixt_s[...], cot[rows, cols])
            yield
        for c in range(DI // 256):
            cols = slice(256 * c, 256 * c + 256)
            acc_g[:, cols] += dot(nbt_s[:, rows], dgate_o[rows, cols])
            yield

    def elementwise(n, part):
        rows = slice(bm * n + part * high, bm * n + part * high + high)
        squares = jnp.zeros((high, 128), f32)
        cross = jnp.zeros((high, 128), f32)
        for t in range(DI // 128):
            cols = slice(128 * t, 128 * t + 128)
            h = h_s[rows, cols]
            gated = scan[rows, cols].astype(f32) * (h + h * jnp.tanh(h))
            eg = e_s[rows, cols] * gg[:, cols]
            squares = squares + gated * gated
            cross = cross + gated * eg
            gated_s[part, :, cols] = gated
            eg_s[part, :, cols] = eg
        rr = lax.rsqrt(jnp.sum(squares, axis=-1, keepdims=True) * (1.0 / DI) + EPS)
        pull = rr * rr * rr * (jnp.sum(cross, axis=-1, keepdims=True) * (1.0 / DI))
        rr = jnp.broadcast_to(rr, (high, 128))
        pull = jnp.broadcast_to(pull, (high, 128))
        yield
        for t in range(DI // 128):
            cols = slice(128 * t, 128 * t + 128)
            h = h_s[rows, cols]
            th = jnp.tanh(h)
            gated = gated_s[part, :, cols]
            mixed_o[rows, cols] = (gated * rr * gg[:, cols]).astype(bf16)
            dg = eg_s[part, :, cols] * rr - gated * pull
            act = h + h * th
            dscan_o[rows, cols] = (dg * act).astype(bf16)
            dg = dg * scan[rows, cols].astype(f32)
            dgate_o[rows, cols] = (dg * ((1.0 + th) + act * (1.0 - th))).astype(bf16)
        yield

    def both(n, matrix):
        vector = [step for part in range(bm // high) for step in [elementwise(n, part)] * 2]
        for step in vector:
            next(step)
            next(matrix, None)
        for _ in matrix:
            pass

    for _ in products(0):
        pass
    for n in range(blocks):
        both(n, products(n + 1) if n + 1 < blocks else sums(n - 1))
    for _ in sums(blocks - 1):
        pass

    @pl.when(i == pl.num_programs(0) - 1)
    def _():
        put = block_order(ri)
        for g in range(D // 96):
            at = slice(96 * g, 96 * g + 96)
            early[at, :DI] = (0.5 * acc_g[at, :]).astype(bf16)
            halves = dot_tn(put, acc_o[192 * g : 192 * g + 192, :].astype(bf16)).astype(bf16)
            early[at, DI : DI + D] = halves[:96]
            early[at, DI + D :] = halves[96:]
            pltpu.make_async_copy(early.at[at], early_o.at[at], sems.at[3 + g]).start()
        for g in range(D // 96):
            at = slice(96 * g, 96 * g + 96)
            pltpu.make_async_copy(early.at[at], early_o.at[at], sems.at[3 + g]).wait()
        wo_copy.wait()


def gate_pass(tok, scan, cot, later, gain, gg, ri, bm=512):
    rows = tok.shape[0]
    one = pl.Buffered(buffer_count=1)
    full = lambda shape: pl.BlockSpec(shape, lambda i: (0,) * len(shape), pipeline_mode=one)
    blk = lambda w: pl.BlockSpec((bm, w), lambda i: (i, 0))
    hbm = pl.BlockSpec(memory_space=pl.ANY)
    low = lambda *shape: jax.ShapeDtypeStruct(shape, bf16)
    return pl.pallas_call(
        functools.partial(gate_kernel, ri),
        grid=(rows // bm,),
        in_specs=[blk(D), blk(DI), blk(D), hbm, full(gain.shape), full(gg.shape)],
        out_specs=[blk(DI), blk(DI), blk(DI), hbm, hbm],
        out_shape=[low(rows, DI), low(rows, DI), low(rows, DI), low(D, 2 * DI), low(DI, D)],
        scratch_shapes=[pltpu.VMEM((D, 2 * DI), bf16), pltpu.VMEM((DI, D), bf16), pltpu.VMEM((D, 2 * DI), bf16),
                        pltpu.SemaphoreType.DMA((3 + D // 96,)), pltpu.VMEM((D, DI), f32), pltpu.VMEM((DI, D), f32), pltpu.VMEM((bm, D), bf16), pltpu.VMEM((D, bm), bf16),
                        pltpu.VMEM((DI, 256), bf16),
                        pltpu.VMEM((bm, DI), f32), pltpu.VMEM((bm, DI), f32), pltpu.VMEM((8, 32, DI), f32),
                        pltpu.VMEM((8, 32, DI), f32)],
        compiler_params=pltpu.CompilerParams(vmem_limit_bytes=VM),
        name="gate_pass",
    )(tok, scan, cot, later, gain, gg)


def out_kernel(mixed, tok, wo, out_o):
    out_o[...] = (tok[...].astype(f32) + dot(mixed[...], wo[...])).astype(bf16)


def out_pass(mixed, tok, wo, bm=512):
    rows = tok.shape[0]
    blk = lambda w: pl.BlockSpec((bm, w), lambda i: (i, 0))
    return pl.pallas_call(
        out_kernel,
        grid=(rows // bm,),
        in_specs=[blk(DI), blk(D), pl.BlockSpec((DI, D), lambda i: (0, 0), pipeline_mode=pl.Buffered(buffer_count=1))],
        out_specs=blk(D),
        out_shape=jax.ShapeDtypeStruct((rows, D), bf16),
        compiler_params=pltpu.CompilerParams(vmem_limit_bytes=50 << 20),
        cost_estimate=pl.CostEstimate(flops=0, bytes_accessed=0, transcendentals=0),
        name="out_pass",
    )(mixed, tok, wo)


def pack_grads(nf, share, tall, gcw, gcb, gsk, ghd, device, sums, rows, out_o):
    nd = device.shape[0]
    owner = device[...][:, 0:1]
    first_lane = nf * share

    def spread(values, width, who):
        total = values[0].shape[1]
        lane = lax.broadcasted_iota(jnp.int32, (128, total), 1).astype(f32)
        piece = jnp.floor((lane + 0.5) * (1.0 / width))
        place = lax.broadcasted_iota(jnp.int32, (128, total), 0).astype(f32) - first_lane
        pick = ((place == lane - piece * width) & (place < width)).astype(bf16)
        mine = piece[0:1, :] == who
        terms = []
        for value in values:
            hi = value.astype(bf16).astype(f32)
            terms += [jnp.where(mine, part, 0.0).astype(bf16) for part in (hi, value - hi)]
        out = dot_nt(jnp.concatenate(terms, axis=0), pick)
        return [out[nd * k : nd * k + nd] for k in range(len(terms))]

    rows[...] = jnp.zeros_like(rows)

    def put(n, values):
        rows[pl.ds(n, nd, stride=tall), :] = values

    taps = [0.5 * jnp.sum(gcw[8 * k : 8 * k + 8, :], axis=0, keepdims=True) for k in range(4)]
    taps.append(0.5 * jnp.sum(gcb[...], axis=0, keepdims=True))
    for k, part in enumerate(spread(taps, CONV // nd, owner)):
        put(k // 2 + 5 * (k % 2), part)
    group = owner - nf * jnp.floor((owner + 0.5) * (1.0 / nf))
    skips = two_parts(jnp.broadcast_to(jnp.sum(gsk[...], axis=0, keepdims=True), (8, DI)))
    skips = dot(skips[:, :DI], sums[...]) + dot(skips[:, DI:], sums[...])
    per_head = [jnp.sum(ghd[0:8, :], axis=0, keepdims=True), jnp.sum(ghd[8:16, :], axis=0, keepdims=True), skips[0:1, :]]
    for k, part in enumerate(spread(per_head, share, group)):
        put(10 + k // 2 + 3 * (k % 2), part)
    out_o[...] = rows[...].astype(bf16)


def backward_scan_kernel(heads, per_seq, nf, share, tall, dscan, cin, act, dact, z_r, st, cw, head_terms, skip, seg, seg_before,
                         wc_0, wc_1, wc_2, wc_3, device, dproj_o, gproj_o, pack_o, gproj,
                         dstate, p1buf, qbuf, xwbuf, rowbuf, lastbuf, mbuf, onehot, sums, docs,
                         gcw_o, gcb_o, gsk_o, ghd_o, rows_s, wc, dlast, sems):
    i = pl.program_id(0)
    steps = pl.num_programs(0)

    @pl.when(i == 0)
    def _():
        copies = copies_of((wc_0, wc_1, wc_2, wc_3), wc, sems)
        for copy in copies:
            copy.start()
        dlast[...] = jnp.zeros_like(dlast)
        gcw_o[...] = jnp.zeros_like(gcw_o)
        gcb_o[...] = jnp.zeros_like(gcb_o)
        gsk_o[...] = jnp.zeros_like(gsk_o)
        ghd_o[...] = jnp.zeros_like(ghd_o)
        rowbuf[...] = jnp.zeros_like(rowbuf)
        lastbuf[...] = jnp.zeros_like(lastbuf)
        onehot[...] = head_onehot(onehot.shape)
        head = lax.broadcasted_iota(jnp.int32, sums.shape, 0) >> 6
        sums[...] = (head == lax.broadcasted_iota(jnp.int32, sums.shape, 1)).astype(bf16)
        for copy in copies:
            copy.wait()
        clear_free(wc, heads)

    @pl.when(lax.rem(i, per_seq) == 0)
    def _():
        mbuf[:, :, Q : Q + 8, :] = jnp.zeros((3, CONV // 128, 8, 128), f32)
        dstate[...] = jnp.zeros_like(dstate)

    z = z_r[...]
    rate = head_terms[1:2, :]
    doc_row = seg[0].astype(f32)
    before_row = jnp.where(lax.rem(i, per_seq) == per_seq - 1, -1.0, seg_before[0].astype(f32))
    doc, masks = documents(doc_row, before_row, docs)
    prev = docs[7:8, :]
    soft, a, b, reach, tail, keep = scan_factors(z, rate, doc, prev)
    factors = two_parts(jnp.concatenate([reach, tail, jnp.broadcast_to(keep, (8, 128))], axis=0))
    at = a.T
    row = lax.broadcasted_iota(jnp.int32, (Q, Q), 0)
    lane = lax.broadcasted_iota(jnp.int32, (Q, Q), 1)
    joined = (lane >= row) & (doc == doc_row)
    low = lane < HD
    bmat = act[:, DI : DI + N]
    cmat = act[:, DI + N :]
    ct_mat = cmat.astype(f32).T.astype(bf16)
    s = dot_nt(bmat, cmat)
    ds_low = dstate[...].astype(bf16)
    zero = jnp.zeros((Q, Q), bf16)
    dst = jnp.zeros((Q, Q), f32)

    def conv_back(t, grad):
        cols = slice(128 * t, 128 * t + 128)
        dpre = grad * dact[:, cols].astype(f32)
        for k in range(3):
            mbuf[k, t, 0:Q, :] = dpre * masks[k]
        cv = cin[:, cols].astype(f32)
        dcin = cw[3:4, cols] * dpre
        gcb_o[:, cols] += jnp.sum(dpre.reshape(-1, 8, 128), axis=0)
        gcw_o[24:32, cols] += jnp.sum((cv * dpre).reshape(-1, 8, 128), axis=0)
        for k in range(3):
            moved = mbuf[k, t, 3 - k : 3 - k + Q, :]
            dcin = dcin + cw[k : k + 1, cols] * moved
            gcw_o[8 * k : 8 * k + 8, cols] += jnp.sum((cv * moved).reshape(-1, 8, 128), axis=0)
        dproj_o[:, cols] = dcin.astype(bf16)
        mbuf[:, t, Q : Q + 8, :] = mbuf[:, t, 0:8, :]

    def project_back(given, block, part):
        cols = slice(256 * part, 256 * part + 256)
        gproj[pl.ds(block * Q, Q), cols] = dot_nt(given[...], wc[cols, :]).astype(bf16)

    block_before = steps - jnp.maximum(i, 1)
    for p in range(heads // 2):
        cols = slice(128 * p, 128 * p + 128)
        half = slice(128 * (p % 2), 128 * (p % 2) + 128)
        if p % 2 == 0:
            group = slice(128 * p, 128 * p + 256)
            wide = dot(factors, onehot[:, group])
            cs = dot(cmat, st[0, :, group])
            bd = dot(bmat, ds_low[:, group])
        if p % 4 == 1:
            project_back(dlast, block_before, p // 4)
        xp = act[:, cols]
        dy = dscan[:, cols]
        dybd = jnp.concatenate([jnp.where(low, dy, zero), jnp.where(low, zero, dy)], axis=0)
        dm = dot_nt(xp, dybd)
        parts = []
        for n, h in enumerate((2 * p, 2 * p + 1)):
            spread = at[h : h + 1, :] - jnp.broadcast_to(b[:, h : h + 1], (Q, Q))
            e = jnp.exp2(jnp.where(joined, spread, NEG))
            m = (e * s).astype(bf16)
            parts.append(m)
            dmh = dm[:, 128 * n : 128 * n + 128]
            dst = dst + dmh * e
            rowbuf[h : h + 1, :] = jnp.sum(dmh * m.astype(f32), axis=0, keepdims=True)
        xf = xp.astype(f32)
        dyf = dy.astype(f32)
        tail_p = wide[Q : 2 * Q, half]
        fresh = bd[:, half] * tail_p
        dx = dot(jnp.concatenate(parts, axis=1), dybd) + fresh
        p1 = xf * dx
        hi = p1.astype(bf16)
        p1buf[:, cols] = hi
        p1buf[:, DI + 128 * p : DI + 128 * p + 128] = (p1 - hi.astype(f32)).astype(bf16)
        dyr = dyf * wide[0:Q, half]
        qbuf[:, cols] = (dyr * cs[:, half]).astype(bf16)
        dyr = dyr.astype(bf16)
        ds = dstate[:, cols]
        lastbuf[0:1, cols] = jnp.sum(xf * fresh, axis=0, keepdims=True) + wide[2 * Q : 2 * Q + 1, half] * jnp.sum(
            ds * st[0, :, cols].astype(f32), axis=0, keepdims=True)
        gsk_o[:, cols] += jnp.sum((dyf * xf).reshape(-1, 8, 128), axis=0)
        xwbuf[:, cols] = (xf * tail_p).astype(bf16)
        xwbuf[:, DI + 128 * p : DI + 128 * p + 128] = dyr
        dstate[:, cols] = ds * wide[2 * Q : 2 * Q + 1, half] + dot(ct_mat, dyr)
        conv_back(p, dx + skip[:, cols] * dyf)
    dst_low = dst.astype(bf16)
    conv_back(DI // 128, dot(dst_low, cmat) + dot_nt(xwbuf[:, :DI], ds_low))
    conv_back(DI // 128 + 1, dot_tn(dst_low, bmat) + dot_nt(xwbuf[:, DI:], st[0]))
    hot = sums[...]
    p1 = dot(p1buf[:, :DI], hot) + dot(p1buf[:, DI:], hot)
    last = two_parts(lastbuf[...])
    last = (dot(last[:, :DI], hot) + dot(last[:, DI:], hot))[0:1, :]
    da = dot(qbuf[...], hot) - p1 + rowbuf[...].T
    g = cumsum_rows(da, reverse=True) + last
    sig = sigmoid(z)
    ratio = jnp.where(z < -15.0, 1.0, sig / jnp.where(z < -15.0, 1.0, soft))
    dz = g * rate * sig + p1 * ratio
    dproj_o[:, CONV:] = dz.astype(bf16)
    ghd_o[0:8, :] += jnp.sum(dz.reshape(-1, 8, 128), axis=0)
    ghd_o[8:16, :] += rate * jnp.sum((g * soft).reshape(-1, 8, 128), axis=0)
    dlast[...] = dproj_o[...]

    def copy_out(block):
        at = pl.ds(block * Q, Q)
        return pltpu.make_async_copy(gproj.at[at], gproj_o.at[at], sems.at[4])

    @pl.when(i > 0)
    def _():
        copy_out(block_before).start()

    @pl.when(i == steps - 1)
    def _():
        for part in range(D // 256):
            project_back(dlast, 0, part)
        copy_out(0).start()
        pack_grads(nf, share, tall, gcw_o, gcb_o, gsk_o, ghd_o, device, sums, rows_s, pack_o)
        pltpu.make_async_copy(gproj, gproj_o, sems.at[4]).wait()


def backward_scan(dscan, cin, act, dact, z, st, cw, head_terms, skip, seg, wc, device, heads, seqs, nf, share, tall):
    rows = dscan.shape[0]
    n = rows // Q
    nd = device.shape[0]
    one = pl.Buffered(buffer_count=1)
    full = lambda shape: pl.BlockSpec(shape, lambda i: (0,) * len(shape), pipeline_mode=one)
    blk = lambda w: pl.BlockSpec((Q, w), lambda i: (n - 1 - i, 0))
    blk3 = lambda s1, s2: pl.BlockSpec((1, s1, s2), lambda i: (n - 1 - i, 0, 0))
    hbm = pl.BlockSpec(memory_space=pl.ANY)
    return pl.pallas_call(
        functools.partial(backward_scan_kernel, heads, n // seqs, nf, share, tall),
        grid=(n,),
        in_specs=[blk(DI), blk(CONV), blk(CONV), blk(CONV), blk(128), blk3(N, DI), full(cw.shape), full(head_terms.shape),
                  full(skip.shape), blk3(1, Q), pl.BlockSpec((1, 1, Q), lambda i: (jnp.maximum(n - 2 - i, 0), 0, 0)),
                  hbm, hbm, hbm, hbm, full(device.shape)],
        out_specs=[blk(CONV + 128), hbm, full((nd * tall, 128))],
        out_shape=[jax.ShapeDtypeStruct((rows, CONV + 128), bf16), jax.ShapeDtypeStruct((rows, D), bf16),
                   jax.ShapeDtypeStruct((nd * tall, 128), bf16)],
        scratch_shapes=[pltpu.VMEM((rows, D), bf16), pltpu.VMEM((N, DI), f32), pltpu.VMEM((Q, 2 * DI), bf16), pltpu.VMEM((Q, DI), bf16),
                        pltpu.VMEM((Q, 2 * DI), bf16), pltpu.VMEM((128, 128), f32), pltpu.VMEM((8, DI), f32),
                        pltpu.VMEM((3, CONV // 128, Q + 8, 128), f32), pltpu.VMEM((256, DI), bf16),
                        pltpu.VMEM((DI, 128), bf16), pltpu.VMEM((Q + 8, 128), f32), pltpu.VMEM((32, CONV), f32),
                        pltpu.VMEM((8, CONV), f32), pltpu.VMEM((8, DI), f32), pltpu.VMEM((16, 128), f32),
                        pltpu.VMEM((nd * tall, 128), f32), pltpu.VMEM((D, CONV + 128), bf16), pltpu.VMEM((Q, CONV + 128), bf16),
                        pltpu.SemaphoreType.DMA((5,))],
        compiler_params=pltpu.CompilerParams(vmem_limit_bytes=52 << 20),
        cost_estimate=pl.CostEstimate(flops=0, bytes_accessed=0, transcendentals=0),
        name="backward_scan",
    )(dscan, cin, act, dact, z, st, cw, head_terms, skip, seg, seg, *wc, device)


def norm_back_kernel(ri, gproj, dgate, tok, cot, wg_abs, gain, device, out_o, wg, order):
    @pl.when(pl.program_id(0) == 0)
    def _():
        column = lax.broadcasted_iota(jnp.int32, (8, D), 1).astype(f32)
        slot = jnp.floor((column + 0.5) * (1.0 / ri))
        nd = device.shape[0]
        mine = lax.broadcasted_iota(jnp.int32, (nd, D), 0).astype(f32) == slot[0:1, :]
        feature = jnp.sum(jnp.where(mine, device[...][:, 0:1], 0.0), axis=0, keepdims=True) * ri + (column - slot * ri)[0:1, :]
        order[...] = (lax.broadcasted_iota(jnp.int32, (D, D), 0).astype(f32) == feature).astype(bf16)
        wg[...] = (0.5 * dot_tn(order[...], wg_abs[...])).astype(bf16)

    grad = dot_nt(dgate[...], wg[...]) + gproj[...].astype(f32)
    x = tok[...].astype(f32)
    r = lax.rsqrt(jnp.mean(x * x, axis=-1, keepdims=True) + EPS)
    unit = x * r
    e = gain[...] * grad
    back = r * (e - unit * jnp.mean(unit * e, axis=-1, keepdims=True))
    res = (cot[...].astype(f32) + back).astype(bf16)
    out_o[...] = dot_nt(res, order[...]).astype(bf16)


def norm_back(gproj, dgate, tok, cot, later, gain, device, ri, bm=512):
    rows = gproj.shape[0]
    one = pl.Buffered(buffer_count=1)
    full = lambda shape: pl.BlockSpec(shape, lambda i: (0,) * len(shape), pipeline_mode=one)
    blk = lambda w: pl.BlockSpec((bm, w), lambda i: (i, 0))
    return pl.pallas_call(
        functools.partial(norm_back_kernel, ri),
        grid=(rows // bm,),
        in_specs=[blk(D), blk(DI), blk(D), blk(D), full((D, DI)), full(gain.shape), full(device.shape)],
        out_specs=blk(D),
        out_shape=jax.ShapeDtypeStruct((rows, D), bf16),
        scratch_shapes=[pltpu.VMEM((D, DI), bf16), pltpu.VMEM((D, D), bf16)],
        compiler_params=pltpu.CompilerParams(vmem_limit_bytes=46 << 20),
        cost_estimate=pl.CostEstimate(flops=0, bytes_accessed=0, transcendentals=0),
        name="norm_back",
    )(gproj, dgate, tok, cot, later, gain, device)


def conv_weight_kernel(nrm, dproj, small, a_o, b_o):
    grad = lax.dot_general(dproj[...], nrm[...], (((0,), (0,)), ((), ())), preferred_element_type=f32)
    half = a_o.shape[0]
    out = grad.astype(bf16).T
    a_o[...] = out[:half]
    b_o[...] = out[half:]

    @pl.when(pl.program_id(0) == pl.num_programs(0) - 1)
    def _():
        last = slice(a_o.shape[1] - 128, a_o.shape[1])
        out = (grad[a_o.shape[1] - 128 :].T + small[...].astype(f32)).astype(bf16)
        a_o[:, last] = out[:half]
        b_o[:, last] = out[half:]


def conv_weight_grad(nrm, dproj, small, bn=640):
    rows = nrm.shape[0]
    one = pl.Buffered(buffer_count=1)
    return pl.pallas_call(
        conv_weight_kernel,
        grid=((CONV + 128) // bn,),
        in_specs=[pl.BlockSpec((rows, D), lambda i: (0, 0), pipeline_mode=one), pl.BlockSpec((rows, bn), lambda i: (0, i)),
                  pl.BlockSpec((D, 128), lambda i: (0, 0), pipeline_mode=one)],
        out_specs=[pl.BlockSpec((D // 2, bn), lambda i: (0, i))] * 2,
        out_shape=[jax.ShapeDtypeStruct((D // 2, CONV + 128), bf16)] * 2,
        compiler_params=pltpu.CompilerParams(vmem_limit_bytes=50 << 20),
        cost_estimate=pl.CostEstimate(flops=0, bytes_accessed=0, transcendentals=0),
        name="conv_weight_grad",
    )(nrm, dproj, small)


def finish_kernel(heads, share, parts, early, w_in, w_out, in_gain, gate_gain, *refs):
    own, got = refs[0], refs[1:parts]
    in_o, out_o, in_gain_o, gate_gain_o, cw_o, cb_o, sb_o, dl_o, sg_o, total = refs[parts:]
    ri, ro, cc = w_in.shape[0], w_out.shape[0], cb_o.shape[1]
    value = own[...]
    for part in got:
        value = value + part[...].astype(f32)
    total[...] = value
    in_o[:, :DI] = early[:, :DI].astype(f32)
    in_o[:, DI:] = total[0:ri, : CONV + heads]
    out_o[0:ri, :] = early[:, DI : DI + D].astype(f32)
    out_o[ri:, :] = early[:, DI + D :].astype(f32)

    def across(column, count):
        spot = lax.broadcasted_iota(jnp.int32, (count, count), 0) == lax.broadcasted_iota(jnp.int32, (count, count), 1)
        return jnp.sum(jnp.where(spot, column, 0.0), axis=0, keepdims=True)

    in_gain_o[...] = across(jnp.sum(w_in[...].astype(f32) * in_o[...], axis=-1, keepdims=True), ri) / in_gain[...].astype(f32)
    gate_gain_o[...] = across(jnp.sum(w_out[...].astype(f32) * out_o[...], axis=-1, keepdims=True), ro) / gate_gain[...].astype(f32)
    at = CONV + heads
    cw_o[...] = total[0:4, at : at + cc] + total[5:9, at : at + cc]
    cb_o[...] = total[4:5, at : at + cc] + total[9:10, at : at + cc]
    for k, term in enumerate((sb_o, dl_o, sg_o)):
        term[...] = total[10 + k : 11 + k, at : at + share] + total[13 + k : 14 + k, at : at + share]


def finish(early, w_in, w_out, in_gain, gate_gain, own, got, heads, share, cc):
    ri, ro = w_in.shape[0], w_out.shape[0]
    shapes = [(ri, w_in.shape[1]), (ro, D), (1, ri), (1, ro), (4, cc), (1, cc)] + [(1, share)] * 3
    return pl.pallas_call(
        functools.partial(finish_kernel, heads, share, 1 + len(got)),
        out_shape=[jax.ShapeDtypeStruct(shape, f32) for shape in shapes],
        scratch_shapes=[pltpu.VMEM(own.shape, f32)],
        compiler_params=pltpu.CompilerParams(vmem_limit_bytes=12 << 20),
        name="finish",
    )(early, w_in, w_out, in_gain, gate_gain, own, *got)


def stages_of(mesh):
    ndp, nf = mesh.shape["dp"], mesh.shape["fsdp"]
    out = []
    stride = 1
    while stride < nf:
        group = 2 if stride == 1 else min(4, nf // stride)
        out.append(("fsdp", stride, group, stride))
        stride *= group
    stride = 1
    while stride < ndp:
        group = min(4, ndp // stride)
        out.append(("dp", stride, group, stride * nf))
        stride *= group
    return out[::-1]


def pairs_of(stages):
    out = []
    for axis, stride, group, number in stages[::-1]:
        step = 1
        while step < group:
            out.append((axis, stride * step, 2, number * step))
            step *= 2
    return out


def slot_devices(stages):
    rel = np.zeros((1,), np.int32)
    for _, _, group, number in stages:
        rel = (np.arange(group, dtype=np.int32)[:, None] * number + rel[None, :]).reshape(-1)
    return jnp.asarray(rel)


def swap(arr, axis, size, offset):
    return lax.ppermute(arr, axis, [(i, i ^ offset) for i in range(size)])


def gather_stage(block, stage, sizes, first=0):
    axis, stride, group, _ = stage
    if first == 0 or group != 4:
        return jnp.stack([block] + [swap(block, axis, sizes[axis], k * stride) for k in range(1, group)])
    if first == 1:
        block = jnp.stack([block, swap(block, axis, sizes[axis], stride)])
        return jnp.concatenate([block, swap(block, axis, sizes[axis], 2 * stride)])
    block = jnp.stack([block, swap(block, axis, sizes[axis], 2 * stride)])
    block = jnp.stack([block, swap(block, axis, sizes[axis], stride)], axis=1)
    return block.reshape((4,) + block.shape[2:])


def scatter_parts(kept, stage, sizes):
    axis, stride, group, _ = stage
    return [swap(kept[k].astype(bf16), axis, sizes[axis], k * stride) for k in range(1, group)]


def scatter_stage(kept, stage, sizes):
    total = kept[0]
    for part in scatter_parts(kept, stage, sizes):
        total = total + part.astype(f32)
    return total


def before(value, *others):
    return lax.optimization_barrier((value,) + others)


def local(mesh, tokens, cotangent, segments, in_gain, weight_in, conv_weight, conv_bias, step_bias, decay_log, skip_gain,
          gate_gain, weight_out):
    sizes = {"dp": mesh.shape["dp"], "fsdp": mesh.shape["fsdp"]}
    nf = sizes["fsdp"]
    nd = sizes["dp"] * nf
    axes = ("dp", "fsdp")
    stages = stages_of(mesh)
    me = lax.axis_index("dp") * nf + lax.axis_index("fsdp")
    seqs, length, _ = tokens.shape
    rows = seqs * length
    ri, ro, cc, share = weight_in.shape[0], weight_out.shape[0], conv_bias.shape[0], step_bias.shape[0]
    heads = share * nf

    device = slot_devices(stages) ^ me
    feature = (device[:, None] * ri + jnp.arange(ri)[None, :]).reshape(-1)
    order = (jnp.arange(D)[:, None] == feature[None, :]).astype(bf16)

    tall = max(ri, 16)
    wc, later = pack(weight_in, weight_out, in_gain[None], conv_weight, conv_bias[None], gate_gain[None],
                     step_bias[None], decay_log[None], skip_gain[None], ri, tall)
    later = lax.all_gather(later, axes, axis=0, tiled=True)
    tok = tokens.reshape(rows, D)
    up = cotangent.reshape(rows, D)
    wc = gather_stage(wc, stages[0], sizes)
    tok_s = jnp.dot(tok, order, preferred_element_type=bf16)
    device_rows = jnp.broadcast_to(device.astype(f32)[:, None], (nd, 128))
    seg = segments.reshape(rows // Q, 1, Q)
    wc, tok_s, device_rows, seg = before(wc, tok_s, device_rows, seg)
    one, two = wc[..., :SPLIT], wc[..., SPLIT:]
    for stage in stages[1:-1]:
        one = gather_stage(one, stage, sizes, 1)
        two = gather_stage(two, stage, sizes, 2)
    up_s = jnp.dot(up, order, preferred_element_type=bf16)
    two, up_s = before(two, up_s)
    axis, stride = stages[-1][:2]
    quarters = [part.reshape(nd // 2, tall, part.shape[-1])
                for part in (one, two, swap(one, axis, sizes[axis], stride), swap(two, axis, sizes[axis], stride))]
    last = [part[:, :16, CONV - SPLIT :] for part in (quarters[1], quarters[3])]
    small = jnp.concatenate(last, axis=0).transpose(1, 0, 2).astype(f32)
    wc = [part[:, :ri].reshape(D // 2, part.shape[-1]) for part in quarters]

    cin, act, dact, nrm, scan, st, z, gain, gain_abs, cw, cb, gg, head_terms, skip = forward_scan(
        tok_s, wc, small, device_rows, seg, seqs, ri, ro, share, heads)
    mixed, dscan, dgate, early, wo = gate_pass(tok, scan, up, later, gain_abs, gg, ri)
    early = lax.psum_scatter(early, axes, scatter_dimension=0, tiled=True)

    dproj, gproj, small = backward_scan(
        dscan, cin, act, dact, z, st, cw, head_terms, skip, seg, wc, device_rows, heads, seqs, nf, share, tall)
    if ri == tall:
        halves = conv_weight_grad(nrm, dproj, small)
        halves = [half.reshape(nd // 2, tall, CONV + 128) for half in halves]
    else:
        halves = conv_weight_grad(nrm, dproj, jnp.zeros((D, 128), bf16))
        halves = [jnp.pad(half.reshape(nd // 2, ri, CONV + 128), ((0, 0), (0, tall - ri), (0, 0))) for half in halves]
        small = jnp.pad(small.reshape(nd, tall, 128), ((0, 0), (0, 0), (CONV, 0)))
        halves = [half + part for half, part in zip(halves, (small[: nd // 2], small[nd // 2 :]))]

    axis, stride, group, _ = stages[-1]
    got = swap(halves[1], axis, sizes[axis], stride)
    shape = [g for _, _, g, _ in stages[-2::-1]] + [tall, CONV + 128]
    pieces = zip(halves[0].reshape(shape), got.reshape(shape))
    total = [mine.astype(f32) + part.astype(f32) for mine, part in pieces]
    total[0], gain = before(total[0], gain)
    gtok = norm_back(gproj, dgate, tok_s, up_s, later, gain, device_rows, ri)
    for stage in stages[-2:0:-1]:
        total = scatter_stage(total, stage, sizes)
    total, gtok, wo = before(total, gtok, wo)
    got = scatter_parts(total, stages[0], sizes)
    out = out_pass(mixed, tok, wo)
    early, out = before(early, out)
    g_in, g_out, g_in_gain, g_gate_gain, g_cw, g_cb, g_sb, g_dl, g_sg = finish(
        early, weight_in, weight_out, in_gain[None], gate_gain[None], total[0], got, heads, share, cc)
    return (out.reshape(tokens.shape), gtok.reshape(tokens.shape), g_in_gain[0], g_in, g_cw, g_cb[0],
            g_sb[0], g_dl[0], g_sg[0], g_gate_gain[0], g_out)


def solution(mesh):
    every = ("dp", "fsdp")
    return jax.shard_map(
        functools.partial(local, mesh),
        mesh=mesh,
        in_specs=(P(every, None, None), P(every, None, None), P(every, None), P(every), P(every, None), P(None, every),
                  P(every), P("fsdp"), P("fsdp"), P("fsdp"), P(every), P(every, None)),
        out_specs=(P(every, None, None), P(every, None, None), P(every), P(every, None), P(None, every), P(every),
                   P("fsdp"), P("fsdp"), P("fsdp"), P(every), P(every, None)),
        check_vma=False,
    )
```

```python
import functools

import jax
import jax.numpy as jnp
import numpy as np
from jax import lax
from jax.experimental import pallas as pl
from jax.experimental.pallas import tpu as pltpu
from jax.sharding import PartitionSpec as P

EPS = 1e-05
LOG2E = 1.4426950408889634
NEG = -1e30
f32, bf16 = jnp.float32, jnp.bfloat16
Q = 128
VM = 60 * 1024 * 1024

D, DI, CONV, N, HD = 768, 1536, 1792, 128, 64
SPLIT = 1024


def dot(a, b):
    return lax.dot_general(a, b, (((1,), (0,)), ((), ())), preferred_element_type=f32)


def dot_nt(a, b):
    return lax.dot_general(a, b, (((1,), (1,)), ((), ())), preferred_element_type=f32)


def dot_tn(a, b):
    return lax.dot_general(a, b, (((0,), (0,)), ((), ())), preferred_element_type=f32)


def sigmoid(v):
    return 1.0 / (1.0 + jnp.exp(-v))


def cumsum_rows(v, reverse=False):
    rows = lax.broadcasted_iota(jnp.int32, v.shape, 0)
    count = v.shape[0]
    shift = 1
    while shift < count:
        if reverse:
            moved = pltpu.roll(v, count - shift, 0)
            v = v + jnp.where(rows < count - shift, moved, 0.0)
        else:
            moved = pltpu.roll(v, shift, 0)
            v = v + jnp.where(rows >= shift, moved, 0.0)
        shift *= 2
    return v


def step_terms(z):
    e = jnp.exp(-jnp.abs(z))
    soft = jnp.maximum(z, 0.0) + jnp.log1p(e)
    tiny = z < -15.0
    log_soft = jnp.where(tiny, z, jnp.log(jnp.where(tiny, 1.0, soft)))
    return soft, log_soft


def columns(row):
    return jnp.broadcast_to(row, (Q, 128)).T


def documents(row, before_row, docs):
    doc = columns(row)
    docs[0:8, :] = columns(before_row)[Q - 8 : Q, :]
    docs[8 : 8 + Q, :] = doc
    return doc, [(docs[8 - s : 8 - s + Q, :] == doc).astype(f32) for s in (3, 2, 1)]


def scan_factors(z, rate, doc, prev_doc):
    soft, log_soft = step_terms(z)
    a = cumsum_rows(soft * (rate * LOG2E))
    b = a - log_soft * LOG2E
    last = a[Q - 1 : Q, :]
    last_doc = doc[Q - 1 : Q, :]
    reach = jnp.where(doc == prev_doc, jnp.exp2(a), 0.0)
    tail = jnp.where(doc == last_doc, jnp.exp2(last - b), 0.0)
    keep = jnp.where(last_doc == prev_doc, jnp.exp2(last), 0.0)
    return soft, a, b, reach, tail, keep


def pair_of(cols, p, low):
    left = jnp.broadcast_to(cols[:, 2 * p : 2 * p + 1], low.shape)
    right = jnp.broadcast_to(cols[:, 2 * p + 1 : 2 * p + 2], low.shape)
    return jnp.where(low, left, right)


def two_parts(cols):
    hi = cols.astype(bf16)
    return jnp.concatenate([hi, (cols - hi.astype(f32)).astype(bf16)], axis=1)


def head_onehot(shape):
    head = lax.broadcasted_iota(jnp.int32, shape, 1) >> 6
    return (lax.broadcasted_iota(jnp.int32, shape, 0) & 127 == head).astype(bf16)


def pack_kernel(ri, w_in, w_out, in_gain, cw, cb, gg, sb, dl, sg, wc_o, later_o, rows):
    wc_o[...] = jnp.zeros_like(wc_o)
    wc_o[0:ri, : w_in.shape[1] - DI] = w_in[:, DI:]
    rows[...] = jnp.zeros_like(rows)
    at = w_in.shape[1] - DI - CONV

    def put(n, value):
        rows[n : n + value.shape[0], at : at + value.shape[1]] = value.astype(f32)

    put(0, in_gain[...])
    put(1, cw[...])
    put(5, cb[...])
    put(6, gg[...])
    for k, term in enumerate((sb, dl, sg)):
        value = term[...]
        for n in range(3):
            part = value.astype(bf16).astype(f32)
            put(7 + 3 * n + k, part)
            value = value - part
    wc_o[0:16, CONV:] = (wc_o[0:16, CONV:].astype(f32) + rows[...]).astype(bf16)
    later_o[:, :DI] = w_in[:, :DI]
    later_o[:, DI : DI + D] = w_out[0:ri, :]
    later_o[:, DI + D :] = w_out[ri:, :]


def pack(w_in, w_out, in_gain, cw, cb, gg, sb, dl, sg, ri, tall):
    return pl.pallas_call(
        functools.partial(pack_kernel, ri),
        out_shape=[jax.ShapeDtypeStruct((tall, CONV + 128), bf16), jax.ShapeDtypeStruct((ri, 2 * DI), bf16)],
        scratch_shapes=[pltpu.VMEM((16, 128), f32)],
        name="pack",
    )(w_in, w_out, in_gain, cw, cb, gg, sb, dl, sg)


def unpack_small(ri, ro, share, first_lane, small, device, onehot, gain, gain_abs, cw, cb, gg, heads_o, skip):
    nd = small.shape[1]
    slot = lax.broadcasted_iota(jnp.int32, (nd, 128), 0).astype(f32)[:, 0:1]
    owner = device[...][:, 0:1]

    def spread(rows, width, total, who):
        lane = lax.broadcasted_iota(jnp.int32, (128, total), 1).astype(f32)
        piece = jnp.floor((lane + 0.5) * (1.0 / width))
        inner = lane - piece * width
        pick = (lax.broadcasted_iota(jnp.int32, (128, total), 0).astype(f32) - first_lane == inner).astype(bf16)
        mine = piece[0:1, :] == who
        out = dot(jnp.concatenate([small[r].astype(bf16) for r in rows], axis=0), pick)
        return [jnp.sum(jnp.where(mine, out[nd * n : nd * n + nd], 0.0), axis=0, keepdims=True) for n in range(len(rows))]

    gain[...] = spread([0], ri, D, slot)[0]
    gain_abs[...] = spread([0], ri, D, owner)[0]
    taps = spread(range(1, 6), CONV // nd, CONV, owner)
    for k in range(4):
        cw[k : k + 1, :] = 0.5 * taps[k]
    cw[4:8, :] = jnp.zeros((4, CONV), f32)
    cb[...] = 0.5 * taps[4]
    gg[...] = spread([6], ro, DI, owner)[0]
    parts = spread(range(7, 16), share, 128, owner)
    per_head = [parts[n] + parts[n + 3] + parts[n + 6] for n in range(3)]
    heads_o[0:1, :] = per_head[0]
    heads_o[1:2, :] = -jnp.exp(per_head[1])
    skip[...] = dot(two_parts(jnp.broadcast_to(per_head[2], (8, 128))), onehot[...])[0:1, :]


def copies_of(pieces, wc, sems):
    rows = pieces[0].shape[0]
    spots = [(n // 2, slice(0, SPLIT) if n % 2 == 0 else slice(SPLIT, CONV + 128)) for n in range(4)]
    return [pltpu.make_async_copy(piece, wc.at[rows * r : rows * r + rows, cols], sems.at[n])
            for n, (piece, (r, cols)) in enumerate(zip(pieces, spots))]


def clear_free(wc, heads):
    last = wc[:, CONV:]
    wc[:, CONV:] = jnp.where(lax.broadcasted_iota(jnp.int32, last.shape, 1) < heads, last, jnp.zeros_like(last))


def forward_scan_kernel(heads, per_seq, ri, ro, share, first, tok, wc_0, wc_1, wc_2, wc_3, small, device, seg, seg_before,
                        cin_o, act_o, dact_o, nrm_o, scan_o, st_o, z_o, gain, gain_abs, cw, cb, gg, heads_o, skip,
                        pbuf, zbuf, nbuf, pnext, znext, nnext, state, docs, onehot, wc, sems):
    i = pl.program_id(0)
    tiles = CONV // 128

    def normed(block):
        x = block[...].astype(f32)
        r = lax.rsqrt(jnp.mean(x * x, axis=-1, keepdims=True) + EPS)
        nnext[...] = (x * r * gain[...]).astype(bf16)

    def project(t):
        part = dot(nnext[...], wc[:, 128 * t : 128 * t + 256])
        pnext[t] = part[:, :128]
        pnext[t + 1] = part[:, 128:]

    def project_step():
        znext[...] = dot(nnext[...], wc[:, CONV:]) + heads_o[0:1, :]

    def advance():
        pbuf[:, 8 : 8 + Q, :] = pnext[...]
        zbuf[...] = znext[...]
        nbuf[...] = nnext[...]

    @pl.when(i == 0)
    def _():
        copies = copies_of((wc_0, wc_1, wc_2, wc_3), wc, sems)
        for copy in copies:
            copy.start()
        onehot[...] = head_onehot(onehot.shape)
        unpack_small(ri, ro, share, heads, small, device, onehot, gain, gain_abs, cw, cb, gg, heads_o, skip)
        normed(first)
        for copy in copies:
            copy.wait()
        clear_free(wc, heads)
        for t in range(0, tiles, 2):
            project(t)
        project_step()
        advance()

    @pl.when(lax.rem(i, per_seq) == 0)
    def _():
        pbuf[:, 0:8, :] = jnp.zeros((tiles, 8, 128), f32)
        state[...] = jnp.zeros_like(state)

    nrm_o[...] = nbuf[...]
    z = zbuf[...]
    z_o[...] = z
    doc_row = seg[0].astype(f32)
    before_row = jnp.where(lax.rem(i, per_seq) == 0, -1.0, seg_before[0].astype(f32))
    doc, masks = documents(doc_row, before_row, docs)
    prev = docs[7:8, :]
    soft, a, b, reach, tail, keep = scan_factors(z, heads_o[1:2, :], doc, prev)
    factors = two_parts(jnp.concatenate([reach, tail, jnp.broadcast_to(keep, (8, 128))], axis=0))
    bt = b.T
    row = lax.broadcasted_iota(jnp.int32, (Q, Q), 0)
    lane = lax.broadcasted_iota(jnp.int32, (Q, Q), 1)
    joined = (row >= lane) & (doc == doc_row)
    low = lane < HD
    zero = jnp.zeros((Q, Q), bf16)

    def conv(t):
        cols = slice(128 * t, 128 * t + 128)
        here = pbuf[t, 8 : 8 + Q, :]
        cin_o[:, cols] = here.astype(bf16)
        half = cb[:, cols] + cw[3:4, cols] * here
        for k in range(3):
            half = half + cw[k : k + 1, cols] * (pbuf[t, 5 + k : 5 + k + Q, :] * masks[k])
        pbuf[t, 0:8, :] = pbuf[t, Q : Q + 8, :]
        up = 1.0 + jnp.tanh(half)
        act = half * up
        dact_o[:, cols] = (up + act * (2.0 - up)).astype(bf16)
        act = act.astype(bf16)
        act_o[:, cols] = act
        return act

    normed(tok)
    bmat = conv(tiles - 2)
    cmat = conv(tiles - 1)
    bt_mat = bmat.astype(f32).T.astype(bf16)
    s = dot_nt(cmat, bmat)
    for p in range(heads // 2):
        cols = slice(128 * p, 128 * p + 128)
        half = slice(128 * (p % 2), 128 * (p % 2) + 128)
        if p % 2 == 0:
            group = slice(128 * p, 128 * p + 256)
            wide = dot(factors, onehot[:, group])
            st_low = state[:, group].astype(bf16)
            st_o[0, :, group] = st_low
            cs = dot(cmat, st_low)
        xp = conv(p)
        if p < tiles // 2:
            project(2 * p)
        if p == tiles // 2:
            project_step()
        parts = []
        for h in (2 * p, 2 * p + 1):
            spread = jnp.broadcast_to(a[:, h : h + 1], (Q, Q)) - bt[h : h + 1, :]
            parts.append((jnp.exp2(jnp.where(joined, spread, NEG)) * s).astype(bf16))
        xbd = jnp.concatenate([jnp.where(low, xp, zero), jnp.where(low, zero, xp)], axis=0)
        y = dot(jnp.concatenate(parts, axis=1), xbd)
        xf = xp.astype(f32)
        y = y + cs[:, half] * wide[0:Q, half] + xf * skip[:, cols]
        scan_o[:, cols] = y.astype(bf16)
        xw = (xf * wide[Q : 2 * Q, half]).astype(bf16)
        state[:, cols] = state[:, cols] * wide[2 * Q : 2 * Q + 1, half] + dot(bt_mat, xw)
    advance()


def forward_scan(tok, wc, small, device, seg, seqs, ri, ro, share, heads):
    rows = tok.shape[0]
    n = rows // Q
    one = pl.Buffered(buffer_count=1)
    full = lambda arr: pl.BlockSpec(arr.shape, lambda i: (0,) * arr.ndim, pipeline_mode=one)
    blk = lambda w: pl.BlockSpec((Q, w), lambda i: (i, 0))
    hbm = pl.BlockSpec(memory_space=pl.ANY)
    low = lambda *shape: jax.ShapeDtypeStruct(shape, bf16)
    sides = [(1, D), (1, D), (8, CONV), (1, CONV), (1, DI), (8, 128), (1, DI)]
    side = lambda shape: pl.BlockSpec(shape, lambda i: (0, 0))
    return pl.pallas_call(
        functools.partial(forward_scan_kernel, heads, n // seqs, ri, ro, share),
        grid=(n,),
        in_specs=[pl.BlockSpec((Q, D), lambda i: (0, 0), pipeline_mode=one),
                  pl.BlockSpec((Q, D), lambda i: (jnp.minimum(i + 1, n - 1), 0)), hbm, hbm, hbm, hbm, full(small), full(device),
                  pl.BlockSpec((1, 1, Q), lambda i: (i, 0, 0)), pl.BlockSpec((1, 1, Q), lambda i: (jnp.maximum(i - 1, 0), 0, 0))],
        out_specs=[blk(CONV), blk(CONV), blk(CONV), blk(D), blk(DI), pl.BlockSpec((1, N, DI), lambda i: (i, 0, 0)), blk(128)]
        + [side(shape) for shape in sides],
        out_shape=[low(rows, CONV), low(rows, CONV), low(rows, CONV), low(rows, D), low(rows, DI), low(n, N, DI),
                   jax.ShapeDtypeStruct((rows, 128), f32)] + [jax.ShapeDtypeStruct(shape, f32) for shape in sides],
        scratch_shapes=[pltpu.VMEM((CONV // 128, Q + 8, 128), f32), pltpu.VMEM((Q, 128), f32), pltpu.VMEM((Q, D), bf16),
                        pltpu.VMEM((CONV // 128, Q, 128), f32), pltpu.VMEM((Q, 128), f32), pltpu.VMEM((Q, D), bf16),
                        pltpu.VMEM((N, DI), f32), pltpu.VMEM((Q + 8, 128), f32), pltpu.VMEM((256, DI), bf16),
                        pltpu.VMEM((D, CONV + 128), bf16), pltpu.SemaphoreType.DMA((4,))],
        compiler_params=pltpu.CompilerParams(vmem_limit_bytes=56 << 20),
        name="forward_scan",
    )(tok, tok, *wc, small, device, seg, seg)


def block_order(ri):
    row = lax.broadcasted_iota(jnp.int32, (192, 192), 0)
    lane = lax.broadcasted_iota(jnp.int32, (192, 192), 1)
    second = lane >= 96
    at = jnp.where(second, lane - 96, lane)
    owner = lax.div(at, ri)
    target = owner * (2 * ri) + (at - owner * ri) + jnp.where(second, ri, 0)
    return (row == target).astype(bf16)


def gate_kernel(ri, tok, scan, cot, later_in, gain, gg, mixed_o, dscan_o, dgate_o, early_o, wo_o, later, wo, early, sems,
                acc_g, acc_o, nb_s, nbt_s, mixt_s, h_s, e_s, gated_s, eg_s):
    i = pl.program_id(0)
    bm, high = 256, 32
    blocks = tok.shape[0] // bm

    wo_copy = pltpu.make_async_copy(wo, wo_o, sems.at[2])

    @pl.when(i == 0)
    def _():
        copies = [pltpu.make_async_copy(later_in.at[:, cols], later.at[:, cols], sems.at[n])
                  for n, cols in enumerate((slice(DI, 2 * DI), slice(0, DI)))]
        for copy in copies:
            copy.start()
        acc_g[...] = jnp.zeros_like(acc_g)
        acc_o[...] = jnp.zeros_like(acc_o)
        copies[0].wait()
        put = block_order(ri)
        for g in range(D // 96):
            at = slice(96 * g, 96 * g + 96)
            halves = jnp.concatenate([later[at, DI : DI + D], later[at, DI + D :]], axis=0)
            wo[192 * g : 192 * g + 192, :] = dot(put, halves).astype(bf16)
        wo_copy.start()
        copies[1].wait()

    x = tok[...].astype(f32)
    r = lax.rsqrt(jnp.mean(x * x, axis=-1, keepdims=True) + EPS)
    nb = (x * r * gain[...]).astype(bf16)
    nb_s[...] = nb * 0.5
    nbt_s[...] = nb.T

    def products(n):
        rows = slice(bm * n, bm * n + bm)
        for c in range(DI // 256):
            cols = slice(256 * c, 256 * c + 256)
            h_s[rows, cols] = dot(nb_s[rows, :], later[:, cols])
            yield
            e_s[rows, cols] = dot_nt(cot[rows, :], wo[cols, :])
            yield

    def sums(n):
        rows = slice(bm * n, bm * n + bm)
        for c in range(DI // 256):
            cols = slice(256 * c, 256 * c + 256)
            mixt_s[cols, :] = mixed_o[rows, cols].T
        for c in range(D // 256):
            cols = slice(256 * c, 256 * c + 256)
            acc_o[:, cols] += dot(mixt_s[...], cot[rows, cols])
            yield
        for c in range(DI // 256):
            cols = slice(256 * c, 256 * c + 256)
            acc_g[:, cols] += dot(nbt_s[:, rows], dgate_o[rows, cols])
            yield

    def elementwise(n, part):
        rows = slice(bm * n + part * high, bm * n + part * high + high)
        squares = jnp.zeros((high, 128), f32)
        cross = jnp.zeros((high, 128), f32)
        for t in range(DI // 128):
            cols = slice(128 * t, 128 * t + 128)
            h = h_s[rows, cols]
            gated = scan[rows, cols].astype(f32) * (h + h * jnp.tanh(h))
            eg = e_s[rows, cols] * gg[:, cols]
            squares = squares + gated * gated
            cross = cross + gated * eg
            gated_s[part, :, cols] = gated
            eg_s[part, :, cols] = eg
        rr = lax.rsqrt(jnp.sum(squares, axis=-1, keepdims=True) * (1.0 / DI) + EPS)
        pull = rr * rr * rr * (jnp.sum(cross, axis=-1, keepdims=True) * (1.0 / DI))
        rr = jnp.broadcast_to(rr, (high, 128))
        pull = jnp.broadcast_to(pull, (high, 128))
        yield
        for t in range(DI // 128):
            cols = slice(128 * t, 128 * t + 128)
            h = h_s[rows, cols]
            th = jnp.tanh(h)
            gated = gated_s[part, :, cols]
            mixed_o[rows, cols] = (gated * rr * gg[:, cols]).astype(bf16)
            dg = eg_s[part, :, cols] * rr - gated * pull
            act = h + h * th
            dscan_o[rows, cols] = (dg * act).astype(bf16)
            dg = dg * scan[rows, cols].astype(f32)
            dgate_o[rows, cols] = (dg * ((1.0 + th) + act * (1.0 - th))).astype(bf16)
        yield

    def both(n, matrix):
        vector = [step for part in range(bm // high) for step in [elementwise(n, part)] * 2]
        for step in vector:
            next(step)
            next(matrix, None)
        for _ in matrix:
            pass

    for _ in products(0):
        pass
    for n in range(blocks):
        both(n, products(n + 1) if n + 1 < blocks else sums(n - 1))
    for _ in sums(blocks - 1):
        pass

    @pl.when(i == pl.num_programs(0) - 1)
    def _():
        put = block_order(ri)
        for g in range(D // 96):
            at = slice(96 * g, 96 * g + 96)
            early[at, :DI] = (0.5 * acc_g[at, :]).astype(bf16)
            halves = dot_tn(put, acc_o[192 * g : 192 * g + 192, :].astype(bf16)).astype(bf16)
            early[at, DI : DI + D] = halves[:96]
            early[at, DI + D :] = halves[96:]
            pltpu.make_async_copy(early.at[at], early_o.at[at], sems.at[3 + g]).start()
        for g in range(D // 96):
            at = slice(96 * g, 96 * g + 96)
            pltpu.make_async_copy(early.at[at], early_o.at[at], sems.at[3 + g]).wait()
        wo_copy.wait()


def gate_pass(tok, scan, cot, later, gain, gg, ri, bm=512):
    rows = tok.shape[0]
    one = pl.Buffered(buffer_count=1)
    full = lambda shape: pl.BlockSpec(shape, lambda i: (0,) * len(shape), pipeline_mode=one)
    blk = lambda w: pl.BlockSpec((bm, w), lambda i: (i, 0))
    hbm = pl.BlockSpec(memory_space=pl.ANY)
    low = lambda *shape: jax.ShapeDtypeStruct(shape, bf16)
    return pl.pallas_call(
        functools.partial(gate_kernel, ri),
        grid=(rows // bm,),
        in_specs=[blk(D), blk(DI), blk(D), hbm, full(gain.shape), full(gg.shape)],
        out_specs=[blk(DI), blk(DI), blk(DI), hbm, hbm],
        out_shape=[low(rows, DI), low(rows, DI), low(rows, DI), low(D, 2 * DI), low(DI, D)],
        scratch_shapes=[pltpu.VMEM((D, 2 * DI), bf16), pltpu.VMEM((DI, D), bf16), pltpu.VMEM((D, 2 * DI), bf16),
                        pltpu.SemaphoreType.DMA((3 + D // 96,)), pltpu.VMEM((D, DI), f32), pltpu.VMEM((DI, D), f32), pltpu.VMEM((bm, D), bf16), pltpu.VMEM((D, bm), bf16),
                        pltpu.VMEM((DI, 256), bf16),
                        pltpu.VMEM((bm, DI), f32), pltpu.VMEM((bm, DI), f32), pltpu.VMEM((8, 32, DI), f32),
                        pltpu.VMEM((8, 32, DI), f32)],
        compiler_params=pltpu.CompilerParams(vmem_limit_bytes=VM),
        name="gate_pass",
    )(tok, scan, cot, later, gain, gg)


def out_kernel(mixed, tok, wo, out_o):
    out_o[...] = (tok[...].astype(f32) + dot(mixed[...], wo[...])).astype(bf16)


def out_pass(mixed, tok, wo, bm=512):
    rows = tok.shape[0]
    blk = lambda w: pl.BlockSpec((bm, w), lambda i: (i, 0))
    return pl.pallas_call(
        out_kernel,
        grid=(rows // bm,),
        in_specs=[blk(DI), blk(D), pl.BlockSpec((DI, D), lambda i: (0, 0), pipeline_mode=pl.Buffered(buffer_count=1))],
        out_specs=blk(D),
        out_shape=jax.ShapeDtypeStruct((rows, D), bf16),
        compiler_params=pltpu.CompilerParams(vmem_limit_bytes=50 << 20),
        cost_estimate=pl.CostEstimate(flops=0, bytes_accessed=0, transcendentals=0),
        name="out_pass",
    )(mixed, tok, wo)


def pack_grads(nf, share, tall, gcw, gcb, gsk, ghd, device, sums, rows, out_o):
    nd = device.shape[0]
    owner = device[...][:, 0:1]
    first_lane = nf * share

    def spread(values, width, who):
        total = values[0].shape[1]
        lane = lax.broadcasted_iota(jnp.int32, (128, total), 1).astype(f32)
        piece = jnp.floor((lane + 0.5) * (1.0 / width))
        place = lax.broadcasted_iota(jnp.int32, (128, total), 0).astype(f32) - first_lane
        pick = ((place == lane - piece * width) & (place < width)).astype(bf16)
        mine = piece[0:1, :] == who
        terms = []
        for value in values:
            hi = value.astype(bf16).astype(f32)
            terms += [jnp.where(mine, part, 0.0).astype(bf16) for part in (hi, value - hi)]
        out = dot_nt(jnp.concatenate(terms, axis=0), pick)
        return [out[nd * k : nd * k + nd] for k in range(len(terms))]

    rows[...] = jnp.zeros_like(rows)

    def put(n, values):
        rows[pl.ds(n, nd, stride=tall), :] = values

    taps = [0.5 * jnp.sum(gcw[8 * k : 8 * k + 8, :], axis=0, keepdims=True) for k in range(4)]
    taps.append(0.5 * jnp.sum(gcb[...], axis=0, keepdims=True))
    for k, part in enumerate(spread(taps, CONV // nd, owner)):
        put(k // 2 + 5 * (k % 2), part)
    group = owner - nf * jnp.floor((owner + 0.5) * (1.0 / nf))
    skips = two_parts(jnp.broadcast_to(jnp.sum(gsk[...], axis=0, keepdims=True), (8, DI)))
    skips = dot(skips[:, :DI], sums[...]) + dot(skips[:, DI:], sums[...])
    per_head = [jnp.sum(ghd[0:8, :], axis=0, keepdims=True), jnp.sum(ghd[8:16, :], axis=0, keepdims=True), skips[0:1, :]]
    for k, part in enumerate(spread(per_head, share, group)):
        put(10 + k // 2 + 3 * (k % 2), part)
    out_o[...] = rows[...].astype(bf16)


def backward_scan_kernel(heads, per_seq, nf, share, tall, dscan, cin, act, dact, z_r, st, cw, head_terms, skip, seg, seg_before,
                         wc_0, wc_1, wc_2, wc_3, device, dproj_o, gproj_o, pack_o, gproj,
                         dstate, p1buf, qbuf, xwbuf, rowbuf, lastbuf, mbuf, onehot, sums, docs,
                         gcw_o, gcb_o, gsk_o, ghd_o, rows_s, wc, dlast, sems):
    i = pl.program_id(0)
    steps = pl.num_programs(0)

    @pl.when(i == 0)
    def _():
        copies = copies_of((wc_0, wc_1, wc_2, wc_3), wc, sems)
        for copy in copies:
            copy.start()
        dlast[...] = jnp.zeros_like(dlast)
        gcw_o[...] = jnp.zeros_like(gcw_o)
        gcb_o[...] = jnp.zeros_like(gcb_o)
        gsk_o[...] = jnp.zeros_like(gsk_o)
        ghd_o[...] = jnp.zeros_like(ghd_o)
        rowbuf[...] = jnp.zeros_like(rowbuf)
        lastbuf[...] = jnp.zeros_like(lastbuf)
        onehot[...] = head_onehot(onehot.shape)
        head = lax.broadcasted_iota(jnp.int32, sums.shape, 0) >> 6
        sums[...] = (head == lax.broadcasted_iota(jnp.int32, sums.shape, 1)).astype(bf16)
        for copy in copies:
            copy.wait()
        clear_free(wc, heads)

    @pl.when(lax.rem(i, per_seq) == 0)
    def _():
        mbuf[:, :, Q : Q + 8, :] = jnp.zeros((3, CONV // 128, 8, 128), f32)
        dstate[...] = jnp.zeros_like(dstate)

    z = z_r[...]
    rate = head_terms[1:2, :]
    doc_row = seg[0].astype(f32)
    before_row = jnp.where(lax.rem(i, per_seq) == per_seq - 1, -1.0, seg_before[0].astype(f32))
    doc, masks = documents(doc_row, before_row, docs)
    prev = docs[7:8, :]
    soft, a, b, reach, tail, keep = scan_factors(z, rate, doc, prev)
    factors = two_parts(jnp.concatenate([reach, tail, jnp.broadcast_to(keep, (8, 128))], axis=0))
    at = a.T
    row = lax.broadcasted_iota(jnp.int32, (Q, Q), 0)
    lane = lax.broadcasted_iota(jnp.int32, (Q, Q), 1)
    joined = (lane >= row) & (doc == doc_row)
    low = lane < HD
    bmat = act[:, DI : DI + N]
    cmat = act[:, DI + N :]
    ct_mat = cmat.astype(f32).T.astype(bf16)
    s = dot_nt(bmat, cmat)
    ds_low = dstate[...].astype(bf16)
    zero = jnp.zeros((Q, Q), bf16)
    dst = jnp.zeros((Q, Q), f32)

    def conv_back(t, grad):
        cols = slice(128 * t, 128 * t + 128)
        dpre = grad * dact[:, cols].astype(f32)
        for k in range(3):
            mbuf[k, t, 0:Q, :] = dpre * masks[k]
        cv = cin[:, cols].astype(f32)
        dcin = cw[3:4, cols] * dpre
        gcb_o[:, cols] += jnp.sum(dpre.reshape(-1, 8, 128), axis=0)
        gcw_o[24:32, cols] += jnp.sum((cv * dpre).reshape(-1, 8, 128), axis=0)
        for k in range(3):
            moved = mbuf[k, t, 3 - k : 3 - k + Q, :]
            dcin = dcin + cw[k : k + 1, cols] * moved
            gcw_o[8 * k : 8 * k + 8, cols] += jnp.sum((cv * moved).reshape(-1, 8, 128), axis=0)
        dproj_o[:, cols] = dcin.astype(bf16)
        mbuf[:, t, Q : Q + 8, :] = mbuf[:, t, 0:8, :]

    def project_back(given, block, part):
        cols = slice(256 * part, 256 * part + 256)
        gproj[pl.ds(block * Q, Q), cols] = dot_nt(given[...], wc[cols, :]).astype(bf16)

    block_before = steps - jnp.maximum(i, 1)
    for p in range(heads // 2):
        cols = slice(128 * p, 128 * p + 128)
        half = slice(128 * (p % 2), 128 * (p % 2) + 128)
        if p % 2 == 0:
            group = slice(128 * p, 128 * p + 256)
            wide = dot(factors, onehot[:, group])
            cs = dot(cmat, st[0, :, group])
            bd = dot(bmat, ds_low[:, group])
        if p % 4 == 1:
            project_back(dlast, block_before, p // 4)
        xp = act[:, cols]
        dy = dscan[:, cols]
        dybd = jnp.concatenate([jnp.where(low, dy, zero), jnp.where(low, zero, dy)], axis=0)
        dm = dot_nt(xp, dybd)
        parts = []
        for n, h in enumerate((2 * p, 2 * p + 1)):
            spread = at[h : h + 1, :] - jnp.broadcast_to(b[:, h : h + 1], (Q, Q))
            e = jnp.exp2(jnp.where(joined, spread, NEG))
            m = (e * s).astype(bf16)
            parts.append(m)
            dmh = dm[:, 128 * n : 128 * n + 128]
            dst = dst + dmh * e
            rowbuf[h : h + 1, :] = jnp.sum(dmh * m.astype(f32), axis=0, keepdims=True)
        xf = xp.astype(f32)
        dyf = dy.astype(f32)
        tail_p = wide[Q : 2 * Q, half]
        fresh = bd[:, half] * tail_p
        dx = dot(jnp.concatenate(parts, axis=1), dybd) + fresh
        p1 = xf * dx
        hi = p1.astype(bf16)
        p1buf[:, cols] = hi
        p1buf[:, DI + 128 * p : DI + 128 * p + 128] = (p1 - hi.astype(f32)).astype(bf16)
        dyr = dyf * wide[0:Q, half]
        qbuf[:, cols] = (dyr * cs[:, half]).astype(bf16)
        dyr = dyr.astype(bf16)
        ds = dstate[:, cols]
        lastbuf[0:1, cols] = jnp.sum(xf * fresh, axis=0, keepdims=True) + wide[2 * Q : 2 * Q + 1, half] * jnp.sum(
            ds * st[0, :, cols].astype(f32), axis=0, keepdims=True)
        gsk_o[:, cols] += jnp.sum((dyf * xf).reshape(-1, 8, 128), axis=0)
        xwbuf[:, cols] = (xf * tail_p).astype(bf16)
        xwbuf[:, DI + 128 * p : DI + 128 * p + 128] = dyr
        dstate[:, cols] = ds * wide[2 * Q : 2 * Q + 1, half] + dot(ct_mat, dyr)
        conv_back(p, dx + skip[:, cols] * dyf)
    dst_low = dst.astype(bf16)
    conv_back(DI // 128, dot(dst_low, cmat) + dot_nt(xwbuf[:, :DI], ds_low))
    conv_back(DI // 128 + 1, dot_tn(dst_low, bmat) + dot_nt(xwbuf[:, DI:], st[0]))
    hot = sums[...]
    p1 = dot(p1buf[:, :DI], hot) + dot(p1buf[:, DI:], hot)
    last = two_parts(lastbuf[...])
    last = (dot(last[:, :DI], hot) + dot(last[:, DI:], hot))[0:1, :]
    da = dot(qbuf[...], hot) - p1 + rowbuf[...].T
    g = cumsum_rows(da, reverse=True) + last
    sig = sigmoid(z)
    ratio = jnp.where(z < -15.0, 1.0, sig / jnp.where(z < -15.0, 1.0, soft))
    dz = g * rate * sig + p1 * ratio
    dproj_o[:, CONV:] = dz.astype(bf16)
    ghd_o[0:8, :] += jnp.sum(dz.reshape(-1, 8, 128), axis=0)
    ghd_o[8:16, :] += rate * jnp.sum((g * soft).reshape(-1, 8, 128), axis=0)
    dlast[...] = dproj_o[...]

    def copy_out(block):
        at = pl.ds(block * Q, Q)
        return pltpu.make_async_copy(gproj.at[at], gproj_o.at[at], sems.at[4])

    @pl.when(i > 0)
    def _():
        copy_out(block_before).start()

    @pl.when(i == steps - 1)
    def _():
        for part in range(D // 256):
            project_back(dlast, 0, part)
        copy_out(0).start()
        pack_grads(nf, share, tall, gcw_o, gcb_o, gsk_o, ghd_o, device, sums, rows_s, pack_o)
        pltpu.make_async_copy(gproj, gproj_o, sems.at[4]).wait()


def backward_scan(dscan, cin, act, dact, z, st, cw, head_terms, skip, seg, wc, device, heads, seqs, nf, share, tall):
    rows = dscan.shape[0]
    n = rows // Q
    nd = device.shape[0]
    one = pl.Buffered(buffer_count=1)
    full = lambda shape: pl.BlockSpec(shape, lambda i: (0,) * len(shape), pipeline_mode=one)
    blk = lambda w: pl.BlockSpec((Q, w), lambda i: (n - 1 - i, 0))
    blk3 = lambda s1, s2: pl.BlockSpec((1, s1, s2), lambda i: (n - 1 - i, 0, 0))
    hbm = pl.BlockSpec(memory_space=pl.ANY)
    return pl.pallas_call(
        functools.partial(backward_scan_kernel, heads, n // seqs, nf, share, tall),
        grid=(n,),
        in_specs=[blk(DI), blk(CONV), blk(CONV), blk(CONV), blk(128), blk3(N, DI), full(cw.shape), full(head_terms.shape),
                  full(skip.shape), blk3(1, Q), pl.BlockSpec((1, 1, Q), lambda i: (jnp.maximum(n - 2 - i, 0), 0, 0)),
                  hbm, hbm, hbm, hbm, full(device.shape)],
        out_specs=[blk(CONV + 128), hbm, full((nd * tall, 128))],
        out_shape=[jax.ShapeDtypeStruct((rows, CONV + 128), bf16), jax.ShapeDtypeStruct((rows, D), bf16),
                   jax.ShapeDtypeStruct((nd * tall, 128), bf16)],
        scratch_shapes=[pltpu.VMEM((rows, D), bf16), pltpu.VMEM((N, DI), f32), pltpu.VMEM((Q, 2 * DI), bf16), pltpu.VMEM((Q, DI), bf16),
                        pltpu.VMEM((Q, 2 * DI), bf16), pltpu.VMEM((128, 128), f32), pltpu.VMEM((8, DI), f32),
                        pltpu.VMEM((3, CONV // 128, Q + 8, 128), f32), pltpu.VMEM((256, DI), bf16),
                        pltpu.VMEM((DI, 128), bf16), pltpu.VMEM((Q + 8, 128), f32), pltpu.VMEM((32, CONV), f32),
                        pltpu.VMEM((8, CONV), f32), pltpu.VMEM((8, DI), f32), pltpu.VMEM((16, 128), f32),
                        pltpu.VMEM((nd * tall, 128), f32), pltpu.VMEM((D, CONV + 128), bf16), pltpu.VMEM((Q, CONV + 128), bf16),
                        pltpu.SemaphoreType.DMA((5,))],
        compiler_params=pltpu.CompilerParams(vmem_limit_bytes=52 << 20),
        cost_estimate=pl.CostEstimate(flops=0, bytes_accessed=0, transcendentals=0),
        name="backward_scan",
    )(dscan, cin, act, dact, z, st, cw, head_terms, skip, seg, seg, *wc, device)


def norm_back_kernel(ri, gproj, dgate, tok, cot, wg_abs, gain, device, out_o, wg, order):
    @pl.when(pl.program_id(0) == 0)
    def _():
        column = lax.broadcasted_iota(jnp.int32, (8, D), 1).astype(f32)
        slot = jnp.floor((column + 0.5) * (1.0 / ri))
        nd = device.shape[0]
        mine = lax.broadcasted_iota(jnp.int32, (nd, D), 0).astype(f32) == slot[0:1, :]
        feature = jnp.sum(jnp.where(mine, device[...][:, 0:1], 0.0), axis=0, keepdims=True) * ri + (column - slot * ri)[0:1, :]
        order[...] = (lax.broadcasted_iota(jnp.int32, (D, D), 0).astype(f32) == feature).astype(bf16)
        wg[...] = (0.5 * dot_tn(order[...], wg_abs[...])).astype(bf16)

    grad = dot_nt(dgate[...], wg[...]) + gproj[...].astype(f32)
    x = tok[...].astype(f32)
    r = lax.rsqrt(jnp.mean(x * x, axis=-1, keepdims=True) + EPS)
    unit = x * r
    e = gain[...] * grad
    back = r * (e - unit * jnp.mean(unit * e, axis=-1, keepdims=True))
    res = (cot[...].astype(f32) + back).astype(bf16)
    out_o[...] = dot_nt(res, order[...]).astype(bf16)


def norm_back(gproj, dgate, tok, cot, later, gain, device, ri, bm=512):
    rows = gproj.shape[0]
    one = pl.Buffered(buffer_count=1)
    full = lambda shape: pl.BlockSpec(shape, lambda i: (0,) * len(shape), pipeline_mode=one)
    blk = lambda w: pl.BlockSpec((bm, w), lambda i: (i, 0))
    return pl.pallas_call(
        functools.partial(norm_back_kernel, ri),
        grid=(rows // bm,),
        in_specs=[blk(D), blk(DI), blk(D), blk(D), full((D, DI)), full(gain.shape), full(device.shape)],
        out_specs=blk(D),
        out_shape=jax.ShapeDtypeStruct((rows, D), bf16),
        scratch_shapes=[pltpu.VMEM((D, DI), bf16), pltpu.VMEM((D, D), bf16)],
        compiler_params=pltpu.CompilerParams(vmem_limit_bytes=46 << 20),
        cost_estimate=pl.CostEstimate(flops=0, bytes_accessed=0, transcendentals=0),
        name="norm_back",
    )(gproj, dgate, tok, cot, later, gain, device)


def conv_weight_kernel(nrm, dproj, small, a_o, b_o):
    grad = lax.dot_general(dproj[...], nrm[...], (((0,), (0,)), ((), ())), preferred_element_type=f32)
    half = a_o.shape[0]
    out = grad.astype(bf16).T
    a_o[...] = out[:half]
    b_o[...] = out[half:]

    @pl.when(pl.program_id(0) == pl.num_programs(0) - 1)
    def _():
        last = slice(a_o.shape[1] - 128, a_o.shape[1])
        out = (grad[a_o.shape[1] - 128 :].T + small[...].astype(f32)).astype(bf16)
        a_o[:, last] = out[:half]
        b_o[:, last] = out[half:]


def conv_weight_grad(nrm, dproj, small, bn=640):
    rows = nrm.shape[0]
    one = pl.Buffered(buffer_count=1)
    return pl.pallas_call(
        conv_weight_kernel,
        grid=((CONV + 128) // bn,),
        in_specs=[pl.BlockSpec((rows, D), lambda i: (0, 0), pipeline_mode=one), pl.BlockSpec((rows, bn), lambda i: (0, i)),
                  pl.BlockSpec((D, 128), lambda i: (0, 0), pipeline_mode=one)],
        out_specs=[pl.BlockSpec((D // 2, bn), lambda i: (0, i))] * 2,
        out_shape=[jax.ShapeDtypeStruct((D // 2, CONV + 128), bf16)] * 2,
        compiler_params=pltpu.CompilerParams(vmem_limit_bytes=50 << 20),
        cost_estimate=pl.CostEstimate(flops=0, bytes_accessed=0, transcendentals=0),
        name="conv_weight_grad",
    )(nrm, dproj, small)


def finish_kernel(heads, share, parts, early_in, w_in, w_out, in_gain, gate_gain, *refs):
    own, got = refs[0], refs[1:parts]
    in_o, out_o, in_gain_o, gate_gain_o, cw_o, cb_o, sb_o, dl_o, sg_o, total, early, sem = refs[parts:]
    copy = pltpu.make_async_copy(early_in, early, sem)
    copy.start()
    ri, ro, cc = w_in.shape[0], w_out.shape[0], cb_o.shape[1]
    value = own[...]
    for part in got:
        value = value + part[...].astype(f32)
    total[...] = value
    in_o[:, DI:] = total[0:ri, : CONV + heads]
    copy.wait()
    in_o[:, :DI] = early[:, :DI].astype(f32)
    out_o[0:ri, :] = early[:, DI : DI + D].astype(f32)
    out_o[ri:, :] = early[:, DI + D :].astype(f32)

    def across(column, count):
        spot = lax.broadcasted_iota(jnp.int32, (count, count), 0) == lax.broadcasted_iota(jnp.int32, (count, count), 1)
        return jnp.sum(jnp.where(spot, column, 0.0), axis=0, keepdims=True)

    in_gain_o[...] = across(jnp.sum(w_in[...].astype(f32) * in_o[...], axis=-1, keepdims=True), ri) / in_gain[...].astype(f32)
    gate_gain_o[...] = across(jnp.sum(w_out[...].astype(f32) * out_o[...], axis=-1, keepdims=True), ro) / gate_gain[...].astype(f32)
    at = CONV + heads
    cw_o[...] = total[0:4, at : at + cc] + total[5:9, at : at + cc]
    cb_o[...] = total[4:5, at : at + cc] + total[9:10, at : at + cc]
    for k, term in enumerate((sb_o, dl_o, sg_o)):
        term[...] = total[10 + k : 11 + k, at : at + share] + total[13 + k : 14 + k, at : at + share]


def finish(early, w_in, w_out, in_gain, gate_gain, own, got, heads, share, cc):
    ri, ro = w_in.shape[0], w_out.shape[0]
    shapes = [(ri, w_in.shape[1]), (ro, D), (1, ri), (1, ro), (4, cc), (1, cc)] + [(1, share)] * 3
    return pl.pallas_call(
        functools.partial(finish_kernel, heads, share, 1 + len(got)),
        out_shape=[jax.ShapeDtypeStruct(shape, f32) for shape in shapes],
        in_specs=[pl.BlockSpec(memory_space=pl.ANY)] + [pl.BlockSpec(memory_space=pltpu.VMEM)] * (5 + len(got)),
        scratch_shapes=[pltpu.VMEM(own.shape, f32), pltpu.VMEM(early.shape, bf16), pltpu.SemaphoreType.DMA],
        compiler_params=pltpu.CompilerParams(vmem_limit_bytes=12 << 20),
        name="finish",
    )(early, w_in, w_out, in_gain, gate_gain, own, *got)


def stages_of(mesh):
    ndp, nf = mesh.shape["dp"], mesh.shape["fsdp"]
    out = []
    stride = 1
    while stride < nf:
        group = 2 if stride == 1 else min(4, nf // stride)
        out.append(("fsdp", stride, group, stride))
        stride *= group
    stride = 1
    while stride < ndp:
        group = min(4, ndp // stride)
        out.append(("dp", stride, group, stride * nf))
        stride *= group
    return out[::-1]


def pairs_of(stages):
    out = []
    for axis, stride, group, number in stages[::-1]:
        step = 1
        while step < group:
            out.append((axis, stride * step, 2, number * step))
            step *= 2
    return out


def slot_devices(stages):
    rel = np.zeros((1,), np.int32)
    for _, _, group, number in stages:
        rel = (np.arange(group, dtype=np.int32)[:, None] * number + rel[None, :]).reshape(-1)
    return jnp.asarray(rel)


def swap(arr, axis, size, offset):
    return lax.ppermute(arr, axis, [(i, i ^ offset) for i in range(size)])


def gather_stage(block, stage, sizes, first=0):
    axis, stride, group, _ = stage
    if first == 0 or group != 4:
        return jnp.stack([block] + [swap(block, axis, sizes[axis], k * stride) for k in range(1, group)])
    if first == 1:
        block = jnp.stack([block, swap(block, axis, sizes[axis], stride)])
        return jnp.concatenate([block, swap(block, axis, sizes[axis], 2 * stride)])
    block = jnp.stack([block, swap(block, axis, sizes[axis], 2 * stride)])
    block = jnp.stack([block, swap(block, axis, sizes[axis], stride)], axis=1)
    return block.reshape((4,) + block.shape[2:])


def scatter_parts(kept, stage, sizes):
    axis, stride, group, _ = stage
    return [swap(kept[k].astype(bf16), axis, sizes[axis], k * stride) for k in range(1, group)]


def scatter_stage(kept, stage, sizes):
    total = kept[0]
    for part in scatter_parts(kept, stage, sizes):
        total = total + part.astype(f32)
    return total


def before(value, *others):
    return lax.optimization_barrier((value,) + others)


def local(mesh, tokens, cotangent, segments, in_gain, weight_in, conv_weight, conv_bias, step_bias, decay_log, skip_gain,
          gate_gain, weight_out):
    sizes = {"dp": mesh.shape["dp"], "fsdp": mesh.shape["fsdp"]}
    nf = sizes["fsdp"]
    nd = sizes["dp"] * nf
    axes = ("dp", "fsdp")
    stages = stages_of(mesh)
    me = lax.axis_index("dp") * nf + lax.axis_index("fsdp")
    seqs, length, _ = tokens.shape
    rows = seqs * length
    ri, ro, cc, share = weight_in.shape[0], weight_out.shape[0], conv_bias.shape[0], step_bias.shape[0]
    heads = share * nf

    device = slot_devices(stages) ^ me
    feature = (device[:, None] * ri + jnp.arange(ri)[None, :]).reshape(-1)
    order = (jnp.arange(D)[:, None] == feature[None, :]).astype(bf16)

    tall = max(ri, 16)
    wc, later = pack(weight_in, weight_out, in_gain[None], conv_weight, conv_bias[None], gate_gain[None],
                     step_bias[None], decay_log[None], skip_gain[None], ri, tall)
    later = lax.all_gather(later, axes, axis=0, tiled=True)
    tok = tokens.reshape(rows, D)
    up = cotangent.reshape(rows, D)
    wc = gather_stage(wc, stages[0], sizes)
    tok_s = jnp.dot(tok, order, preferred_element_type=bf16)
    device_rows = jnp.broadcast_to(device.astype(f32)[:, None], (nd, 128))
    seg = segments.reshape(rows // Q, 1, Q)
    wc, tok_s = before(wc, tok_s)
    one, two = wc[..., :SPLIT], wc[..., SPLIT:]
    for stage in stages[1:-1]:
        one = gather_stage(one, stage, sizes, 1)
        two = gather_stage(two, stage, sizes, 2)
    up_s = jnp.dot(up, order, preferred_element_type=bf16)
    two, up_s, device_rows, seg = before(two, up_s, device_rows, seg)
    axis, stride = stages[-1][:2]
    quarters = [part.reshape(nd // 2, tall, part.shape[-1])
                for part in (one, two, swap(one, axis, sizes[axis], stride), swap(two, axis, sizes[axis], stride))]
    last = [part[:, :16, CONV - SPLIT :] for part in (quarters[1], quarters[3])]
    small = jnp.concatenate(last, axis=0).transpose(1, 0, 2).astype(f32)
    wc = [part[:, :ri].reshape(D // 2, part.shape[-1]) for part in quarters]

    cin, act, dact, nrm, scan, st, z, gain, gain_abs, cw, cb, gg, head_terms, skip = forward_scan(
        tok_s, wc, small, device_rows, seg, seqs, ri, ro, share, heads)
    mixed, dscan, dgate, early, wo = gate_pass(tok, scan, up, later, gain_abs, gg, ri)
    early = lax.psum_scatter(early, axes, scatter_dimension=0, tiled=True)

    dproj, gproj, small = backward_scan(
        dscan, cin, act, dact, z, st, cw, head_terms, skip, seg, wc, device_rows, heads, seqs, nf, share, tall)
    if ri == tall:
        halves = conv_weight_grad(nrm, dproj, small)
        halves = [half.reshape(nd // 2, tall, CONV + 128) for half in halves]
    else:
        halves = conv_weight_grad(nrm, dproj, jnp.zeros((D, 128), bf16))
        halves = [jnp.pad(half.reshape(nd // 2, ri, CONV + 128), ((0, 0), (0, tall - ri), (0, 0))) for half in halves]
        small = jnp.pad(small.reshape(nd, tall, 128), ((0, 0), (0, 0), (CONV, 0)))
        halves = [half + part for half, part in zip(halves, (small[: nd // 2], small[nd // 2 :]))]

    axis, stride, group, _ = stages[-1]
    got = swap(halves[1], axis, sizes[axis], stride)
    shape = [g for _, _, g, _ in stages[-2::-1]] + [tall, CONV + 128]
    pieces = zip(halves[0].reshape(shape), got.reshape(shape))
    total = [mine.astype(f32) + part.astype(f32) for mine, part in pieces]
    total[0], gain = before(total[0], gain)
    gtok = norm_back(gproj, dgate, tok_s, up_s, later, gain, device_rows, ri)
    for stage in stages[-2:0:-1]:
        total = scatter_stage(total, stage, sizes)
    total, gtok, wo = before(total, gtok, wo)
    got = scatter_parts(total, stages[0], sizes)
    out = out_pass(mixed, tok, wo)
    early, out = before(early, out)
    g_in, g_out, g_in_gain, g_gate_gain, g_cw, g_cb, g_sb, g_dl, g_sg = finish(
        early, weight_in, weight_out, in_gain[None], gate_gain[None], total[0], got, heads, share, cc)
    return (out.reshape(tokens.shape), gtok.reshape(tokens.shape), g_in_gain[0], g_in, g_cw, g_cb[0],
            g_sb[0], g_dl[0], g_sg[0], g_gate_gain[0], g_out)


def solution(mesh):
    every = ("dp", "fsdp")
    return jax.shard_map(
        functools.partial(local, mesh),
        mesh=mesh,
        in_specs=(P(every, None, None), P(every, None, None), P(every, None), P(every), P(every, None), P(None, every),
                  P(every), P("fsdp"), P("fsdp"), P("fsdp"), P(every), P(every, None)),
        out_specs=(P(every, None, None), P(every, None, None), P(every), P(every, None), P(None, every), P(every),
                   P("fsdp"), P("fsdp"), P("fsdp"), P(every), P(every, None)),
        check_vma=False,
    )
```

```python
import functools

import jax
import jax.numpy as jnp
import numpy as np
from jax import lax
from jax.experimental import pallas as pl
from jax.experimental.pallas import tpu as pltpu
from jax.sharding import PartitionSpec as P

EPS = 1e-05
LOG2E = 1.4426950408889634
NEG = -1e30
f32, bf16 = jnp.float32, jnp.bfloat16
Q = 128
VM = 60 * 1024 * 1024

D, DI, CONV, N, HD = 768, 1536, 1792, 128, 64
SPLIT = 1024


def dot(a, b):
    return lax.dot_general(a, b, (((1,), (0,)), ((), ())), preferred_element_type=f32)


def dot_nt(a, b):
    return lax.dot_general(a, b, (((1,), (1,)), ((), ())), preferred_element_type=f32)


def dot_tn(a, b):
    return lax.dot_general(a, b, (((0,), (0,)), ((), ())), preferred_element_type=f32)


def sigmoid(v):
    return 1.0 / (1.0 + jnp.exp(-v))


def cumsum_rows(v, reverse=False):
    rows = lax.broadcasted_iota(jnp.int32, v.shape, 0)
    count = v.shape[0]
    shift = 1
    while shift < count:
        if reverse:
            moved = pltpu.roll(v, count - shift, 0)
            v = v + jnp.where(rows < count - shift, moved, 0.0)
        else:
            moved = pltpu.roll(v, shift, 0)
            v = v + jnp.where(rows >= shift, moved, 0.0)
        shift *= 2
    return v


def step_terms(z):
    e = jnp.exp(-jnp.abs(z))
    soft = jnp.maximum(z, 0.0) + jnp.log1p(e)
    tiny = z < -15.0
    log_soft = jnp.where(tiny, z, jnp.log(jnp.where(tiny, 1.0, soft)))
    return soft, log_soft


def columns(row):
    return jnp.broadcast_to(row, (Q, 128)).T


def documents(row, before_row, docs):
    doc = columns(row)
    docs[0:8, :] = columns(before_row)[Q - 8 : Q, :]
    docs[8 : 8 + Q, :] = doc
    return doc, [(docs[8 - s : 8 - s + Q, :] == doc).astype(f32) for s in (3, 2, 1)]


def scan_factors(z, rate, doc, prev_doc):
    soft, log_soft = step_terms(z)
    a = cumsum_rows(soft * (rate * LOG2E))
    b = a - log_soft * LOG2E
    last = a[Q - 1 : Q, :]
    last_doc = doc[Q - 1 : Q, :]
    reach = jnp.where(doc == prev_doc, jnp.exp2(a), 0.0)
    tail = jnp.where(doc == last_doc, jnp.exp2(last - b), 0.0)
    keep = jnp.where(last_doc == prev_doc, jnp.exp2(last), 0.0)
    return soft, a, b, reach, tail, keep


def pair_of(cols, p, low):
    left = jnp.broadcast_to(cols[:, 2 * p : 2 * p + 1], low.shape)
    right = jnp.broadcast_to(cols[:, 2 * p + 1 : 2 * p + 2], low.shape)
    return jnp.where(low, left, right)


def two_parts(cols):
    hi = cols.astype(bf16)
    return jnp.concatenate([hi, (cols - hi.astype(f32)).astype(bf16)], axis=1)


def head_onehot(shape):
    head = lax.broadcasted_iota(jnp.int32, shape, 1) >> 6
    return (lax.broadcasted_iota(jnp.int32, shape, 0) & 127 == head).astype(bf16)


def pack_kernel(ri, w_in, w_out, in_gain, cw, cb, gg, sb, dl, sg, wc_o, later_o, rows):
    wc_o[...] = jnp.zeros_like(wc_o)
    wc_o[0:ri, : w_in.shape[1] - DI] = w_in[:, DI:]
    rows[...] = jnp.zeros_like(rows)
    at = w_in.shape[1] - DI - CONV

    def put(n, value):
        rows[n : n + value.shape[0], at : at + value.shape[1]] = value.astype(f32)

    put(0, in_gain[...])
    put(1, cw[...])
    put(5, cb[...])
    put(6, gg[...])
    for k, term in enumerate((sb, dl, sg)):
        value = term[...]
        for n in range(3):
            part = value.astype(bf16).astype(f32)
            put(7 + 3 * n + k, part)
            value = value - part
    wc_o[0:16, CONV:] = (wc_o[0:16, CONV:].astype(f32) + rows[...]).astype(bf16)
    later_o[:, :DI] = w_in[:, :DI]
    later_o[:, DI : DI + D] = w_out[0]
    later_o[:, DI + D :] = w_out[1]


def pack(w_in, w_out, in_gain, cw, cb, gg, sb, dl, sg, ri, tall):
    return pl.pallas_call(
        functools.partial(pack_kernel, ri),
        out_shape=[jax.ShapeDtypeStruct((tall, CONV + 128), bf16), jax.ShapeDtypeStruct((ri, 2 * DI), bf16)],
        scratch_shapes=[pltpu.VMEM((16, 128), f32)],
        name="pack",
    )(w_in, w_out.reshape(2, ri, D), in_gain, cw, cb, gg, sb, dl, sg)


def unpack_small(ri, ro, share, first_lane, small, device, onehot, gain, gain_abs, cw, cb, gg, heads_o, skip):
    nd = small.shape[1]
    slot = lax.broadcasted_iota(jnp.int32, (nd, 128), 0).astype(f32)[:, 0:1]
    owner = device[...][:, 0:1]

    def spread(rows, width, total, who):
        lane = lax.broadcasted_iota(jnp.int32, (128, total), 1).astype(f32)
        piece = jnp.floor((lane + 0.5) * (1.0 / width))
        inner = lane - piece * width
        pick = (lax.broadcasted_iota(jnp.int32, (128, total), 0).astype(f32) - first_lane == inner).astype(bf16)
        mine = piece[0:1, :] == who
        out = dot(jnp.concatenate([small[r].astype(bf16) for r in rows], axis=0), pick)
        return [jnp.sum(jnp.where(mine, out[nd * n : nd * n + nd], 0.0), axis=0, keepdims=True) for n in range(len(rows))]

    gain[...] = spread([0], ri, D, slot)[0]
    gain_abs[...] = spread([0], ri, D, owner)[0]
    taps = spread(range(1, 6), CONV // nd, CONV, owner)
    for k in range(4):
        cw[k : k + 1, :] = 0.5 * taps[k]
    cw[4:8, :] = jnp.zeros((4, CONV), f32)
    cb[...] = 0.5 * taps[4]
    gg[...] = spread([6], ro, DI, owner)[0]
    parts = spread(range(7, 16), share, 128, owner)
    per_head = [parts[n] + parts[n + 3] + parts[n + 6] for n in range(3)]
    heads_o[0:1, :] = per_head[0]
    heads_o[1:2, :] = -jnp.exp(per_head[1])
    skip[...] = dot(two_parts(jnp.broadcast_to(per_head[2], (8, 128))), onehot[...])[0:1, :]


def copies_of(pieces, wc, sems):
    rows = pieces[0].shape[0]
    spots = [(n // 2, slice(0, SPLIT) if n % 2 == 0 else slice(SPLIT, CONV + 128)) for n in range(4)]
    return [pltpu.make_async_copy(piece, wc.at[rows * r : rows * r + rows, cols], sems.at[n])
            for n, (piece, (r, cols)) in enumerate(zip(pieces, spots))]


def clear_free(wc, heads):
    last = wc[:, CONV:]
    wc[:, CONV:] = jnp.where(lax.broadcasted_iota(jnp.int32, last.shape, 1) < heads, last, jnp.zeros_like(last))


def forward_scan_kernel(heads, per_seq, ri, ro, share, first, tok, wc_0, wc_1, wc_2, wc_3, small, device, seg, seg_before,
                        cin_o, act_o, dact_o, nrm_o, scan_o, st_o, z_o, gain, gain_abs, cw, cb, gg, heads_o, skip,
                        pbuf, zbuf, nbuf, pnext, znext, nnext, state, docs, onehot, wc, sems):
    i = pl.program_id(0)
    tiles = CONV // 128

    def normed(block):
        x = block[...].astype(f32)
        r = lax.rsqrt(jnp.mean(x * x, axis=-1, keepdims=True) + EPS)
        nnext[...] = (x * r * gain[...]).astype(bf16)

    def project(t):
        part = dot(nnext[...], wc[:, 128 * t : 128 * t + 256])
        pnext[t] = part[:, :128]
        pnext[t + 1] = part[:, 128:]

    def project_step():
        znext[...] = dot(nnext[...], wc[:, CONV:]) + heads_o[0:1, :]

    def advance():
        pbuf[:, 8 : 8 + Q, :] = pnext[...]
        zbuf[...] = znext[...]
        nbuf[...] = nnext[...]

    @pl.when(i == 0)
    def _():
        copies = copies_of((wc_0, wc_1, wc_2, wc_3), wc, sems)
        for copy in copies:
            copy.start()
        onehot[...] = head_onehot(onehot.shape)
        unpack_small(ri, ro, share, heads, small, device, onehot, gain, gain_abs, cw, cb, gg, heads_o, skip)
        normed(first)
        for copy in copies:
            copy.wait()
        clear_free(wc, heads)
        for t in range(0, tiles, 2):
            project(t)
        project_step()
        advance()

    @pl.when(lax.rem(i, per_seq) == 0)
    def _():
        pbuf[:, 0:8, :] = jnp.zeros((tiles, 8, 128), f32)
        state[...] = jnp.zeros_like(state)

    nrm_o[...] = nbuf[...]
    z = zbuf[...]
    z_o[...] = z
    doc_row = seg[0].astype(f32)
    before_row = jnp.where(lax.rem(i, per_seq) == 0, -1.0, seg_before[0].astype(f32))
    doc, masks = documents(doc_row, before_row, docs)
    prev = docs[7:8, :]
    soft, a, b, reach, tail, keep = scan_factors(z, heads_o[1:2, :], doc, prev)
    factors = two_parts(jnp.concatenate([reach, tail, jnp.broadcast_to(keep, (8, 128))], axis=0))
    bt = b.T
    row = lax.broadcasted_iota(jnp.int32, (Q, Q), 0)
    lane = lax.broadcasted_iota(jnp.int32, (Q, Q), 1)
    joined = (row >= lane) & (doc == doc_row)
    low = lane < HD
    zero = jnp.zeros((Q, Q), bf16)

    def conv(t):
        cols = slice(128 * t, 128 * t + 128)
        here = pbuf[t, 8 : 8 + Q, :]
        cin_o[:, cols] = here.astype(bf16)
        half = cb[:, cols] + cw[3:4, cols] * here
        for k in range(3):
            half = half + cw[k : k + 1, cols] * (pbuf[t, 5 + k : 5 + k + Q, :] * masks[k])
        pbuf[t, 0:8, :] = pbuf[t, Q : Q + 8, :]
        up = 1.0 + jnp.tanh(half)
        act = half * up
        dact_o[:, cols] = (up + act * (2.0 - up)).astype(bf16)
        act = act.astype(bf16)
        act_o[:, cols] = act
        return act

    normed(tok)
    bmat = conv(tiles - 2)
    cmat = conv(tiles - 1)
    bt_mat = bmat.astype(f32).T.astype(bf16)
    s = dot_nt(cmat, bmat)
    for p in range(heads // 2):
        cols = slice(128 * p, 128 * p + 128)
        half = slice(128 * (p % 2), 128 * (p % 2) + 128)
        if p % 2 == 0:
            group = slice(128 * p, 128 * p + 256)
            wide = dot(factors, onehot[:, group])
            st_low = state[:, group].astype(bf16)
            st_o[0, :, group] = st_low
            cs = dot(cmat, st_low)
        xp = conv(p)
        if p < tiles // 2:
            project(2 * p)
        if p == tiles // 2:
            project_step()
        parts = []
        for h in (2 * p, 2 * p + 1):
            spread = jnp.broadcast_to(a[:, h : h + 1], (Q, Q)) - bt[h : h + 1, :]
            parts.append((jnp.exp2(jnp.where(joined, spread, NEG)) * s).astype(bf16))
        xbd = jnp.concatenate([jnp.where(low, xp, zero), jnp.where(low, zero, xp)], axis=0)
        y = dot(jnp.concatenate(parts, axis=1), xbd)
        xf = xp.astype(f32)
        y = y + cs[:, half] * wide[0:Q, half] + xf * skip[:, cols]
        scan_o[:, cols] = y.astype(bf16)
        xw = (xf * wide[Q : 2 * Q, half]).astype(bf16)
        state[:, cols] = state[:, cols] * wide[2 * Q : 2 * Q + 1, half] + dot(bt_mat, xw)
    advance()


def forward_scan(tok, wc, small, device, seg, seqs, ri, ro, share, heads):
    rows = tok.shape[0]
    n = rows // Q
    one = pl.Buffered(buffer_count=1)
    full = lambda arr: pl.BlockSpec(arr.shape, lambda i: (0,) * arr.ndim, pipeline_mode=one)
    blk = lambda w: pl.BlockSpec((Q, w), lambda i: (i, 0))
    hbm = pl.BlockSpec(memory_space=pl.ANY)
    low = lambda *shape: jax.ShapeDtypeStruct(shape, bf16)
    sides = [(1, D), (1, D), (8, CONV), (1, CONV), (1, DI), (8, 128), (1, DI)]
    side = lambda shape: pl.BlockSpec(shape, lambda i: (0, 0))
    return pl.pallas_call(
        functools.partial(forward_scan_kernel, heads, n // seqs, ri, ro, share),
        grid=(n,),
        in_specs=[pl.BlockSpec((Q, D), lambda i: (0, 0), pipeline_mode=one),
                  pl.BlockSpec((Q, D), lambda i: (jnp.minimum(i + 1, n - 1), 0)), hbm, hbm, hbm, hbm, full(small), full(device),
                  pl.BlockSpec((1, 1, Q), lambda i: (i, 0, 0)), pl.BlockSpec((1, 1, Q), lambda i: (jnp.maximum(i - 1, 0), 0, 0))],
        out_specs=[blk(CONV), blk(CONV), blk(CONV), blk(D), blk(DI), pl.BlockSpec((1, N, DI), lambda i: (i, 0, 0)), blk(128)]
        + [side(shape) for shape in sides],
        out_shape=[low(rows, CONV), low(rows, CONV), low(rows, CONV), low(rows, D), low(rows, DI), low(n, N, DI),
                   jax.ShapeDtypeStruct((rows, 128), f32)] + [jax.ShapeDtypeStruct(shape, f32) for shape in sides],
        scratch_shapes=[pltpu.VMEM((CONV // 128, Q + 8, 128), f32), pltpu.VMEM((Q, 128), f32), pltpu.VMEM((Q, D), bf16),
                        pltpu.VMEM((CONV // 128, Q, 128), f32), pltpu.VMEM((Q, 128), f32), pltpu.VMEM((Q, D), bf16),
                        pltpu.VMEM((N, DI), f32), pltpu.VMEM((Q + 8, 128), f32), pltpu.VMEM((256, DI), bf16),
                        pltpu.VMEM((D, CONV + 128), bf16), pltpu.SemaphoreType.DMA((4,))],
        compiler_params=pltpu.CompilerParams(vmem_limit_bytes=56 << 20),
        name="forward_scan",
    )(tok, tok, *wc, small, device, seg, seg)


def block_order(ri):
    row = lax.broadcasted_iota(jnp.int32, (192, 192), 0)
    lane = lax.broadcasted_iota(jnp.int32, (192, 192), 1)
    second = lane >= 96
    at = jnp.where(second, lane - 96, lane)
    owner = lax.div(at, ri)
    target = owner * (2 * ri) + (at - owner * ri) + jnp.where(second, ri, 0)
    return (row == target).astype(bf16)


def gate_kernel(ri, tok, scan, cot, later_in, gain, gg, mixed_o, dscan_o, dgate_o, early_o, wo_o, later, wo, early, sems,
                acc_g, acc_o, nb_s, nbt_s, mixt_s, h_s, e_s, gated_s, eg_s):
    i = pl.program_id(0)
    bm, high = 256, 32
    blocks = tok.shape[0] // bm

    wo_copy = pltpu.make_async_copy(wo, wo_o, sems.at[2])

    @pl.when(i == 0)
    def _():
        copies = [pltpu.make_async_copy(later_in.at[:, cols], later.at[:, cols], sems.at[n])
                  for n, cols in enumerate((slice(DI, 2 * DI), slice(0, DI)))]
        for copy in copies:
            copy.start()
        acc_g[...] = jnp.zeros_like(acc_g)
        acc_o[...] = jnp.zeros_like(acc_o)
        copies[0].wait()
        put = block_order(ri)
        for g in range(D // 96):
            at = slice(96 * g, 96 * g + 96)
            halves = jnp.concatenate([later[at, DI : DI + D], later[at, DI + D :]], axis=0)
            wo[192 * g : 192 * g + 192, :] = dot(put, halves).astype(bf16)
        wo_copy.start()
        copies[1].wait()

    x = tok[...].astype(f32)
    r = lax.rsqrt(jnp.mean(x * x, axis=-1, keepdims=True) + EPS)
    nb = (x * r * gain[...]).astype(bf16)
    nb_s[...] = nb * 0.5
    nbt_s[...] = nb.T

    def products(n):
        rows = slice(bm * n, bm * n + bm)
        for c in range(DI // 256):
            cols = slice(256 * c, 256 * c + 256)
            h_s[rows, cols] = dot(nb_s[rows, :], later[:, cols])
            yield
            e_s[rows, cols] = dot_nt(cot[rows, :], wo[cols, :])
            yield

    def sums(n):
        rows = slice(bm * n, bm * n + bm)
        for c in range(DI // 256):
            cols = slice(256 * c, 256 * c + 256)
            mixt_s[cols, :] = mixed_o[rows, cols].T
        for c in range(D // 256):
            cols = slice(256 * c, 256 * c + 256)
            acc_o[:, cols] += dot(mixt_s[...], cot[rows, cols])
            yield
        for c in range(DI // 256):
            cols = slice(256 * c, 256 * c + 256)
            acc_g[:, cols] += dot(nbt_s[:, rows], dgate_o[rows, cols])
            yield

    def elementwise(n, part):
        rows = slice(bm * n + part * high, bm * n + part * high + high)
        squares = jnp.zeros((high, 128), f32)
        cross = jnp.zeros((high, 128), f32)
        for t in range(DI // 128):
            cols = slice(128 * t, 128 * t + 128)
            h = h_s[rows, cols]
            gated = scan[rows, cols].astype(f32) * (h + h * jnp.tanh(h))
            eg = e_s[rows, cols] * gg[:, cols]
            squares = squares + gated * gated
            cross = cross + gated * eg
            gated_s[part, :, cols] = gated
            eg_s[part, :, cols] = eg
        rr = lax.rsqrt(jnp.sum(squares, axis=-1, keepdims=True) * (1.0 / DI) + EPS)
        pull = rr * rr * rr * (jnp.sum(cross, axis=-1, keepdims=True) * (1.0 / DI))
        rr = jnp.broadcast_to(rr, (high, 128))
        pull = jnp.broadcast_to(pull, (high, 128))
        yield
        for t in range(DI // 128):
            cols = slice(128 * t, 128 * t + 128)
            h = h_s[rows, cols]
            th = jnp.tanh(h)
            gated = gated_s[part, :, cols]
            mixed_o[rows, cols] = (gated * rr * gg[:, cols]).astype(bf16)
            dg = eg_s[part, :, cols] * rr - gated * pull
            act = h + h * th
            dscan_o[rows, cols] = (dg * act).astype(bf16)
            dg = dg * scan[rows, cols].astype(f32)
            dgate_o[rows, cols] = (dg * ((1.0 + th) + act * (1.0 - th))).astype(bf16)
        yield

    def both(n, matrix):
        vector = [step for part in range(bm // high) for step in [elementwise(n, part)] * 2]
        for step in vector:
            next(step)
            next(matrix, None)
        for _ in matrix:
            pass

    for _ in products(0):
        pass
    for n in range(blocks):
        both(n, products(n + 1) if n + 1 < blocks else sums(n - 1))
    for _ in sums(blocks - 1):
        pass

    @pl.when(i == pl.num_programs(0) - 1)
    def _():
        put = block_order(ri)
        for g in range(D // 96):
            at = slice(96 * g, 96 * g + 96)
            early[at, :DI] = (0.5 * acc_g[at, :]).astype(bf16)
            halves = dot_tn(put, acc_o[192 * g : 192 * g + 192, :].astype(bf16)).astype(bf16)
            early[at, DI : DI + D] = halves[:96]
            early[at, DI + D :] = halves[96:]
            pltpu.make_async_copy(early.at[at], early_o.at[at], sems.at[3 + g]).start()
        for g in range(D // 96):
            at = slice(96 * g, 96 * g + 96)
            pltpu.make_async_copy(early.at[at], early_o.at[at], sems.at[3 + g]).wait()
        wo_copy.wait()


def gate_pass(tok, scan, cot, later, gain, gg, ri, bm=512):
    rows = tok.shape[0]
    one = pl.Buffered(buffer_count=1)
    full = lambda shape: pl.BlockSpec(shape, lambda i: (0,) * len(shape), pipeline_mode=one)
    blk = lambda w: pl.BlockSpec((bm, w), lambda i: (i, 0))
    hbm = pl.BlockSpec(memory_space=pl.ANY)
    low = lambda *shape: jax.ShapeDtypeStruct(shape, bf16)
    return pl.pallas_call(
        functools.partial(gate_kernel, ri),
        grid=(rows // bm,),
        in_specs=[blk(D), blk(DI), blk(D), hbm, full(gain.shape), full(gg.shape)],
        out_specs=[blk(DI), blk(DI), blk(DI), hbm, hbm],
        out_shape=[low(rows, DI), low(rows, DI), low(rows, DI), low(D, 2 * DI), low(DI, D)],
        scratch_shapes=[pltpu.VMEM((D, 2 * DI), bf16), pltpu.VMEM((DI, D), bf16), pltpu.VMEM((D, 2 * DI), bf16),
                        pltpu.SemaphoreType.DMA((3 + D // 96,)), pltpu.VMEM((D, DI), f32), pltpu.VMEM((DI, D), f32), pltpu.VMEM((bm, D), bf16), pltpu.VMEM((D, bm), bf16),
                        pltpu.VMEM((DI, 256), bf16),
                        pltpu.VMEM((bm, DI), f32), pltpu.VMEM((bm, DI), f32), pltpu.VMEM((8, 32, DI), f32),
                        pltpu.VMEM((8, 32, DI), f32)],
        compiler_params=pltpu.CompilerParams(vmem_limit_bytes=VM),
        name="gate_pass",
    )(tok, scan, cot, later, gain, gg)


def out_kernel(mixed, tok, wo, out_o):
    out_o[...] = (tok[...].astype(f32) + dot(mixed[...], wo[...])).astype(bf16)


def out_pass(mixed, tok, wo, bm=512):
    rows = tok.shape[0]
    blk = lambda w: pl.BlockSpec((bm, w), lambda i: (i, 0))
    return pl.pallas_call(
        out_kernel,
        grid=(rows // bm,),
        in_specs=[blk(DI), blk(D), pl.BlockSpec((DI, D), lambda i: (0, 0), pipeline_mode=pl.Buffered(buffer_count=1))],
        out_specs=blk(D),
        out_shape=jax.ShapeDtypeStruct((rows, D), bf16),
        compiler_params=pltpu.CompilerParams(vmem_limit_bytes=50 << 20),
        cost_estimate=pl.CostEstimate(flops=0, bytes_accessed=0, transcendentals=0),
        name="out_pass",
    )(mixed, tok, wo)


def pack_grads(nf, share, tall, gcw, gcb, gsk, ghd, device, sums, rows, out_o):
    nd = device.shape[0]
    owner = device[...][:, 0:1]
    first_lane = nf * share

    def spread(values, width, who):
        total = values[0].shape[1]
        lane = lax.broadcasted_iota(jnp.int32, (128, total), 1).astype(f32)
        piece = jnp.floor((lane + 0.5) * (1.0 / width))
        place = lax.broadcasted_iota(jnp.int32, (128, total), 0).astype(f32) - first_lane
        pick = ((place == lane - piece * width) & (place < width)).astype(bf16)
        mine = piece[0:1, :] == who
        terms = []
        for value in values:
            hi = value.astype(bf16).astype(f32)
            terms += [jnp.where(mine, part, 0.0).astype(bf16) for part in (hi, value - hi)]
        out = dot_nt(jnp.concatenate(terms, axis=0), pick)
        return [out[nd * k : nd * k + nd] for k in range(len(terms))]

    rows[...] = jnp.zeros_like(rows)

    def put(n, values):
        rows[pl.ds(n, nd, stride=tall), :] = values

    taps = [0.5 * jnp.sum(gcw[8 * k : 8 * k + 8, :], axis=0, keepdims=True) for k in range(4)]
    taps.append(0.5 * jnp.sum(gcb[...], axis=0, keepdims=True))
    for k, part in enumerate(spread(taps, CONV // nd, owner)):
        put(k // 2 + 5 * (k % 2), part)
    group = owner - nf * jnp.floor((owner + 0.5) * (1.0 / nf))
    skips = two_parts(jnp.broadcast_to(jnp.sum(gsk[...], axis=0, keepdims=True), (8, DI)))
    skips = dot(skips[:, :DI], sums[...]) + dot(skips[:, DI:], sums[...])
    per_head = [jnp.sum(ghd[0:8, :], axis=0, keepdims=True), jnp.sum(ghd[8:16, :], axis=0, keepdims=True), skips[0:1, :]]
    for k, part in enumerate(spread(per_head, share, group)):
        put(10 + k // 2 + 3 * (k % 2), part)
    out_o[...] = rows[...].astype(bf16)


def backward_scan_kernel(heads, per_seq, nf, share, tall, dscan, cin, act, dact, z_r, st, cw, head_terms, skip, seg, seg_before,
                         wc_0, wc_1, wc_2, wc_3, device, dproj_o, gproj_o, pack_o, gproj,
                         dstate, p1buf, qbuf, xwbuf, rowbuf, lastbuf, mbuf, onehot, sums, docs,
                         gcw_o, gcb_o, gsk_o, ghd_o, rows_s, wc, dlast, sems):
    i = pl.program_id(0)
    steps = pl.num_programs(0)

    @pl.when(i == 0)
    def _():
        copies = copies_of((wc_0, wc_1, wc_2, wc_3), wc, sems)
        for copy in copies:
            copy.start()
        dlast[...] = jnp.zeros_like(dlast)
        gcw_o[...] = jnp.zeros_like(gcw_o)
        gcb_o[...] = jnp.zeros_like(gcb_o)
        gsk_o[...] = jnp.zeros_like(gsk_o)
        ghd_o[...] = jnp.zeros_like(ghd_o)
        rowbuf[...] = jnp.zeros_like(rowbuf)
        lastbuf[...] = jnp.zeros_like(lastbuf)
        onehot[...] = head_onehot(onehot.shape)
        head = lax.broadcasted_iota(jnp.int32, sums.shape, 0) >> 6
        sums[...] = (head == lax.broadcasted_iota(jnp.int32, sums.shape, 1)).astype(bf16)
        for copy in copies:
            copy.wait()
        clear_free(wc, heads)

    @pl.when(lax.rem(i, per_seq) == 0)
    def _():
        mbuf[:, :, Q : Q + 8, :] = jnp.zeros((3, CONV // 128, 8, 128), f32)
        dstate[...] = jnp.zeros_like(dstate)

    z = z_r[...]
    rate = head_terms[1:2, :]
    doc_row = seg[0].astype(f32)
    before_row = jnp.where(lax.rem(i, per_seq) == per_seq - 1, -1.0, seg_before[0].astype(f32))
    doc, masks = documents(doc_row, before_row, docs)
    prev = docs[7:8, :]
    soft, a, b, reach, tail, keep = scan_factors(z, rate, doc, prev)
    factors = two_parts(jnp.concatenate([reach, tail, jnp.broadcast_to(keep, (8, 128))], axis=0))
    at = a.T
    row = lax.broadcasted_iota(jnp.int32, (Q, Q), 0)
    lane = lax.broadcasted_iota(jnp.int32, (Q, Q), 1)
    joined = (lane >= row) & (doc == doc_row)
    low = lane < HD
    bmat = act[:, DI : DI + N]
    cmat = act[:, DI + N :]
    ct_mat = cmat.astype(f32).T.astype(bf16)
    s = dot_nt(bmat, cmat)
    ds_low = dstate[...].astype(bf16)
    zero = jnp.zeros((Q, Q), bf16)
    dst = jnp.zeros((Q, Q), f32)

    def conv_back(t, grad):
        cols = slice(128 * t, 128 * t + 128)
        dpre = grad * dact[:, cols].astype(f32)
        for k in range(3):
            mbuf[k, t, 0:Q, :] = dpre * masks[k]
        cv = cin[:, cols].astype(f32)
        dcin = cw[3:4, cols] * dpre
        gcb_o[:, cols] += jnp.sum(dpre.reshape(-1, 8, 128), axis=0)
        gcw_o[24:32, cols] += jnp.sum((cv * dpre).reshape(-1, 8, 128), axis=0)
        for k in range(3):
            moved = mbuf[k, t, 3 - k : 3 - k + Q, :]
            dcin = dcin + cw[k : k + 1, cols] * moved
            gcw_o[8 * k : 8 * k + 8, cols] += jnp.sum((cv * moved).reshape(-1, 8, 128), axis=0)
        dproj_o[:, cols] = dcin.astype(bf16)
        mbuf[:, t, Q : Q + 8, :] = mbuf[:, t, 0:8, :]

    def project_back(given, block, part):
        cols = slice(256 * part, 256 * part + 256)
        gproj[pl.ds(block * Q, Q), cols] = dot_nt(given[...], wc[cols, :]).astype(bf16)

    block_before = steps - jnp.maximum(i, 1)
    for p in range(heads // 2):
        cols = slice(128 * p, 128 * p + 128)
        half = slice(128 * (p % 2), 128 * (p % 2) + 128)
        if p % 2 == 0:
            group = slice(128 * p, 128 * p + 256)
            wide = dot(factors, onehot[:, group])
            cs = dot(cmat, st[0, :, group])
            bd = dot(bmat, ds_low[:, group])
        if p % 4 == 1:
            project_back(dlast, block_before, p // 4)
        xp = act[:, cols]
        dy = dscan[:, cols]
        dybd = jnp.concatenate([jnp.where(low, dy, zero), jnp.where(low, zero, dy)], axis=0)
        dm = dot_nt(xp, dybd)
        parts = []
        for n, h in enumerate((2 * p, 2 * p + 1)):
            spread = at[h : h + 1, :] - jnp.broadcast_to(b[:, h : h + 1], (Q, Q))
            e = jnp.exp2(jnp.where(joined, spread, NEG))
            m = (e * s).astype(bf16)
            parts.append(m)
            dmh = dm[:, 128 * n : 128 * n + 128]
            dst = dst + dmh * e
            rowbuf[h : h + 1, :] = jnp.sum(dmh * m.astype(f32), axis=0, keepdims=True)
        xf = xp.astype(f32)
        dyf = dy.astype(f32)
        tail_p = wide[Q : 2 * Q, half]
        fresh = bd[:, half] * tail_p
        dx = dot(jnp.concatenate(parts, axis=1), dybd) + fresh
        p1 = xf * dx
        hi = p1.astype(bf16)
        p1buf[:, cols] = hi
        p1buf[:, DI + 128 * p : DI + 128 * p + 128] = (p1 - hi.astype(f32)).astype(bf16)
        dyr = dyf * wide[0:Q, half]
        qbuf[:, cols] = (dyr * cs[:, half]).astype(bf16)
        dyr = dyr.astype(bf16)
        ds = dstate[:, cols]
        lastbuf[0:1, cols] = jnp.sum(xf * fresh, axis=0, keepdims=True) + wide[2 * Q : 2 * Q + 1, half] * jnp.sum(
            ds * st[0, :, cols].astype(f32), axis=0, keepdims=True)
        gsk_o[:, cols] += jnp.sum((dyf * xf).reshape(-1, 8, 128), axis=0)
        xwbuf[:, cols] = (xf * tail_p).astype(bf16)
        xwbuf[:, DI + 128 * p : DI + 128 * p + 128] = dyr
        dstate[:, cols] = ds * wide[2 * Q : 2 * Q + 1, half] + dot(ct_mat, dyr)
        conv_back(p, dx + skip[:, cols] * dyf)
    dst_low = dst.astype(bf16)
    conv_back(DI // 128, dot(dst_low, cmat) + dot_nt(xwbuf[:, :DI], ds_low))
    conv_back(DI // 128 + 1, dot_tn(dst_low, bmat) + dot_nt(xwbuf[:, DI:], st[0]))
    hot = sums[...]
    p1 = dot(p1buf[:, :DI], hot) + dot(p1buf[:, DI:], hot)
    last = two_parts(lastbuf[...])
    last = (dot(last[:, :DI], hot) + dot(last[:, DI:], hot))[0:1, :]
    da = dot(qbuf[...], hot) - p1 + rowbuf[...].T
    g = cumsum_rows(da, reverse=True) + last
    sig = sigmoid(z)
    ratio = jnp.where(z < -15.0, 1.0, sig / jnp.where(z < -15.0, 1.0, soft))
    dz = g * rate * sig + p1 * ratio
    dproj_o[:, CONV:] = dz.astype(bf16)
    ghd_o[0:8, :] += jnp.sum(dz.reshape(-1, 8, 128), axis=0)
    ghd_o[8:16, :] += rate * jnp.sum((g * soft).reshape(-1, 8, 128), axis=0)
    dlast[...] = dproj_o[...]

    def copy_out(block):
        at = pl.ds(block * Q, Q)
        return pltpu.make_async_copy(gproj.at[at], gproj_o.at[at], sems.at[4])

    @pl.when(i > 0)
    def _():
        copy_out(block_before).start()

    @pl.when(i == steps - 1)
    def _():
        for part in range(D // 256):
            project_back(dlast, 0, part)
        copy_out(0).start()
        pack_grads(nf, share, tall, gcw_o, gcb_o, gsk_o, ghd_o, device, sums, rows_s, pack_o)
        pltpu.make_async_copy(gproj, gproj_o, sems.at[4]).wait()


def backward_scan(dscan, cin, act, dact, z, st, cw, head_terms, skip, seg, wc, device, heads, seqs, nf, share, tall):
    rows = dscan.shape[0]
    n = rows // Q
    nd = device.shape[0]
    one = pl.Buffered(buffer_count=1)
    full = lambda shape: pl.BlockSpec(shape, lambda i: (0,) * len(shape), pipeline_mode=one)
    blk = lambda w: pl.BlockSpec((Q, w), lambda i: (n - 1 - i, 0))
    blk3 = lambda s1, s2: pl.BlockSpec((1, s1, s2), lambda i: (n - 1 - i, 0, 0))
    hbm = pl.BlockSpec(memory_space=pl.ANY)
    return pl.pallas_call(
        functools.partial(backward_scan_kernel, heads, n // seqs, nf, share, tall),
        grid=(n,),
        in_specs=[blk(DI), blk(CONV), blk(CONV), blk(CONV), blk(128), blk3(N, DI), full(cw.shape), full(head_terms.shape),
                  full(skip.shape), blk3(1, Q), pl.BlockSpec((1, 1, Q), lambda i: (jnp.maximum(n - 2 - i, 0), 0, 0)),
                  hbm, hbm, hbm, hbm, full(device.shape)],
        out_specs=[blk(CONV + 128), hbm, full((nd * tall, 128))],
        out_shape=[jax.ShapeDtypeStruct((rows, CONV + 128), bf16), jax.ShapeDtypeStruct((rows, D), bf16),
                   jax.ShapeDtypeStruct((nd * tall, 128), bf16)],
        scratch_shapes=[pltpu.VMEM((rows, D), bf16), pltpu.VMEM((N, DI), f32), pltpu.VMEM((Q, 2 * DI), bf16), pltpu.VMEM((Q, DI), bf16),
                        pltpu.VMEM((Q, 2 * DI), bf16), pltpu.VMEM((128, 128), f32), pltpu.VMEM((8, DI), f32),
                        pltpu.VMEM((3, CONV // 128, Q + 8, 128), f32), pltpu.VMEM((256, DI), bf16),
                        pltpu.VMEM((DI, 128), bf16), pltpu.VMEM((Q + 8, 128), f32), pltpu.VMEM((32, CONV), f32),
                        pltpu.VMEM((8, CONV), f32), pltpu.VMEM((8, DI), f32), pltpu.VMEM((16, 128), f32),
                        pltpu.VMEM((nd * tall, 128), f32), pltpu.VMEM((D, CONV + 128), bf16), pltpu.VMEM((Q, CONV + 128), bf16),
                        pltpu.SemaphoreType.DMA((5,))],
        compiler_params=pltpu.CompilerParams(vmem_limit_bytes=52 << 20),
        cost_estimate=pl.CostEstimate(flops=0, bytes_accessed=0, transcendentals=0),
        name="backward_scan",
    )(dscan, cin, act, dact, z, st, cw, head_terms, skip, seg, seg, *wc, device)


def norm_back_kernel(ri, gproj, dgate, tok, cot, wg_abs, gain, device, out_o, wg, order):
    @pl.when(pl.program_id(0) == 0)
    def _():
        column = lax.broadcasted_iota(jnp.int32, (8, D), 1).astype(f32)
        slot = jnp.floor((column + 0.5) * (1.0 / ri))
        nd = device.shape[0]
        mine = lax.broadcasted_iota(jnp.int32, (nd, D), 0).astype(f32) == slot[0:1, :]
        feature = jnp.sum(jnp.where(mine, device[...][:, 0:1], 0.0), axis=0, keepdims=True) * ri + (column - slot * ri)[0:1, :]
        order[...] = (lax.broadcasted_iota(jnp.int32, (D, D), 0).astype(f32) == feature).astype(bf16)
        wg[...] = (0.5 * dot_tn(order[...], wg_abs[...])).astype(bf16)

    grad = dot_nt(dgate[...], wg[...]) + gproj[...].astype(f32)
    x = tok[...].astype(f32)
    r = lax.rsqrt(jnp.mean(x * x, axis=-1, keepdims=True) + EPS)
    unit = x * r
    e = gain[...] * grad
    back = r * (e - unit * jnp.mean(unit * e, axis=-1, keepdims=True))
    res = (cot[...].astype(f32) + back).astype(bf16)
    out_o[...] = dot_nt(res, order[...]).astype(bf16)


def norm_back(gproj, dgate, tok, cot, later, gain, device, ri, bm=512):
    rows = gproj.shape[0]
    one = pl.Buffered(buffer_count=1)
    full = lambda shape: pl.BlockSpec(shape, lambda i: (0,) * len(shape), pipeline_mode=one)
    blk = lambda w: pl.BlockSpec((bm, w), lambda i: (i, 0))
    return pl.pallas_call(
        functools.partial(norm_back_kernel, ri),
        grid=(rows // bm,),
        in_specs=[blk(D), blk(DI), blk(D), blk(D), full((D, DI)), full(gain.shape), full(device.shape)],
        out_specs=blk(D),
        out_shape=jax.ShapeDtypeStruct((rows, D), bf16),
        scratch_shapes=[pltpu.VMEM((D, DI), bf16), pltpu.VMEM((D, D), bf16)],
        compiler_params=pltpu.CompilerParams(vmem_limit_bytes=46 << 20),
        cost_estimate=pl.CostEstimate(flops=0, bytes_accessed=0, transcendentals=0),
        name="norm_back",
    )(gproj, dgate, tok, cot, later, gain, device)


def conv_weight_kernel(nrm, dproj, small, a_o, b_o):
    grad = lax.dot_general(dproj[...], nrm[...], (((0,), (0,)), ((), ())), preferred_element_type=f32)
    half = a_o.shape[0]
    out = grad.astype(bf16).T
    a_o[...] = out[:half]
    b_o[...] = out[half:]

    @pl.when(pl.program_id(0) == pl.num_programs(0) - 1)
    def _():
        last = slice(a_o.shape[1] - 128, a_o.shape[1])
        out = (grad[a_o.shape[1] - 128 :].T + small[...].astype(f32)).astype(bf16)
        a_o[:, last] = out[:half]
        b_o[:, last] = out[half:]


def conv_weight_grad(nrm, dproj, small, bn=640):
    rows = nrm.shape[0]
    one = pl.Buffered(buffer_count=1)
    return pl.pallas_call(
        conv_weight_kernel,
        grid=((CONV + 128) // bn,),
        in_specs=[pl.BlockSpec((rows, D), lambda i: (0, 0), pipeline_mode=one), pl.BlockSpec((rows, bn), lambda i: (0, i)),
                  pl.BlockSpec((D, 128), lambda i: (0, 0), pipeline_mode=one)],
        out_specs=[pl.BlockSpec((D // 2, bn), lambda i: (0, i))] * 2,
        out_shape=[jax.ShapeDtypeStruct((D // 2, CONV + 128), bf16)] * 2,
        compiler_params=pltpu.CompilerParams(vmem_limit_bytes=50 << 20),
        cost_estimate=pl.CostEstimate(flops=0, bytes_accessed=0, transcendentals=0),
        name="conv_weight_grad",
    )(nrm, dproj, small)


def finish_kernel(heads, share, parts, early, w_in, w_out, in_gain, gate_gain, *refs):
    own, got = refs[0], refs[1:parts]
    in_o, out_o, in_gain_o, gate_gain_o, cw_o, cb_o, sb_o, dl_o, sg_o, total = refs[parts:]
    ri, ro, cc = w_in.shape[0], w_out.shape[0], cb_o.shape[1]
    value = own[...]
    for part in got:
        value = value + part[...].astype(f32)
    total[...] = value
    in_o[:, :DI] = early[:, :DI].astype(f32)
    in_o[:, DI:] = total[0:ri, : CONV + heads]
    out_o[0:ri, :] = early[:, DI : DI + D].astype(f32)
    out_o[ri:, :] = early[:, DI + D :].astype(f32)

    def across(column, count):
        spot = lax.broadcasted_iota(jnp.int32, (count, count), 0) == lax.broadcasted_iota(jnp.int32, (count, count), 1)
        return jnp.sum(jnp.where(spot, column, 0.0), axis=0, keepdims=True)

    in_gain_o[...] = across(jnp.sum(w_in[...].astype(f32) * in_o[...], axis=-1, keepdims=True), ri) / in_gain[...].astype(f32)
    gate_gain_o[...] = across(jnp.sum(w_out[...].astype(f32) * out_o[...], axis=-1, keepdims=True), ro) / gate_gain[...].astype(f32)
    at = CONV + heads
    cw_o[...] = total[0:4, at : at + cc] + total[5:9, at : at + cc]
    cb_o[...] = total[4:5, at : at + cc] + total[9:10, at : at + cc]
    for k, term in enumerate((sb_o, dl_o, sg_o)):
        term[...] = total[10 + k : 11 + k, at : at + share] + total[13 + k : 14 + k, at : at + share]


def finish(early, w_in, w_out, in_gain, gate_gain, own, got, heads, share, cc):
    ri, ro = w_in.shape[0], w_out.shape[0]
    shapes = [(ri, w_in.shape[1]), (ro, D), (1, ri), (1, ro), (4, cc), (1, cc)] + [(1, share)] * 3
    return pl.pallas_call(
        functools.partial(finish_kernel, heads, share, 1 + len(got)),
        out_shape=[jax.ShapeDtypeStruct(shape, f32) for shape in shapes],
        scratch_shapes=[pltpu.VMEM(own.shape, f32)],
        compiler_params=pltpu.CompilerParams(vmem_limit_bytes=12 << 20),
        name="finish",
    )(early, w_in, w_out, in_gain, gate_gain, own, *got)


def stages_of(mesh):
    ndp, nf = mesh.shape["dp"], mesh.shape["fsdp"]
    out = []
    stride = 1
    while stride < nf:
        group = 2 if stride == 1 else min(4, nf // stride)
        out.append(("fsdp", stride, group, stride))
        stride *= group
    stride = 1
    while stride < ndp:
        group = min(4, ndp // stride)
        out.append(("dp", stride, group, stride * nf))
        stride *= group
    return out[::-1]


def pairs_of(stages):
    out = []
    for axis, stride, group, number in stages[::-1]:
        step = 1
        while step < group:
            out.append((axis, stride * step, 2, number * step))
            step *= 2
    return out


def slot_devices(stages):
    rel = np.zeros((1,), np.int32)
    for _, _, group, number in stages:
        rel = (np.arange(group, dtype=np.int32)[:, None] * number + rel[None, :]).reshape(-1)
    return jnp.asarray(rel)


def swap(arr, axis, size, offset):
    return lax.ppermute(arr, axis, [(i, i ^ offset) for i in range(size)])


def gather_stage(block, stage, sizes, first=0):
    axis, stride, group, _ = stage
    if first == 0 or group != 4:
        return jnp.stack([block] + [swap(block, axis, sizes[axis], k * stride) for k in range(1, group)])
    if first == 1:
        block = jnp.stack([block, swap(block, axis, sizes[axis], stride)])
        return jnp.concatenate([block, swap(block, axis, sizes[axis], 2 * stride)])
    block = jnp.stack([block, swap(block, axis, sizes[axis], 2 * stride)])
    block = jnp.stack([block, swap(block, axis, sizes[axis], stride)], axis=1)
    return block.reshape((4,) + block.shape[2:])


def scatter_parts(kept, stage, sizes):
    axis, stride, group, _ = stage
    return [swap(kept[k].astype(bf16), axis, sizes[axis], k * stride) for k in range(1, group)]


def scatter_stage(kept, stage, sizes):
    total = kept[0]
    for part in scatter_parts(kept, stage, sizes):
        total = total + part.astype(f32)
    return total


def before(value, *others):
    return lax.optimization_barrier((value,) + others)


def local(mesh, tokens, cotangent, segments, in_gain, weight_in, conv_weight, conv_bias, step_bias, decay_log, skip_gain,
          gate_gain, weight_out):
    sizes = {"dp": mesh.shape["dp"], "fsdp": mesh.shape["fsdp"]}
    nf = sizes["fsdp"]
    nd = sizes["dp"] * nf
    axes = ("dp", "fsdp")
    stages = stages_of(mesh)
    me = lax.axis_index("dp") * nf + lax.axis_index("fsdp")
    seqs, length, _ = tokens.shape
    rows = seqs * length
    ri, ro, cc, share = weight_in.shape[0], weight_out.shape[0], conv_bias.shape[0], step_bias.shape[0]
    heads = share * nf

    device = slot_devices(stages) ^ me
    feature = (device[:, None] * ri + jnp.arange(ri)[None, :]).reshape(-1)
    order = (jnp.arange(D)[:, None] == feature[None, :]).astype(bf16)

    tall = max(ri, 16)
    wc, later = pack(weight_in, weight_out, in_gain[None], conv_weight, conv_bias[None], gate_gain[None],
                     step_bias[None], decay_log[None], skip_gain[None], ri, tall)
    later = lax.all_gather(later, axes, axis=0, tiled=True)
    tok = tokens.reshape(rows, D)
    up = cotangent.reshape(rows, D)
    wc = gather_stage(wc, stages[0], sizes)
    tok_s = jnp.dot(tok, order, preferred_element_type=bf16)
    device_rows = jnp.broadcast_to(device.astype(f32)[:, None], (nd, 128))
    seg = segments.reshape(rows // Q, 1, Q)
    wc, tok_s = before(wc, tok_s)
    one, two = wc[..., :SPLIT], wc[..., SPLIT:]
    for stage in stages[1:-1]:
        one = gather_stage(one, stage, sizes, 1)
        two = gather_stage(two, stage, sizes, 2)
    up_s = jnp.dot(up, order, preferred_element_type=bf16)
    two, up_s, device_rows, seg = before(two, up_s, device_rows, seg)
    axis, stride = stages[-1][:2]
    quarters = [part.reshape(nd // 2, tall, part.shape[-1])
                for part in (one, two, swap(one, axis, sizes[axis], stride), swap(two, axis, sizes[axis], stride))]
    last = [part[:, :16, CONV - SPLIT :] for part in (quarters[1], quarters[3])]
    small = jnp.concatenate(last, axis=0).transpose(1, 0, 2).astype(f32)
    wc = [part[:, :ri].reshape(D // 2, part.shape[-1]) for part in quarters]

    cin, act, dact, nrm, scan, st, z, gain, gain_abs, cw, cb, gg, head_terms, skip = forward_scan(
        tok_s, wc, small, device_rows, seg, seqs, ri, ro, share, heads)
    mixed, dscan, dgate, early, wo = gate_pass(tok, scan, up, later, gain_abs, gg, ri)
    early = lax.psum_scatter(early, axes, scatter_dimension=0, tiled=True)

    dproj, gproj, small = backward_scan(
        dscan, cin, act, dact, z, st, cw, head_terms, skip, seg, wc, device_rows, heads, seqs, nf, share, tall)
    if ri == tall:
        halves = conv_weight_grad(nrm, dproj, small)
        halves = [half.reshape(nd // 2, tall, CONV + 128) for half in halves]
    else:
        halves = conv_weight_grad(nrm, dproj, jnp.zeros((D, 128), bf16))
        halves = [jnp.pad(half.reshape(nd // 2, ri, CONV + 128), ((0, 0), (0, tall - ri), (0, 0))) for half in halves]
        small = jnp.pad(small.reshape(nd, tall, 128), ((0, 0), (0, 0), (CONV, 0)))
        halves = [half + part for half, part in zip(halves, (small[: nd // 2], small[nd // 2 :]))]

    axis, stride, group, _ = stages[-1]
    got = swap(halves[1], axis, sizes[axis], stride)
    shape = [g for _, _, g, _ in stages[-2::-1]] + [tall, CONV + 128]
    pieces = zip(halves[0].reshape(shape), got.reshape(shape))
    total = [mine.astype(f32) + part.astype(f32) for mine, part in pieces]
    total[0], gain = before(total[0], gain)
    gtok = norm_back(gproj, dgate, tok_s, up_s, later, gain, device_rows, ri)
    for stage in stages[-2:0:-1]:
        total = scatter_stage(total, stage, sizes)
    total, gtok, wo = before(total, gtok, wo)
    got = scatter_parts(total, stages[0], sizes)
    out = out_pass(mixed, tok, wo)
    early, out = before(early, out)
    g_in, g_out, g_in_gain, g_gate_gain, g_cw, g_cb, g_sb, g_dl, g_sg = finish(
        early, weight_in, weight_out, in_gain[None], gate_gain[None], total[0], got, heads, share, cc)
    return (out.reshape(tokens.shape), gtok.reshape(tokens.shape), g_in_gain[0], g_in, g_cw, g_cb[0],
            g_sb[0], g_dl[0], g_sg[0], g_gate_gain[0], g_out)


def solution(mesh):
    every = ("dp", "fsdp")
    return jax.shard_map(
        functools.partial(local, mesh),
        mesh=mesh,
        in_specs=(P(every, None, None), P(every, None, None), P(every, None), P(every), P(every, None), P(None, every),
                  P(every), P("fsdp"), P("fsdp"), P("fsdp"), P(every), P(every, None)),
        out_specs=(P(every, None, None), P(every, None, None), P(every), P(every, None), P(None, every), P(every),
                   P("fsdp"), P("fsdp"), P("fsdp"), P(every), P(every, None)),
        check_vma=False,
    )
```
